32 devices in a mesh: xi: 4 (over z), eta: 2 (over y), zeta: 4 (over x, core).
Axes of the slice: x: 2, y: 2, z: 4, core: 2. Of those that a mesh axis runs over, the one named last changes fastest.
Arguments:
- residual: float32 [5, 32, 32, 256], P(None, 'zeta', 'xi', 'eta'), may hold values from -6 to 6
- flow_state: float32 [5, 32, 32, 256], P(None, 'zeta', 'xi', 'eta'), may hold values from -6 to 6
- factors_zeta: float32 [3, 5, 32, 32, 256], P(None, None, 'zeta', 'xi', 'eta'), may hold values from -1.5 to 1.5, as said below
- factors_eta: float32 [3, 5, 32, 32, 256], P(None, None, 'zeta', 'xi', 'eta'), may hold values from -1.5 to 1.5, as said below
- factors_xi: float32 [3, 5, 32, 32, 256], P(None, None, 'zeta', 'xi', 'eta'), may hold values from -1.5 to 1.5, as said below
Outputs:
- update: float32 [5, 32, 32, 256], P(None, 'zeta', 'xi', 'eta')
The draws below stay inside these ranges and needn't reach their ends.
Inputs may be any that keep to these rules, and one draw needn't show every extreme that they name: `factors_zeta`: F[g,2] is positive; the operator of each line is nonsingular. `factors_eta`: F[g,2] is positive; the operator of each line is nonsingular. `factors_xi`: F[g,2] is positive; the operator of each line is nonsingular.
All inputs are finite; a program needn't handle non-finite values.
Results may differ from the reference program's by a relative error of at most 0.000053.
Values sent between devices are 32-bit elements; how exact they have to be, the bound alone decides.
A program may use at most 128 MiB of HBM per device.

```python
import jax
import jax.numpy as jnp
from jax import lax

CZ = 8
CX = 8
CY = 128
NZ = 32
NX = 32
NY = 256


def line_speeds(complete_extent, line_dimension, block_extent, slow_flag, initial_random_key, middle_random_key, final_random_key, pulse_random_key, magnitude_key):
    line_length = complete_extent[line_dimension]
    position = lax.broadcasted_iota(jnp.int32, complete_extent, line_dimension)
    group_row = lax.broadcasted_iota(jnp.int32, complete_extent, 0)
    blocks = line_length // block_extent
    rough = jax.random.uniform(initial_random_key, complete_extent, jnp.float32, 0.6, 1.4)
    device_table = jnp.exp(jax.random.uniform(middle_random_key, (3 * blocks,), jnp.float32, -0.7, 0.7))
    device_factor = jnp.take(device_table, group_row * blocks + position // block_extent)
    fast_rate = jax.random.uniform(final_random_key, (3,), jnp.float32, 1.0 / 50.0, 1.0 / 30.0)
    slow_rate = 1.5 / line_length
    base_rate = jnp.where(slow_flag, slow_rate, fast_rate)
    falloff_speed = base_rate[:, None, None, None] * rough * device_factor
    pulse_event = jax.random.randint(pulse_random_key, complete_extent, 0, line_length) < 2
    reduction_multiplier = jax.random.uniform(magnitude_key, complete_extent, jnp.float32, 0.5, 0.8)
    keep_fraction = jnp.exp(-falloff_speed) * jnp.where(pulse_event, reduction_multiplier, 1.0)
    return (falloff_speed, keep_fraction)


def line_factors(key, line_dimension, block_extent):
    complete_extent = (3, NZ, NX, NY)
    line_length = complete_extent[line_dimension]
    subkeys = jax.random.split(key, 14)
    position = lax.broadcasted_iota(jnp.int32, complete_extent, line_dimension)
    fast_group = jax.random.randint(subkeys[0], (), 0, 3)
    slow_flag = jnp.arange(3) != fast_group
    rate_low, retain_low = line_speeds(complete_extent, line_dimension, block_extent, slow_flag, subkeys[1], subkeys[2], subkeys[3], subkeys[4], subkeys[5])
    rate_high, retain_high = line_speeds(complete_extent, line_dimension, block_extent, slow_flag, subkeys[6], subkeys[7], subkeys[8], subkeys[9], subkeys[10])
    mix_low = jax.random.uniform(subkeys[11], complete_extent, jnp.float32, -0.5, 0.5)
    mix_high = jax.random.uniform(subkeys[12], complete_extent, jnp.float32, -0.5, 0.5)
    before = jnp.roll(retain_low, 1, line_dimension) * (position > 0).astype(jnp.float32)
    after = jnp.roll(retain_high, -1, line_dimension) * (position < line_length - 1).astype(jnp.float32)
    pivot = jax.random.uniform(subkeys[13], complete_extent, jnp.float32, 0.5, 1.5) * 2.0 * jnp.sqrt(rate_low * rate_high)
    pivot = jnp.minimum(pivot, 1.45)
    return jnp.stack([-(retain_low + mix_low), mix_low * before, pivot, -(retain_high + mix_high), mix_high * after], 1)


def draw_factors_zeta(key, part):
    return line_factors(jax.random.fold_in(key, 11), 1, CZ)


def draw_factors_eta(key, part):
    return line_factors(jax.random.fold_in(key, 13), 3, CY)


def draw_factors_xi(key, part):
    return line_factors(jax.random.fold_in(key, 17), 2, CX)


def level_of(own_key, extent, cuts, smallest, largest):
    level, own = 1.0, jax.random.fold_in(own_key, 6)
    for dim, shards_of in cuts:
        heights = jnp.exp(jax.random.uniform(jax.random.fold_in(own, dim), (shards_of,), jnp.float32, smallest / len(cuts), largest / len(cuts)))
        level = level * jnp.repeat(heights, extent[dim] // shards_of).reshape([-1 if axis == dim else 1 for axis in range(len(extent))])
    return level


def noise(rng, shape, scale, most, cuts=(), kind=jnp.bfloat16):
    result = scale * jax.random.normal(rng, shape, jnp.float32)
    if cuts:
        result = result * level_of(rng, shape, cuts, -0.22, 0.18)
    return jnp.clip(result, -most, most).astype(kind)


def setup_inputs(seed: int = 0) -> dict:
    keys = jax.random.split(jax.random.key(seed), 6)
    return {
        "residual": noise(keys[0], (5, NZ, NX, NY), 1.0, 6.0, ((1, 4), (2, 4), (3, 2)), jnp.float32),
        "flow_state": noise(keys[1], (5, NZ, NX, NY), 1.0, 6.0, ((1, 4), (2, 4), (3, 2)), jnp.float32),
        "factors_zeta": draw_factors_zeta(jax.random.fold_in(keys[5], 71), 0),
        "factors_eta": draw_factors_eta(jax.random.fold_in(keys[5], 71), 0),
        "factors_xi": draw_factors_xi(jax.random.fold_in(keys[5], 71), 0),
    }


field_group = (0, 0, 0, 1, 2)
stencil_weights = (1.0, -4.0, 6.0, -4.0, 1.0)
dissipation = 0.05


def run_sweep(values, lead_row, first_row, second_row, line_axis, backward):
    columns = [jnp.moveaxis(array_item, line_axis, 0) for array_item in (values, lead_row, first_row, second_row)]
    if backward:
        columns = [jnp.flip(array_item, 0) for array_item in columns]
    zero_state = jnp.zeros_like(columns[0][0])

    def advance(carried, current):
        recent, before_last = carried
        value, scale, coef_one, coef_two = current
        updated = scale * value - coef_one * recent - coef_two * before_last
        return (updated, recent), updated

    final_state, solved = lax.scan(advance, (zero_state, zero_state), tuple(columns))
    if backward:
        solved = jnp.flip(solved, 0)
    return jnp.moveaxis(solved, 0, line_axis)


def reference(residual, flow_state, factors_zeta, factors_eta, factors_xi):
    padded = jnp.pad(flow_state, ((0, 0), (2, 2), (2, 2), (2, 2)))
    zeta_cells, xi_cells, eta_cells = flow_state.shape[1:]
    dissipated = jnp.zeros_like(flow_state)
    for position, weight in enumerate(stencil_weights):
        dissipated = dissipated + weight * (
            padded[:, position:position + zeta_cells, 2:2 + xi_cells, 2:2 + eta_cells]
            + padded[:, 2:2 + zeta_cells, position:position + xi_cells, 2:2 + eta_cells]
            + padded[:, 2:2 + zeta_cells, 2:2 + xi_cells, position:position + eta_cells])
    source = residual - dissipation * dissipated
    results = []
    for field in range(5):
        group_index = field_group[field]
        value = source[field]
        for factors, line_axis in ((factors_zeta, 0), (factors_eta, 2), (factors_xi, 1)):
            factor_group = factors[group_index]
            value = run_sweep(value, jnp.ones_like(value), factor_group[0], factor_group[1], line_axis, False)
            value = run_sweep(value, factor_group[2], factor_group[3], factor_group[4], line_axis, True)
        results.append(value)
    return jnp.stack(results, 0)
```

```python
import functools

import jax
import jax.numpy as jnp
from jax import lax
from jax.experimental import pallas as pl
from jax.experimental.pallas import tpu as pltpu
from jax.sharding import PartitionSpec as P

field_group = (0, 0, 0, 1, 2)
dissipation = 0.05
sublanes = 8
MESH = pl.DeviceIdType.MESH


def spread(planes):
    return jnp.concatenate([planes[g : g + 1] for g in field_group], 0)


def forward_sweep(steps, factor, value, recent, before):
    rows = []
    for s in range(steps):
        now = -(factor(0, s) * recent + factor(1, s) * before)
        if value is not None:
            now = now + value(s)
        rows.append(now)
        recent, before = now, recent
    return rows


def backward_sweep(steps, factor, value, recent, before, keep):
    rows = [None] * steps
    for s in reversed(range(steps)):
        now = factor(2, s) * value(s) - factor(3, s) * recent - factor(4, s) * before
        rows[s] = now
        keep(s, now)
        recent, before = now, recent
    return rows


def responses(steps, factor, keep):
    one = jnp.ones_like(factor(0, 0))
    zero = jnp.zeros_like(one)
    lift = lambda k, s: factor(k, s)[None]
    forward = forward_sweep(
        steps, lift, None, jnp.stack([one, zero]), jnp.stack([zero, one])
    )
    none = jnp.zeros((2,) + one.shape, jnp.float32)
    backward = backward_sweep(
        steps,
        lift,
        lambda s: jnp.concatenate([forward[s], none], 0),
        jnp.stack([zero, zero, one, zero]),
        jnp.stack([zero, zero, zero, one]),
        keep,
    )
    return jnp.concatenate([forward[-1], forward[-2], backward[0], backward[1]], 0)


def chain(count, matrices, offsets):
    first = offsets(0)
    zero = jnp.zeros_like(first[0])
    c1, c2 = zero, zero
    into = []
    for q in range(count):
        into.append((c1, c2))
        if q < count - 1:
            m, o = matrices(q), offsets(q)
            c1, c2 = o[0] + m[0] * c1 + m[1] * c2, o[1] + m[2] * c1 + m[3] * c2
    d1, d2 = zero, zero
    result = [None] * count
    for q in reversed(range(count)):
        c1, c2 = into[q]
        result[q] = (c1, c2, d1, d2)
        if q > 0:
            m, o = matrices(q), offsets(q)
            d1, d2 = (
                o[2] + (m[4] * c1 + m[5] * c2) + (m[6] * d1 + m[7] * d2),
                o[3] + (m[8] * c1 + m[9] * c2) + (m[10] * d1 + m[11] * d2),
            )
    return result


class Exchange:
    def __init__(self, axis, count, send_sem, recv_sem):
        self.axis, self.count = axis, count
        self.send_sem, self.recv_sem = send_sem, recv_sem
        self.me = lax.axis_index(axis)

    def peers(self):
        return [lax.rem(self.me + k, self.count) for k in range(1, self.count)]

    def copy(self, kind, source, slots, p):
        return pltpu.make_async_remote_copy(
            src_ref=source(p),
            dst_ref=slots.at[self.me],
            send_sem=self.send_sem.at[kind, p],
            recv_sem=self.recv_sem.at[kind, self.me],
            device_id={self.axis: p},
            device_id_type=MESH,
        )

    def start(self, kind, source, slots):
        for p in self.peers():
            self.copy(kind, source, slots, p).start()

    def wait_recv(self, kind, source, slots):
        for p in self.peers():
            pltpu.make_async_remote_copy(
                src_ref=source(p),
                dst_ref=slots.at[p],
                send_sem=self.send_sem.at[kind, p],
                recv_sem=self.recv_sem.at[kind, p],
                device_id={self.axis: p},
                device_id_type=MESH,
            ).wait_recv()

    def wait_send(self, kind, source, slots):
        for p in self.peers():
            self.copy(kind, source, slots, p).wait_send()


class Split:
    def __init__(self, exchange, m_send, m_slots, o_send, o_slots, r_send, r_slots, full):
        self.x = exchange
        self.m_send, self.m_slots = m_send, m_slots
        self.o_send, self.o_slots = o_send, o_slots
        self.r_send, self.r_slots, self.full = r_send, r_slots, full
        self.parts = m_send.shape[0]
        self.rows = sublanes // self.parts
        self.pick = (lambda p: p) if self.parts > 1 else (lambda p: 0)

    def put(self, kind, value, send, slots):
        for p in range(self.parts):
            send[p] = value[:, :, p * self.rows : (p + 1) * self.rows, :]
        slots[self.x.me] = send[self.pick(self.x.me)]
        self.x.start(kind, lambda p: send.at[self.pick(p)], slots)

    def put_matrices(self, value):
        self.put(0, value, self.m_send, self.m_slots)

    def put_offsets(self, value):
        self.put(1, value, self.o_send, self.o_slots)

    def solve(self):
        x = self.x
        x.wait_recv(0, lambda p: self.m_send.at[self.pick(p)], self.m_slots)
        x.wait_recv(1, lambda p: self.o_send.at[self.pick(p)], self.o_slots)
        solved = chain(
            x.count,
            lambda q: [spread(self.m_slots[q, k]) for k in range(12)],
            lambda q: [self.o_slots[q, k] for k in range(4)],
        )
        for q, planes in enumerate(solved):
            for k in range(4):
                self.r_send[q, k] = planes[k]
        if self.parts == 1:
            return [self.r_send[x.me, k] for k in range(4)]
        self.r_slots[x.me] = self.r_send[x.me]
        x.start(2, lambda p: self.r_send.at[p], self.r_slots)
        x.wait_recv(2, lambda p: self.r_send.at[p], self.r_slots)
        for p in range(self.parts):
            self.full[:, :, p * self.rows : (p + 1) * self.rows, :] = self.r_slots[p]
        return [self.full[k] for k in range(4)]

    def finish(self):
        self.x.wait_send(0, lambda p: self.m_send.at[self.pick(p)], self.m_slots)
        self.x.wait_send(1, lambda p: self.o_send.at[self.pick(p)], self.o_slots)
        if self.parts > 1:
            self.x.wait_send(2, lambda p: self.r_send.at[p], self.r_slots)


def corrected(local, response, incoming, lift):
    total = local
    for k in range(4):
        total = total + lift(response[k]) * incoming[k]
    return total


def kernel(
    counts, residual, flow, f_zeta, f_eta, f_xi, out,
    z_msend, z_mslots, z_osend, z_oslots, z_rsend, z_rslots, z_full, z_ss, z_rs,
    x_msend, x_mslots, x_osend, x_oslots, x_rsend, x_rslots, x_full, x_ss, x_rs,
    e_msend, e_mslots, e_osend, e_oslots, e_result, e_ss, e_rs,
    z_response, x_response, e_response, lines, turned, turned_factors,
    hz, hx_send, hx, he_send, he, padded, h_ss, h_rs,
):
    n_xi, n_eta, n_zeta = counts
    fields, cz, cx, cy = flow.shape
    planes = fields * cz
    xz = Exchange("zeta", n_zeta, z_ss, z_rs)
    xe = Exchange("eta", n_eta, e_ss, e_rs)
    xx = Exchange("xi", n_xi, x_ss, x_rs)
    zeta = Split(xz, z_msend, z_mslots, z_osend, z_oslots, z_rsend, z_rslots, z_full)
    xi = Split(xx, x_msend, x_mslots, x_osend, x_oslots, x_rsend, x_rslots, x_full)

    barrier = pltpu.get_barrier_semaphore()
    greeted = 0
    for x in (xz, xe, xx):
        for p in x.peers():
            pl.semaphore_signal(barrier, inc=1, device_id={x.axis: p}, device_id_type=MESH)
            greeted += 1

    per_pack = cy // 4
    lane = lax.broadcasted_iota(jnp.int32, (cx, cy), 1)
    packs = [jnp.zeros((cx, cy), jnp.float32) for _ in range(he_send.shape[0])]
    for k in range(planes):
        at = k % per_pack
        moved = pltpu.roll(flow[k // cz, k % cz], (4 * at + 2) % cy, 1)
        packs[k // per_pack] = jnp.where(lane // 4 == at, moved, packs[k // per_pack])
    for k, pack in enumerate(packs):
        he_send[k] = pack
    hx_send[0] = flow[:, :, cx - 2 : cx, :]
    hx_send[1] = flow[:, :, 0:2, :]

    pl.semaphore_wait(barrier, greeted)

    halos = (
        (xx, hx, lambda side: hx_send.at[side]),
        (xe, he, lambda side: he_send),
        (xz, hz, lambda side: flow.at[:, cz - 2 : cz] if side == 0 else flow.at[:, 0:2]),
    )

    def halo_copy(number, side):
        x, slots, source = halos[number]
        step = 1 if side == 0 else x.count - 1
        return pltpu.make_async_remote_copy(
            src_ref=source(side),
            dst_ref=slots.at[side],
            send_sem=h_ss.at[number, side],
            recv_sem=h_rs.at[number, side],
            device_id={x.axis: lax.rem(x.me + step, x.count)},
            device_id_type=MESH,
        )

    for number, (x, slots, source) in enumerate(halos):
        for side in range(2):
            sends = x.me < x.count - 1 if side == 0 else x.me > 0
            has = x.me > 0 if side == 0 else x.me < x.count - 1
            pl.when(sends)(lambda number=number, side=side: halo_copy(number, side).start())

            @pl.when(jnp.logical_not(has))
            def _(slots=slots, side=side):
                slots[side] = jnp.zeros(slots.shape[1:], jnp.float32)

    def keep_z(s, now):
        z_response[s] = now

    zeta.put_matrices(responses(cz, lambda k, s: f_zeta[:, k, s], keep_z))

    def xi_factor(k, s):
        return jnp.stack(
            [f_xi[pl.ds((g * 5 + k) * cz * cx + s, cz, stride=cx), :] for g in range(3)]
        )

    def keep_x(s, now):
        x_response[s] = now

    xi.put_matrices(responses(cx, xi_factor, keep_x))

    for number, (x, slots, source) in enumerate(halos):
        for side in range(2):
            has = x.me > 0 if side == 0 else x.me < x.count - 1
            pl.when(has)(lambda number=number, side=side: halo_copy(number, side).wait_recv())

    state = flow[...]
    padded[:, :, 8 - 2 : 8, :] = hx[0]
    padded[:, :, 8 : 8 + cx, :] = state
    padded[:, :, 8 + cx : 8 + cx + 2, :] = hx[1]
    long = jnp.concatenate([hz[0], state, hz[1]], 1)
    near = (padded[:, :, 7 : 7 + cx, :] + padded[:, :, 9 : 9 + cx, :]) + (
        long[:, 1 : 1 + cz] + long[:, 3 : 3 + cz]
    )
    far = (padded[:, :, 6 : 6 + cx, :] + padded[:, :, 10 : 10 + cx, :]) + (
        long[:, 0:cz] + long[:, 4 : 4 + cz]
    )
    eta_near, eta_far = [], []
    for k in range(planes):
        at = k % per_pack
        v = flow[k // cz, k % cz]
        back = (cy - (4 * at + 2)) % cy
        low = pltpu.roll(he[0, k // per_pack], back, 1)
        high = pltpu.roll(he[1, k // per_pack], back, 1)
        for s, into in ((1, eta_near), (2, eta_far)):
            into.append(
                pltpu.roll(jnp.where(lane >= cy - s, low, v), s, 1)
                + pltpu.roll(jnp.where(lane < s, high, v), cy - s, 1)
            )
    near = near + jnp.stack(eta_near).reshape(flow.shape)
    far = far + jnp.stack(eta_far).reshape(flow.shape)
    source = residual[...] - dissipation * (18.0 * state - 4.0 * near + far)

    z_factor = lambda k, s: spread(f_zeta[:, k, s])
    zero = jnp.zeros((fields, cx, cy), jnp.float32)
    forward = forward_sweep(cz, z_factor, lambda s: source[:, s], zero, zero)
    local = backward_sweep(cz, z_factor, lambda s: forward[s], zero, zero, lambda s, now: None)
    zeta.put_offsets(jnp.stack([forward[-1], forward[-2], local[0], local[1]]))

    tiles = lines.shape[0] // cy
    steps = cy // sublanes
    total = lines.shape[0]
    per_field = cz * cx
    order = list(field_group) + [field_group[-1]] * (total // per_field - fields)
    for k in range(5):
        whole = jnp.concatenate([f_eta[g * 5 + k] for g in order], 0)
        for t in range(tiles):
            turned_factors[k * total + t * cy : k * total + (t + 1) * cy, :] = whole[
                t * cy : (t + 1) * cy
            ].T

    def eta_factor(k, s):
        return turned_factors[
            pl.ds(k * total + s, tiles * sublanes, stride=steps), :
        ].reshape(tiles, sublanes, cy)

    def keep_e(s, now):
        e_response[s] = now

    e_matrices = responses(steps, eta_factor, keep_e)
    e_msend[...] = e_matrices
    e_mslots[xe.me] = e_matrices
    xe.start(0, lambda p: e_msend, e_mslots)

    incoming = zeta.solve()
    for s in range(cz):
        done = corrected(local[s], z_response[s], incoming, spread)
        for f in range(fields):
            lines[(f * cz + s) * cx : (f * cz + s + 1) * cx, :] = done[f]
    if total > planes * cx:
        lines[planes * cx : total, :] = jnp.zeros((total - planes * cx, cy), jnp.float32)

    for t in range(tiles):
        turned[t * cy : (t + 1) * cy, :] = lines[t * cy : (t + 1) * cy, :].T
    zero = jnp.zeros((tiles, sublanes, cy), jnp.float32)

    def at_step(s):
        return pl.ds(s, tiles * sublanes, stride=steps)

    forward = forward_sweep(
        steps, eta_factor, lambda s: turned[at_step(s), :].reshape(zero.shape), zero, zero
    )
    local = backward_sweep(
        steps, eta_factor, lambda s: forward[s], zero, zero, lambda s, now: None
    )
    offsets = jnp.stack([forward[-1], forward[-2], local[0], local[1]])
    e_osend[...] = offsets
    e_oslots[xe.me] = offsets
    xe.start(1, lambda p: e_osend, e_oslots)
    xe.wait_recv(0, lambda p: e_msend, e_mslots)
    xe.wait_recv(1, lambda p: e_osend, e_oslots)
    solved = chain(
        n_eta * sublanes,
        lambda q: [
            e_mslots[q // sublanes, k, :, q % sublanes : q % sublanes + 1, :] for k in range(12)
        ],
        lambda q: [
            e_oslots[q // sublanes, k, :, q % sublanes : q % sublanes + 1, :] for k in range(4)
        ],
    )
    for q, rows in enumerate(solved):
        c = q % sublanes
        for k in range(4):
            e_result[q // sublanes, k, :, c : c + 1, :] = rows[k]
    incoming = [e_result[xe.me, k] for k in range(4)]
    for s in range(steps):
        done = corrected(local[s], e_response[s], incoming, lambda r: r)
        turned[at_step(s), :] = done.reshape(tiles * sublanes, cy)
    for t in range(tiles):
        lines[t * cy : (t + 1) * cy, :] = turned[t * cy : (t + 1) * cy, :].T

    x_factor = lambda k, s: spread(xi_factor(k, s))
    zero = jnp.zeros((fields, cz, cy), jnp.float32)
    forward = forward_sweep(
        cx,
        x_factor,
        lambda s: lines[pl.ds(s, planes, stride=cx), :].reshape(zero.shape),
        zero,
        zero,
    )
    local = backward_sweep(cx, x_factor, lambda s: forward[s], zero, zero, lambda s, now: None)
    xi.put_offsets(jnp.stack([forward[-1], forward[-2], local[0], local[1]]))
    incoming = xi.solve()
    for s in range(cx):
        done = corrected(local[s], x_response[s], incoming, spread)
        out[pl.ds(s, planes, stride=cx), :] = done.reshape(planes, cy)

    zeta.finish()
    xi.finish()
    xe.wait_send(0, lambda p: e_msend, e_mslots)
    xe.wait_send(1, lambda p: e_osend, e_oslots)
    for number, (x, slots, source) in enumerate(halos):
        for side in range(2):
            sends = x.me < x.count - 1 if side == 0 else x.me > 0
            pl.when(sends)(lambda number=number, side=side: halo_copy(number, side).wait_send())


def split_scratch(count, fields, lanes):
    vmem = lambda *shape: pltpu.VMEM(shape, jnp.float32)
    parts = count if sublanes % count == 0 else 1
    rows = sublanes // parts
    return [
        vmem(parts, 12, 3, rows, lanes),
        vmem(count, 12, 3, rows, lanes),
        vmem(parts, 4, fields, rows, lanes),
        vmem(count, 4, fields, rows, lanes),
        vmem(count, 4, fields, rows, lanes),
        vmem(count, 4, fields, rows, lanes),
        vmem(4, fields, sublanes, lanes),
        pltpu.SemaphoreType.DMA((3, count)),
        pltpu.SemaphoreType.DMA((3, count)),
    ]


def on_device(counts, residual, flow_state, factors_zeta, factors_eta, factors_xi):
    n_xi, n_eta, n_zeta = counts
    fields, cz, cx, cy = flow_state.shape
    total = -(-(fields * cz * cx) // cy) * cy
    tiles = total // cy
    steps = cy // sublanes
    packs = -(-(fields * cz) // (cy // 4))
    vmem = lambda *shape: pltpu.VMEM(shape, jnp.float32)
    dma = pltpu.SemaphoreType.DMA
    whole = pl.BlockSpec(memory_space=pltpu.VMEM)
    scratch = (
        split_scratch(n_zeta, fields, cy)
        + split_scratch(n_xi, fields, cy)
        + [
            vmem(12, tiles, sublanes, cy),
            vmem(n_eta, 12, tiles, sublanes, cy),
            vmem(4, tiles, sublanes, cy),
            vmem(n_eta, 4, tiles, sublanes, cy),
            vmem(n_eta, 4, tiles, sublanes, cy),
            dma((2, n_eta)),
            dma((2, n_eta)),
            vmem(cz, 4, 3, cx, cy),
            vmem(cx, 4, 3, cz, cy),
            vmem(steps, 4, tiles, sublanes, cy),
            vmem(total, cy),
            vmem(total, cy),
            vmem(5 * total, cy),
            vmem(2, fields, 2, cx, cy),
            vmem(2, fields, cz, 2, cy),
            vmem(2, fields, cz, 2, cy),
            vmem(packs, cx, cy),
            vmem(2, packs, cx, cy),
            vmem(fields, cz, cx + 16, cy),
            dma((3, 2)),
            dma((3, 2)),
        ]
    )
    update = pl.pallas_call(
        functools.partial(kernel, counts),
        out_shape=jax.ShapeDtypeStruct((fields * cz * cx, cy), jnp.float32),
        in_specs=[whole] * 5,
        out_specs=whole,
        scratch_shapes=scratch,
        compiler_params=pltpu.CompilerParams(
            collective_id=0, has_side_effects=True, vmem_limit_bytes=48 * 2**20
        ),
    )(
        residual,
        flow_state,
        factors_zeta,
        factors_eta.reshape(15, cz * cx, cy),
        factors_xi.reshape(15 * cz * cx, cy),
    )
    return update.reshape(flow_state.shape)


def solution(mesh):
    fields = P(None, "zeta", "xi", "eta")
    factors = P(None, None, "zeta", "xi", "eta")
    counts = tuple(mesh.shape[axis] for axis in ("xi", "eta", "zeta"))
    return jax.shard_map(
        functools.partial(on_device, counts),
        mesh=mesh,
        in_specs=(fields, fields, factors, factors, factors),
        out_specs=fields,
        check_vma=False,
    )
```

```python
import functools

import jax
import jax.numpy as jnp
from jax import lax
from jax.experimental import pallas as pl
from jax.experimental.pallas import tpu as pltpu
from jax.sharding import PartitionSpec as P

field_group = (0, 0, 0, 1, 2)
dissipation = 0.05
sublanes = 8
MESH = pl.DeviceIdType.MESH


def spread(planes):
    return jnp.concatenate([planes[g : g + 1] for g in field_group], 0)


def forward_sweep(steps, factor, value, recent, before):
    rows = []
    for s in range(steps):
        now = -(factor(0, s) * recent + factor(1, s) * before)
        if value is not None:
            now = now + value(s)
        rows.append(now)
        recent, before = now, recent
    return rows


def backward_sweep(steps, factor, value, recent, before, keep):
    rows = [None] * steps
    for s in reversed(range(steps)):
        now = factor(2, s) * value(s) - factor(3, s) * recent - factor(4, s) * before
        rows[s] = now
        keep(s, now)
        recent, before = now, recent
    return rows


def responses(steps, factor, keep):
    one = jnp.ones_like(factor(0, 0))
    zero = jnp.zeros_like(one)
    lift = lambda k, s: factor(k, s)[None]
    forward = forward_sweep(
        steps, lift, None, jnp.stack([one, zero]), jnp.stack([zero, one])
    )
    none = jnp.zeros((2,) + one.shape, jnp.float32)
    backward = backward_sweep(
        steps,
        lift,
        lambda s: jnp.concatenate([forward[s], none], 0),
        jnp.stack([zero, zero, one, zero]),
        jnp.stack([zero, zero, zero, one]),
        keep,
    )
    return jnp.concatenate([forward[-1], forward[-2], backward[0], backward[1]], 0)


def chain(count, matrices, offsets, into, closed):
    c1, c2, d1, d2 = into
    entered = []
    for q in range(count):
        entered.append((c1, c2))
        if q < count - 1 or not closed:
            m, o = matrices(q), offsets(q)
            n1, n2 = m[0] * c1 + m[1] * c2, m[2] * c1 + m[3] * c2
            c1, c2 = (n1, n2) if o is None else (o[0] + n1, o[1] + n2)
    out = (c1, c2)
    result = [None] * count
    for q in reversed(range(count)):
        c1, c2 = entered[q]
        result[q] = (c1, c2, d1, d2)
        if q > 0 or not closed:
            m, o = matrices(q), offsets(q)
            n1, n2 = m[4] * c1 + m[5] * c2, m[8] * c1 + m[9] * c2
            if o is not None:
                n1, n2 = o[2] + n1, o[3] + n2
            d1, d2 = n1 + (m[6] * d1 + m[7] * d2), n2 + (m[10] * d1 + m[11] * d2)
    return result, out + (d1, d2)


class Exchange:
    def __init__(self, axis, count, send_sem, recv_sem):
        self.axis, self.count = axis, count
        self.send_sem, self.recv_sem = send_sem, recv_sem
        self.me = lax.axis_index(axis)

    def peers(self):
        return [lax.rem(self.me + k, self.count) for k in range(1, self.count)]

    def copy(self, kind, source, slots, p, slot, cut):
        pick = (lambda ref: ref) if cut is None else (lambda ref: ref.at[cut[0] : cut[1]])
        return pltpu.make_async_remote_copy(
            src_ref=pick(source(p)),
            dst_ref=pick(slots.at[slot]),
            send_sem=self.send_sem.at[kind, p],
            recv_sem=self.recv_sem.at[kind, slot],
            device_id={self.axis: p},
            device_id_type=MESH,
        )

    def start(self, kind, source, slots, cut=None, sends=None):
        for p in self.peers():
            go = lambda p=p: self.copy(kind, source, slots, p, self.me, cut).start()
            go() if sends is None else pl.when(sends(self.me, p))(go)

    def wait_recv(self, kind, source, slots, cut=None, sends=None):
        for p in self.peers():
            go = lambda p=p: self.copy(kind, source, slots, p, p, cut).wait_recv()
            go() if sends is None else pl.when(sends(p, self.me))(go)

    def wait_send(self, kind, source, slots, cut=None, sends=None):
        for p in self.peers():
            go = lambda p=p: self.copy(kind, source, slots, p, self.me, cut).wait_send()
            go() if sends is None else pl.when(sends(self.me, p))(go)


class Split:
    def __init__(self, exchange, m_send, m_slots, o_send, o_slots, r_send, r_slots, full):
        self.x = exchange
        self.m_send, self.m_slots = m_send, m_slots
        self.o_send, self.o_slots = o_send, o_slots
        self.r_send, self.r_slots, self.full = r_send, r_slots, full
        self.parts = m_send.shape[0]
        self.rows = sublanes // self.parts
        pick = (lambda p: p) if self.parts > 1 else (lambda p: 0)
        last = exchange.count - 1
        m_from = lambda p: m_send.at[pick(p)]
        o_from = lambda p: o_send.at[pick(p)]
        r_from = lambda p: r_send.at[p]
        self.matrices = (0, m_from, m_slots)
        self.ahead = (1, o_from, o_slots, (0, 2), lambda a, b: a < last)
        self.behind = (2, o_from, o_slots, (2, 4), lambda a, b: a > 0)
        self.carried = (3, r_from, r_slots, (0, 2), lambda a, b: b > 0)
        self.returned = (4, r_from, r_slots, (2, 4), lambda a, b: b < last)
        self.pick = pick

    def clear_ends(self):
        if self.parts > 1:
            nothing = jnp.zeros((self.parts, 2) + self.r_slots.shape[2:], jnp.float32)

            @pl.when(self.x.me == 0)
            def _():
                self.r_slots[:, 0:2] = nothing

            @pl.when(self.x.me == self.x.count - 1)
            def _():
                self.r_slots[:, 2:4] = nothing

    def put(self, route, value, send, slots, lo):
        hi = lo + value.shape[0]
        for p in range(self.parts):
            send[p, lo:hi] = value[:, :, p * self.rows : (p + 1) * self.rows, :]
        slots[self.x.me, lo:hi] = send[self.pick(self.x.me), lo:hi]
        self.x.start(*route)

    def put_matrices(self, value):
        self.put(self.matrices, value, self.m_send, self.m_slots, 0)

    def put_ahead(self, value):
        self.put(self.ahead, value, self.o_send, self.o_slots, 0)

    def put_behind(self, value):
        self.put(self.behind, value, self.o_send, self.o_slots, 2)

    def solve(self):
        x = self.x
        for route in (self.matrices, self.ahead, self.behind):
            x.wait_recv(*route)
        zero = jnp.zeros(self.o_slots.shape[2:], jnp.float32)
        solved, _ = chain(
            x.count,
            lambda q: [spread(self.m_slots[q, k]) for k in range(12)],
            lambda q: [self.o_slots[q, k] for k in range(4)],
            (zero,) * 4,
            True,
        )
        for q, planes in enumerate(solved):
            for k in range(4):
                self.r_send[q, k] = planes[k]
        if self.parts > 1:
            x.start(*self.carried)
            x.start(*self.returned)
            me = x.me

            @pl.when(me > 0)
            def _():
                self.r_slots[me, 0:2] = self.r_send[me, 0:2]

            @pl.when(me < x.count - 1)
            def _():
                self.r_slots[me, 2:4] = self.r_send[me, 2:4]

    def result(self):
        x = self.x
        if self.parts == 1:
            return [self.r_send[x.me, k] for k in range(4)]
        x.wait_recv(*self.carried)
        x.wait_recv(*self.returned)
        for p in range(self.parts):
            self.full[:, :, p * self.rows : (p + 1) * self.rows, :] = self.r_slots[p]
        return [self.full[k] for k in range(4)]

    def finish(self):
        for route in (self.matrices, self.ahead, self.behind):
            self.x.wait_send(*route)
        if self.parts > 1:
            self.x.wait_send(*self.carried)
            self.x.wait_send(*self.returned)


def corrected(local, response, incoming, lift):
    total = local
    for k in range(4):
        total = total + lift(response[k]) * incoming[k]
    return total


def kernel(
    counts, residual_hbm, flow_hbm, f_zeta_hbm, f_eta_hbm, f_xi_hbm, out,
    residual, flow, f_zeta, f_eta, f_xi, in_sem,
    z_msend, z_mslots, z_osend, z_oslots, z_rsend, z_rslots, z_full, z_ss, z_rs,
    x_msend, x_mslots, x_osend, x_oslots, x_rsend, x_rslots, x_full, x_ss, x_rs,
    e_matrices, e_msend, e_mslots, e_offsets, e_osend, e_oslots, e_result, e_own, e_inner,
    e_ss, e_rs,
    z_response, x_response, e_response, lines, turned, turned_factors,
    hz, hx_send, hx, he_send, he, padded, source, h_ss, h_rs,
):
    n_xi, n_eta, n_zeta = counts
    fields, cz, cx, cy = flow.shape
    planes = fields * cz
    xz = Exchange("zeta", n_zeta, z_ss, z_rs)
    xe = Exchange("eta", n_eta, e_ss, e_rs)
    xx = Exchange("xi", n_xi, x_ss, x_rs)
    zeta = Split(xz, z_msend, z_mslots, z_osend, z_oslots, z_rsend, z_rslots, z_full)
    xi = Split(xx, x_msend, x_mslots, x_osend, x_oslots, x_rsend, x_rslots, x_full)

    barrier = pltpu.get_barrier_semaphore()
    greeted = 0
    for x in (xz, xe, xx):
        for p in x.peers():
            pl.semaphore_signal(barrier, inc=1, device_id={x.axis: p}, device_id_type=MESH)
            greeted += 1

    loads = [
        pltpu.make_async_copy(src, dst, in_sem.at[k])
        for k, (src, dst) in enumerate(
            (
                (flow_hbm, flow),
                (f_zeta_hbm, f_zeta),
                (f_xi_hbm, f_xi),
                (residual_hbm, residual),
                (f_eta_hbm, f_eta),
            )
        )
    ]
    for load in loads:
        load.start()
    zeta.clear_ends()
    xi.clear_ends()
    loads[0].wait()

    per_pack = cy // 4
    lane = lax.broadcasted_iota(jnp.int32, (cx, cy), 1)
    packs = [jnp.zeros((cx, cy), jnp.float32) for _ in range(he_send.shape[0])]
    eta_part = []
    for k in range(planes):
        at = k % per_pack
        v = flow[k // cz, k % cz]
        up1, up2 = pltpu.roll(v, 1, 1), pltpu.roll(v, 2, 1)
        down1, down2 = pltpu.roll(v, cy - 1, 1), pltpu.roll(v, cy - 2, 1)
        near_low, near_high = lane < 1, lane >= cy - 1
        far_low, far_high = lane < 2, lane >= cy - 2
        near = jnp.where(near_low, 0.0, up1) + jnp.where(near_high, 0.0, down1)
        far = jnp.where(far_low, 0.0, up2) + jnp.where(far_high, 0.0, down2)
        eta_part.append(far - 4.0 * near)
        near = jnp.where(near_low, up1, jnp.where(near_high, down1, 0.0))
        far = jnp.where(far_low, up2, jnp.where(far_high, down2, 0.0))
        face = -dissipation * (far - 4.0 * near)
        moved = pltpu.roll(face, (4 * at + 2) % cy, 1)
        packs[k // per_pack] = jnp.where(lane // 4 == at, moved, packs[k // per_pack])
    for k, pack in enumerate(packs):
        he_send[k] = pack
    row = lambda x: flow[:, :, x : x + 1, :]
    hx_send[0, :, :, 0:1, :] = -dissipation * (row(cx - 2) - 4.0 * row(cx - 1))
    hx_send[0, :, :, 1:2, :] = -dissipation * row(cx - 1)
    hx_send[1, :, :, 0:1, :] = -dissipation * row(0)
    hx_send[1, :, :, 1:2, :] = -dissipation * (row(1) - 4.0 * row(0))

    pl.semaphore_wait(barrier, greeted)

    halos = (
        (xx, hx, lambda side: hx_send.at[side]),
        (xe, he, lambda side: he_send),
        (xz, hz, lambda side: flow.at[:, cz - 2 : cz] if side == 0 else flow.at[:, 0:2]),
    )

    def halo_copy(number, side):
        x, slots, origin = halos[number]
        step = 1 if side == 0 else x.count - 1
        return pltpu.make_async_remote_copy(
            src_ref=origin(side),
            dst_ref=slots.at[side],
            send_sem=h_ss.at[number, side],
            recv_sem=h_rs.at[number, side],
            device_id={x.axis: lax.rem(x.me + step, x.count)},
            device_id_type=MESH,
        )

    for number, (x, slots, origin) in enumerate(halos):
        for side in range(2):
            sends = x.me < x.count - 1 if side == 0 else x.me > 0
            has = x.me > 0 if side == 0 else x.me < x.count - 1
            pl.when(sends)(lambda number=number, side=side: halo_copy(number, side).start())

            @pl.when(jnp.logical_not(has))
            def _(slots=slots, side=side):
                slots[side] = jnp.zeros(slots.shape[1:], jnp.float32)

    loads[1].wait()

    def keep_z(s, now):
        z_response[s] = now

    zeta.put_matrices(responses(cz, lambda k, s: f_zeta[:, k, s], keep_z))

    state = flow[...]
    nothing = jnp.zeros((fields, cz, 2, cy), jnp.float32)
    padded[:, :, 8 - 2 : 8, :] = nothing
    padded[:, :, 8 : 8 + cx, :] = state
    padded[:, :, 8 + cx : 8 + cx + 2, :] = nothing
    none = jnp.zeros((fields, 2, cx, cy), jnp.float32)
    long = jnp.concatenate([none, state, none], 1)
    near = (padded[:, :, 7 : 7 + cx, :] + padded[:, :, 9 : 9 + cx, :]) + (
        long[:, 1 : 1 + cz] + long[:, 3 : 3 + cz]
    )
    far = (padded[:, :, 6 : 6 + cx, :] + padded[:, :, 10 : 10 + cx, :]) + (
        long[:, 0:cz] + long[:, 4 : 4 + cz]
    )
    total_part = 18.0 * state - 4.0 * near + far + jnp.stack(eta_part).reshape(flow.shape)
    loads[3].wait()
    source[...] = residual[...] - dissipation * total_part

    loads[2].wait()

    def xi_factor(k, s):
        return jnp.stack(
            [f_xi[pl.ds((g * 5 + k) * cz * cx + s, cz, stride=cx), :] for g in range(3)]
        )

    def keep_x(s, now):
        x_response[s] = now

    xi.put_matrices(responses(cx, xi_factor, keep_x))

    for number, (x, slots, origin) in enumerate(halos):
        for side in range(2):
            has = x.me > 0 if side == 0 else x.me < x.count - 1
            pl.when(has)(lambda number=number, side=side: halo_copy(number, side).wait_recv())

    source[:, :, 0:2, :] += hx[0]
    source[:, :, cx - 2 : cx, :] += hx[1]
    zeta_faces = {
        0: hz[0, :, 0] - 4.0 * hz[0, :, 1],
        1: hz[0, :, 1],
        cz - 2: hz[1, :, 0],
        cz - 1: hz[1, :, 1] - 4.0 * hz[1, :, 0],
    }
    faces = [jnp.where(lane % 4 >= 2, he[0, k], he[1, k]) for k in range(he.shape[1])]
    edge = jnp.logical_or(lane < 2, lane >= cy - 2)

    def eta_face(f, z):
        k = f * cz + z
        back = (cy - (4 * (k % per_pack) + 2)) % cy
        return jnp.where(edge, pltpu.roll(faces[k // per_pack], back, 1), 0.0)

    def source_plane(z):
        value = source[:, z] + jnp.stack([eta_face(f, z) for f in range(fields)])
        if z in zeta_faces:
            value = value - dissipation * zeta_faces[z]
        return value

    z_factor = lambda k, s: spread(f_zeta[:, k, s])
    zero = jnp.zeros((fields, cx, cy), jnp.float32)
    forward = forward_sweep(cz, z_factor, source_plane, zero, zero)
    zeta.put_ahead(jnp.stack([forward[-1], forward[-2]]))
    local = backward_sweep(cz, z_factor, lambda s: forward[s], zero, zero, lambda s, now: None)
    zeta.put_behind(jnp.stack([local[0], local[1]]))

    loads[4].wait()
    tiles = lines.shape[0] // cy
    steps = cy // sublanes
    total = lines.shape[0]
    order = list(field_group) + [field_group[-1]] * (total // (cz * cx) - fields)
    for k in range(5):
        whole = jnp.concatenate([f_eta[g * 5 + k] for g in order], 0)
        for t in range(tiles):
            turned_factors[k * total + t * cy : k * total + (t + 1) * cy, :] = whole[
                t * cy : (t + 1) * cy
            ].T

    zeta.solve()

    def eta_factor(k, s):
        return turned_factors[
            pl.ds(k * total + s, tiles * sublanes, stride=steps), :
        ].reshape(tiles, sublanes, cy)

    def keep_e(s, now):
        e_response[s] = now

    e_matrices[...] = responses(steps, eta_factor, keep_e)
    chunk = lambda c: [e_matrices[k, :, c : c + 1, :] for k in range(12)]
    one, zero = jnp.ones((1, tiles, 1, cy), jnp.float32), jnp.zeros((1, tiles, 1, cy), jnp.float32)
    unit = lambda j: jnp.concatenate([one if i == j else zero for i in range(4)], 0)
    inner, left = chain(sublanes, chunk, lambda c: None, [unit(j) for j in range(4)], False)
    for c, values in enumerate(inner):
        for k in range(4):
            e_inner[k, :, :, c : c + 1, :] = values[k]
    e_msend[...] = jnp.concatenate([left[0][0:2], left[1][0:2], left[2], left[3]], 0)
    e_mslots[xe.me] = e_msend[...]
    xe.start(0, lambda p: e_msend, e_mslots)

    incoming = zeta.result()
    for s in range(cz):
        done = corrected(local[s], z_response[s], incoming, spread)
        for f in range(fields):
            lines[(f * cz + s) * cx : (f * cz + s + 1) * cx, :] = done[f]
    if total > planes * cx:
        lines[planes * cx : total, :] = jnp.zeros((total - planes * cx, cy), jnp.float32)

    for t in range(tiles):
        turned[t * cy : (t + 1) * cy, :] = lines[t * cy : (t + 1) * cy, :].T
    zero = jnp.zeros((tiles, sublanes, cy), jnp.float32)

    def at_step(s):
        return pl.ds(s, tiles * sublanes, stride=steps)

    forward = forward_sweep(
        steps, eta_factor, lambda s: turned[at_step(s), :].reshape(zero.shape), zero, zero
    )
    local = backward_sweep(
        steps, eta_factor, lambda s: forward[s], zero, zero, lambda s, now: None
    )
    for k, value in enumerate((forward[-1], forward[-2], local[0], local[1])):
        e_offsets[k] = value
    none = jnp.zeros((tiles, 1, cy), jnp.float32)
    inner, left = chain(
        sublanes,
        chunk,
        lambda c: [e_offsets[k, :, c : c + 1, :] for k in range(4)],
        (none,) * 4,
        False,
    )
    for k in range(4):
        e_osend[k] = left[k]
    e_oslots[xe.me] = e_osend[...]
    xe.start(1, lambda p: e_osend, e_oslots)
    for c, values in enumerate(inner):
        for k in range(4):
            e_own[k, :, c : c + 1, :] = values[k]
    xe.wait_recv(0, lambda p: e_msend, e_mslots)
    xe.wait_recv(1, lambda p: e_osend, e_oslots)
    solved, _ = chain(
        n_eta,
        lambda q: [e_mslots[q, k] for k in range(12)],
        lambda q: [e_oslots[q, k] for k in range(4)],
        (none,) * 4,
        True,
    )
    for q, values in enumerate(solved):
        for k in range(4):
            e_result[q, k] = values[k]
    enters = [e_result[xe.me, k] for k in range(4)]
    incoming = []
    for k in range(4):
        value = e_own[k]
        for j in range(2 if k < 2 else 4):
            value = value + e_inner[k, j] * enters[j]
        incoming.append(value)
    for s in range(steps):
        done = corrected(local[s], e_response[s], incoming, lambda r: r)
        turned[at_step(s), :] = done.reshape(tiles * sublanes, cy)
    for t in range(tiles):
        lines[t * cy : (t + 1) * cy, :] = turned[t * cy : (t + 1) * cy, :].T

    x_factor = lambda k, s: spread(xi_factor(k, s))
    zero = jnp.zeros((fields, cz, cy), jnp.float32)
    forward = forward_sweep(
        cx,
        x_factor,
        lambda s: lines[pl.ds(s, planes, stride=cx), :].reshape(zero.shape),
        zero,
        zero,
    )
    xi.put_ahead(jnp.stack([forward[-1], forward[-2]]))
    local = backward_sweep(cx, x_factor, lambda s: forward[s], zero, zero, lambda s, now: None)
    xi.put_behind(jnp.stack([local[0], local[1]]))
    xi.solve()
    incoming = xi.result()
    for s in range(cx):
        done = corrected(local[s], x_response[s], incoming, spread)
        out[pl.ds(s, planes, stride=cx), :] = done.reshape(planes, cy)

    zeta.finish()
    xi.finish()
    xe.wait_send(0, lambda p: e_msend, e_mslots)
    xe.wait_send(1, lambda p: e_osend, e_oslots)
    for number, (x, slots, origin) in enumerate(halos):
        for side in range(2):
            sends = x.me < x.count - 1 if side == 0 else x.me > 0
            pl.when(sends)(lambda number=number, side=side: halo_copy(number, side).wait_send())


def split_scratch(count, fields, lanes):
    vmem = lambda *shape: pltpu.VMEM(shape, jnp.float32)
    parts = count if sublanes % count == 0 else 1
    rows = sublanes // parts
    return [
        vmem(parts, 12, 3, rows, lanes),
        vmem(count, 12, 3, rows, lanes),
        vmem(parts, 4, fields, rows, lanes),
        vmem(count, 4, fields, rows, lanes),
        vmem(count, 4, fields, rows, lanes),
        vmem(count, 4, fields, rows, lanes),
        vmem(4, fields, sublanes, lanes),
        pltpu.SemaphoreType.DMA((5, count)),
        pltpu.SemaphoreType.DMA((5, count)),
    ]


def on_device(counts, residual, flow_state, factors_zeta, factors_eta, factors_xi):
    n_xi, n_eta, n_zeta = counts
    fields, cz, cx, cy = flow_state.shape
    total = -(-(fields * cz * cx) // cy) * cy
    tiles = total // cy
    steps = cy // sublanes
    packs = -(-(fields * cz) // (cy // 4))
    vmem = lambda *shape: pltpu.VMEM(shape, jnp.float32)
    dma = pltpu.SemaphoreType.DMA
    whole = pl.BlockSpec(memory_space=pltpu.VMEM)
    scratch = (
        [
            vmem(fields, cz, cx, cy),
            vmem(fields, cz, cx, cy),
            vmem(3, 5, cz, cx, cy),
            vmem(15, cz * cx, cy),
            vmem(15 * cz * cx, cy),
            dma((5,)),
        ]
        + split_scratch(n_zeta, fields, cy)
        + split_scratch(n_xi, fields, cy)
        + [
            vmem(12, tiles, sublanes, cy),
            vmem(12, tiles, 1, cy),
            vmem(n_eta, 12, tiles, 1, cy),
            vmem(4, tiles, sublanes, cy),
            vmem(4, tiles, 1, cy),
            vmem(n_eta, 4, tiles, 1, cy),
            vmem(n_eta, 4, tiles, 1, cy),
            vmem(4, tiles, sublanes, cy),
            vmem(4, 4, tiles, sublanes, cy),
            dma((2, n_eta)),
            dma((2, n_eta)),
            vmem(cz, 4, 3, cx, cy),
            vmem(cx, 4, 3, cz, cy),
            vmem(steps, 4, tiles, sublanes, cy),
            vmem(total, cy),
            vmem(total, cy),
            vmem(5 * total, cy),
            vmem(2, fields, 2, cx, cy),
            vmem(2, fields, cz, 2, cy),
            vmem(2, fields, cz, 2, cy),
            vmem(packs, cx, cy),
            vmem(2, packs, cx, cy),
            vmem(fields, cz, cx + 16, cy),
            vmem(fields, cz, cx, cy),
            dma((3, 2)),
            dma((3, 2)),
        ]
    )
    update = pl.pallas_call(
        functools.partial(kernel, counts),
        out_shape=jax.ShapeDtypeStruct((fields * cz * cx, cy), jnp.float32),
        in_specs=[pl.BlockSpec(memory_space=pl.ANY)] * 5,
        out_specs=whole,
        scratch_shapes=scratch,
        compiler_params=pltpu.CompilerParams(
            collective_id=0, has_side_effects=True, vmem_limit_bytes=56 * 2**20
        ),
    )(
        residual,
        flow_state,
        factors_zeta,
        factors_eta.reshape(15, cz * cx, cy),
        factors_xi.reshape(15 * cz * cx, cy),
    )
    return update.reshape(flow_state.shape)


def solution(mesh):
    fields = P(None, "zeta", "xi", "eta")
    factors = P(None, None, "zeta", "xi", "eta")
    counts = tuple(mesh.shape[axis] for axis in ("xi", "eta", "zeta"))
    return jax.shard_map(
        functools.partial(on_device, counts),
        mesh=mesh,
        in_specs=(fields, fields, factors, factors, factors),
        out_specs=fields,
        check_vma=False,
    )
```

```python
import functools

import jax
import jax.numpy as jnp
from jax import lax
from jax.experimental import pallas as pl
from jax.experimental.pallas import tpu as pltpu
from jax.sharding import PartitionSpec as P

field_group = (0, 0, 0, 1, 2)
dissipation = 0.05
sublanes = 8
MESH = pl.DeviceIdType.MESH


line_order = (0, 3, 1, 4, 2)


def spread(planes):
    return jnp.concatenate([planes[g : g + 1] for g in field_group], 0)


def line_spread(planes):
    return jnp.concatenate([planes[field_group[f]][None] for f in line_order], 0)


def line_tiles(per_tile):
    distinct, uses = [], []
    for start in range(0, len(line_order), per_tile):
        groups = [field_group[f] for f in line_order[start : start + per_tile]]
        for number, have in enumerate(distinct):
            if have[: len(groups)] == groups:
                break
        else:
            number = len(distinct)
            distinct.append(groups + [groups[-1]] * (per_tile - len(groups)))
        uses.append(number)
    return distinct, uses


def forward_sweep(steps, factor, value, recent, before):
    rows = []
    for s in range(steps):
        now = -(factor(1, s) * before) if value is None else value(s) - factor(1, s) * before
        now = now - factor(0, s) * recent
        rows.append(now)
        recent, before = now, recent
    return rows


def backward_sweep(steps, factor, value, recent, before, keep):
    rows = [None] * steps
    for s in reversed(range(steps)):
        now = factor(2, s) * value(s) - factor(4, s) * before - factor(3, s) * recent
        rows[s] = now
        keep(s, now)
        recent, before = now, recent
    return rows


def responses(steps, factor, keep):
    one = jnp.ones_like(factor(0, 0))
    zero = jnp.zeros_like(one)
    lift = lambda k, s: factor(k, s)[None]
    forward = forward_sweep(
        steps, lift, None, jnp.stack([one, zero]), jnp.stack([zero, one])
    )
    none = jnp.zeros((2,) + one.shape, jnp.float32)
    backward = backward_sweep(
        steps,
        lift,
        lambda s: jnp.concatenate([forward[s], none], 0),
        jnp.stack([zero, zero, one, zero]),
        jnp.stack([zero, zero, zero, one]),
        keep,
    )
    return jnp.concatenate([forward[-1], forward[-2], backward[0], backward[1]], 0)


def chain(count, matrices, offsets, into, closed):
    c1, c2, d1, d2 = into
    entered = []
    for q in range(count):
        entered.append((c1, c2))
        if q < count - 1 or not closed:
            m, o = matrices(q), offsets(q)
            n1, n2 = m[0] * c1 + m[1] * c2, m[2] * c1 + m[3] * c2
            c1, c2 = (n1, n2) if o is None else (o[0] + n1, o[1] + n2)
    out = (c1, c2)
    result = [None] * count
    for q in reversed(range(count)):
        c1, c2 = entered[q]
        result[q] = (c1, c2, d1, d2)
        if q > 0 or not closed:
            m, o = matrices(q), offsets(q)
            n1, n2 = m[4] * c1 + m[5] * c2, m[8] * c1 + m[9] * c2
            if o is not None:
                n1, n2 = o[2] + n1, o[3] + n2
            d1, d2 = n1 + (m[6] * d1 + m[7] * d2), n2 + (m[10] * d1 + m[11] * d2)
    return result, out + (d1, d2)


class Exchange:
    def __init__(self, axis, count, send_sem, recv_sem):
        self.axis, self.count = axis, count
        self.send_sem, self.recv_sem = send_sem, recv_sem
        self.me = lax.axis_index(axis)

    def peers(self):
        return [lax.rem(self.me + k, self.count) for k in range(1, self.count)]

    def copy(self, kind, source, slots, p, slot, cut):
        pick = (lambda ref: ref) if cut is None else (lambda ref: ref.at[cut[0] : cut[1]])
        return pltpu.make_async_remote_copy(
            src_ref=pick(source(p)),
            dst_ref=pick(slots.at[slot]),
            send_sem=self.send_sem.at[kind, p],
            recv_sem=self.recv_sem.at[kind, slot],
            device_id={self.axis: p},
            device_id_type=MESH,
        )

    def start(self, kind, source, slots, cut=None, sends=None):
        for p in self.peers():
            go = lambda p=p: self.copy(kind, source, slots, p, self.me, cut).start()
            go() if sends is None else pl.when(sends(self.me, p))(go)

    def wait_recv(self, kind, source, slots, cut=None, sends=None):
        for p in self.peers():
            go = lambda p=p: self.copy(kind, source, slots, p, p, cut).wait_recv()
            go() if sends is None else pl.when(sends(p, self.me))(go)

    def wait_send(self, kind, source, slots, cut=None, sends=None):
        for p in self.peers():
            go = lambda p=p: self.copy(kind, source, slots, p, self.me, cut).wait_send()
            go() if sends is None else pl.when(sends(self.me, p))(go)


class Split:
    def __init__(self, exchange, lift, m_send, m_slots, o_send, o_slots, r_send, r_slots, full):
        self.x, self.lift = exchange, lift
        self.m_send, self.m_slots = m_send, m_slots
        self.o_send, self.o_slots = o_send, o_slots
        self.r_send, self.r_slots, self.full = r_send, r_slots, full
        self.parts = m_send.shape[0]
        self.rows = sublanes // self.parts
        pick = (lambda p: p) if self.parts > 1 else (lambda p: 0)
        last = exchange.count - 1
        m_from = lambda p: m_send.at[pick(p)]
        o_from = lambda p: o_send.at[pick(p)]
        r_from = lambda p: r_send.at[p]
        self.matrices = (0, m_from, m_slots)
        self.ahead = (1, o_from, o_slots, (0, 2), lambda a, b: a < last)
        self.behind = (2, o_from, o_slots, (2, 4), lambda a, b: a > 0)
        self.carried = (3, r_from, r_slots, (0, 2), lambda a, b: b > 0)
        self.returned = (4, r_from, r_slots, (2, 4), lambda a, b: b < last)
        self.pick = pick

    def clear_ends(self):
        if self.parts > 1:
            nothing = jnp.zeros((self.parts, 2) + self.r_slots.shape[2:], jnp.float32)

            @pl.when(self.x.me == 0)
            def _():
                self.r_slots[:, 0:2] = nothing

            @pl.when(self.x.me == self.x.count - 1)
            def _():
                self.r_slots[:, 2:4] = nothing

    def put(self, route, value, send, slots, lo):
        hi = lo + value.shape[0]
        for p in range(self.parts):
            send[p, lo:hi] = value[:, :, p * self.rows : (p + 1) * self.rows, :]
        slots[self.x.me, lo:hi] = send[self.pick(self.x.me), lo:hi]
        self.x.start(*route)

    def put_matrices(self, value):
        self.put(self.matrices, value, self.m_send, self.m_slots, 0)

    def put_ahead(self, value):
        self.put(self.ahead, value, self.o_send, self.o_slots, 0)

    def put_behind(self, value):
        self.put(self.behind, value, self.o_send, self.o_slots, 2)

    def solve(self):
        x = self.x
        for route in (self.matrices, self.ahead, self.behind):
            x.wait_recv(*route)
        zero = jnp.zeros(self.o_slots.shape[2:], jnp.float32)
        solved, _ = chain(
            x.count,
            lambda q: [self.lift(self.m_slots[q, k]) for k in range(12)],
            lambda q: [self.o_slots[q, k] for k in range(4)],
            (zero,) * 4,
            True,
        )
        for q, planes in enumerate(solved):
            for k in range(4):
                self.r_send[q, k] = planes[k]
        if self.parts > 1:
            x.start(*self.carried)
            x.start(*self.returned)
            me = x.me

            @pl.when(me > 0)
            def _():
                self.r_slots[me, 0:2] = self.r_send[me, 0:2]

            @pl.when(me < x.count - 1)
            def _():
                self.r_slots[me, 2:4] = self.r_send[me, 2:4]

    def result(self):
        x = self.x
        if self.parts == 1:
            return [self.r_send[x.me, k] for k in range(4)]
        x.wait_recv(*self.carried)
        x.wait_recv(*self.returned)
        for p in range(self.parts):
            self.full[:, :, p * self.rows : (p + 1) * self.rows, :] = self.r_slots[p]
        return [self.full[k] for k in range(4)]

    def finish(self):
        for route in (self.matrices, self.ahead, self.behind):
            self.x.wait_send(*route)
        if self.parts > 1:
            self.x.wait_send(*self.carried)
            self.x.wait_send(*self.returned)


def corrected(local, response, incoming, lift):
    total = local
    for k in range(4):
        total = total + lift(response[k]) * incoming[k]
    return total


def kernel(
    counts, residual_hbm, flow_hbm, f_zeta_hbm, f_eta_hbm, f_xi_hbm, out,
    residual, flow, f_zeta, f_eta, f_xi, in_sem,
    z_msend, z_mslots, z_osend, z_oslots, z_rsend, z_rslots, z_full, z_ss, z_rs,
    x_msend, x_mslots, x_osend, x_oslots, x_rsend, x_rslots, x_full, x_ss, x_rs,
    e_matrices, e_msend, e_mslots, e_offsets, e_osend, e_oslots, e_result, e_own, e_inner,
    e_ss, e_rs,
    z_response, x_response, e_response, x_factors, e_factors, lines, turned, turned_factors,
    hz, hx_send, hx, he_send, he, padded, source, h_ss, h_rs,
):
    n_xi, n_eta, n_zeta = counts
    fields, cz, cx, cy = flow.shape
    planes = fields * cz
    xz = Exchange("zeta", n_zeta, z_ss, z_rs)
    xe = Exchange("eta", n_eta, e_ss, e_rs)
    xx = Exchange("xi", n_xi, x_ss, x_rs)
    zeta = Split(xz, spread, z_msend, z_mslots, z_osend, z_oslots, z_rsend, z_rslots, z_full)
    xi = Split(xx, line_spread, x_msend, x_mslots, x_osend, x_oslots, x_rsend, x_rslots, x_full)

    barrier = pltpu.get_barrier_semaphore()
    greeted = 0
    for x in (xz, xe, xx):
        for p in x.peers():
            pl.semaphore_signal(barrier, inc=1, device_id={x.axis: p}, device_id_type=MESH)
            greeted += 1

    loads = [
        pltpu.make_async_copy(src, dst, in_sem.at[k])
        for k, (src, dst) in enumerate(
            (
                (flow_hbm, flow),
                (f_zeta_hbm, f_zeta),
                (f_xi_hbm, f_xi),
                (residual_hbm, residual),
                (f_eta_hbm, f_eta),
            )
        )
    ]
    for load in loads:
        load.start()
    zeta.clear_ends()
    xi.clear_ends()
    loads[0].wait()

    per_pack = cy // 4
    lane = lax.broadcasted_iota(jnp.int32, (cx, cy), 1)
    packs = [jnp.zeros((cx, cy), jnp.float32) for _ in range(he_send.shape[0])]
    eta_part = []
    for k in range(planes):
        at = k % per_pack
        v = flow[k // cz, k % cz]
        up1, up2 = pltpu.roll(v, 1, 1), pltpu.roll(v, 2, 1)
        down1, down2 = pltpu.roll(v, cy - 1, 1), pltpu.roll(v, cy - 2, 1)
        near_low, near_high = lane < 1, lane >= cy - 1
        far_low, far_high = lane < 2, lane >= cy - 2
        near = jnp.where(near_low, 0.0, up1) + jnp.where(near_high, 0.0, down1)
        far = jnp.where(far_low, 0.0, up2) + jnp.where(far_high, 0.0, down2)
        eta_part.append(far - 4.0 * near)
        near = jnp.where(near_low, up1, jnp.where(near_high, down1, 0.0))
        far = jnp.where(far_low, up2, jnp.where(far_high, down2, 0.0))
        face = -dissipation * (far - 4.0 * near)
        moved = pltpu.roll(face, (4 * at + 2) % cy, 1)
        packs[k // per_pack] = jnp.where(lane // 4 == at, moved, packs[k // per_pack])
    for k, pack in enumerate(packs):
        he_send[k] = pack
    row = lambda x: flow[:, :, x : x + 1, :]
    hx_send[0, :, :, 0:1, :] = -dissipation * (row(cx - 2) - 4.0 * row(cx - 1))
    hx_send[0, :, :, 1:2, :] = -dissipation * row(cx - 1)
    hx_send[1, :, :, 0:1, :] = -dissipation * row(0)
    hx_send[1, :, :, 1:2, :] = -dissipation * (row(1) - 4.0 * row(0))

    pl.semaphore_wait(barrier, greeted)

    halos = (
        (xx, hx, lambda side: hx_send.at[side]),
        (xe, he, lambda side: he_send),
        (xz, hz, lambda side: flow.at[:, cz - 2 : cz] if side == 0 else flow.at[:, 0:2]),
    )

    def halo_copy(number, side):
        x, slots, origin = halos[number]
        step = 1 if side == 0 else x.count - 1
        return pltpu.make_async_remote_copy(
            src_ref=origin(side),
            dst_ref=slots.at[side],
            send_sem=h_ss.at[number, side],
            recv_sem=h_rs.at[number, side],
            device_id={x.axis: lax.rem(x.me + step, x.count)},
            device_id_type=MESH,
        )

    for number, (x, slots, origin) in enumerate(halos):
        for side in range(2):
            sends = x.me < x.count - 1 if side == 0 else x.me > 0
            has = x.me > 0 if side == 0 else x.me < x.count - 1
            pl.when(sends)(lambda number=number, side=side: halo_copy(number, side).start())

            @pl.when(jnp.logical_not(has))
            def _(slots=slots, side=side):
                slots[side] = jnp.zeros(slots.shape[1:], jnp.float32)

    loads[1].wait()

    def keep_z(s, now):
        z_response[s] = now

    zeta.put_matrices(responses(cz, lambda k, s: f_zeta[:, k, s], keep_z))

    state = flow[...]
    nothing = jnp.zeros((fields, cz, 2, cy), jnp.float32)
    padded[:, :, 8 - 2 : 8, :] = nothing
    padded[:, :, 8 : 8 + cx, :] = state
    padded[:, :, 8 + cx : 8 + cx + 2, :] = nothing
    none = jnp.zeros((fields, 2, cx, cy), jnp.float32)
    long = jnp.concatenate([none, state, none], 1)
    near = (padded[:, :, 7 : 7 + cx, :] + padded[:, :, 9 : 9 + cx, :]) + (
        long[:, 1 : 1 + cz] + long[:, 3 : 3 + cz]
    )
    far = (padded[:, :, 6 : 6 + cx, :] + padded[:, :, 10 : 10 + cx, :]) + (
        long[:, 0:cz] + long[:, 4 : 4 + cz]
    )
    total_part = 18.0 * state - 4.0 * near + far + jnp.stack(eta_part).reshape(flow.shape)
    loads[3].wait()
    source[...] = residual[...] - dissipation * total_part

    loads[2].wait()

    for s in range(cx):
        for k in range(5):
            for g in range(3):
                x_factors[k, s, g] = f_xi[pl.ds((g * 5 + k) * cz * cx + s, cz, stride=cx), :]

    def xi_factor(k, s):
        return x_factors[k, s]

    def keep_x(s, now):
        x_response[s] = now

    xi.put_matrices(responses(cx, xi_factor, keep_x))

    for number, (x, slots, origin) in enumerate(halos):
        for side in range(2):
            has = x.me > 0 if side == 0 else x.me < x.count - 1
            pl.when(has)(lambda number=number, side=side: halo_copy(number, side).wait_recv())

    source[:, :, 0:2, :] += hx[0]
    source[:, :, cx - 2 : cx, :] += hx[1]
    zeta_faces = {
        0: hz[0, :, 0] - 4.0 * hz[0, :, 1],
        1: hz[0, :, 1],
        cz - 2: hz[1, :, 0],
        cz - 1: hz[1, :, 1] - 4.0 * hz[1, :, 0],
    }
    faces = [jnp.where(lane % 4 >= 2, he[0, k], he[1, k]) for k in range(he.shape[1])]
    edge = jnp.logical_or(lane < 2, lane >= cy - 2)

    def eta_face(f, z):
        k = f * cz + z
        back = (cy - (4 * (k % per_pack) + 2)) % cy
        return jnp.where(edge, pltpu.roll(faces[k // per_pack], back, 1), 0.0)

    def source_plane(z):
        value = source[:, z] + jnp.stack([eta_face(f, z) for f in range(fields)])
        if z in zeta_faces:
            value = value - dissipation * zeta_faces[z]
        return value

    z_factor = lambda k, s: spread(f_zeta[:, k, s])
    zero = jnp.zeros((fields, cx, cy), jnp.float32)
    forward = forward_sweep(cz, z_factor, source_plane, zero, zero)
    zeta.put_ahead(jnp.stack([forward[-1], forward[-2]]))
    local = backward_sweep(cz, z_factor, lambda s: forward[s], zero, zero, lambda s, now: None)
    zeta.put_behind(jnp.stack([local[0], local[1]]))

    loads[4].wait()
    tiles = lines.shape[0] // cy
    steps = cy // sublanes
    total = lines.shape[0]
    distinct, uses = line_tiles(cy // (cz * cx))
    for k in range(5):
        for t, groups in enumerate(distinct):
            whole = jnp.concatenate([f_eta[g * 5 + k] for g in groups], 0)
            turned_factors[t * cy : (t + 1) * cy, :] = whole.T
        for s in range(steps):
            e_factors[k, s] = turned_factors[
                pl.ds(s, len(distinct) * sublanes, stride=steps), :
            ].reshape(len(distinct), sublanes, cy)

    def tiled(planes):
        return jnp.concatenate([planes[u : u + 1] for u in uses], 0)

    zeta.solve()

    def eta_factor(k, s):
        return e_factors[k, s]

    def keep_e(s, now):
        e_response[s] = now

    e_matrices[...] = responses(steps, eta_factor, keep_e)
    chunk = lambda c: [e_matrices[k, :, c : c + 1, :] for k in range(12)]
    one = jnp.ones((1, len(distinct), 1, cy), jnp.float32)
    zero = jnp.zeros_like(one)
    unit = lambda j: jnp.concatenate([one if i == j else zero for i in range(4)], 0)
    inner, left = chain(sublanes, chunk, lambda c: None, [unit(j) for j in range(4)], False)
    for c, values in enumerate(inner):
        for k in range(4):
            e_inner[k, :, :, c : c + 1, :] = values[k]
    e_msend[...] = jnp.concatenate([left[0][0:2], left[1][0:2], left[2], left[3]], 0)
    e_mslots[xe.me] = e_msend[...]
    xe.start(0, lambda p: e_msend, e_mslots)

    incoming = zeta.result()
    for s in range(cz):
        done = corrected(local[s], z_response[s], incoming, spread)
        for place, f in enumerate(line_order):
            lines[(place * cz + s) * cx : (place * cz + s + 1) * cx, :] = done[f]
    if total > planes * cx:
        lines[planes * cx : total, :] = jnp.zeros((total - planes * cx, cy), jnp.float32)

    for t in range(tiles):
        turned[t * cy : (t + 1) * cy, :] = lines[t * cy : (t + 1) * cy, :].T
    zero = jnp.zeros((tiles, sublanes, cy), jnp.float32)

    eta_tiles = lambda k, s: tiled(e_factors[k, s])

    def at_step(s):
        return pl.ds(s, tiles * sublanes, stride=steps)

    forward = forward_sweep(
        steps, eta_tiles, lambda s: turned[at_step(s), :].reshape(zero.shape), zero, zero
    )
    local = backward_sweep(
        steps, eta_tiles, lambda s: forward[s], zero, zero, lambda s, now: None
    )
    for k, value in enumerate((forward[-1], forward[-2], local[0], local[1])):
        e_offsets[k] = value
    none = jnp.zeros((tiles, 1, cy), jnp.float32)
    inner, left = chain(
        sublanes,
        lambda c: [tiled(plane) for plane in chunk(c)],
        lambda c: [e_offsets[k, :, c : c + 1, :] for k in range(4)],
        (none,) * 4,
        False,
    )
    for k in range(4):
        e_osend[k] = left[k]
    e_oslots[xe.me] = e_osend[...]
    xe.start(1, lambda p: e_osend, e_oslots)
    for c, values in enumerate(inner):
        for k in range(4):
            e_own[k, :, c : c + 1, :] = values[k]
    xe.wait_recv(0, lambda p: e_msend, e_mslots)
    xe.wait_recv(1, lambda p: e_osend, e_oslots)
    solved, _ = chain(
        n_eta,
        lambda q: [tiled(e_mslots[q, k]) for k in range(12)],
        lambda q: [e_oslots[q, k] for k in range(4)],
        (none,) * 4,
        True,
    )
    for q, values in enumerate(solved):
        for k in range(4):
            e_result[q, k] = values[k]
    enters = [e_result[xe.me, k] for k in range(4)]
    incoming = []
    for k in range(4):
        value = e_own[k]
        for j in range(2 if k < 2 else 4):
            value = value + tiled(e_inner[k, j]) * enters[j]
        incoming.append(value)
    for s in range(steps):
        done = corrected(local[s], e_response[s], incoming, tiled)
        turned[at_step(s), :] = done.reshape(tiles * sublanes, cy)
    for t in range(tiles):
        lines[t * cy : (t + 1) * cy, :] = turned[t * cy : (t + 1) * cy, :].T

    x_factor = lambda k, s: line_spread(xi_factor(k, s))
    zero = jnp.zeros((fields, cz, cy), jnp.float32)
    forward = forward_sweep(
        cx,
        x_factor,
        lambda s: lines[pl.ds(s, planes, stride=cx), :].reshape(zero.shape),
        zero,
        zero,
    )
    xi.put_ahead(jnp.stack([forward[-1], forward[-2]]))
    local = backward_sweep(cx, x_factor, lambda s: forward[s], zero, zero, lambda s, now: None)
    xi.put_behind(jnp.stack([local[0], local[1]]))
    xi.solve()
    incoming = xi.result()
    for s in range(cx):
        done = corrected(local[s], x_response[s], incoming, line_spread)
        for place, f in enumerate(line_order):
            out[pl.ds(f * cz * cx + s, cz, stride=cx), :] = done[place]

    zeta.finish()
    xi.finish()
    xe.wait_send(0, lambda p: e_msend, e_mslots)
    xe.wait_send(1, lambda p: e_osend, e_oslots)
    for number, (x, slots, origin) in enumerate(halos):
        for side in range(2):
            sends = x.me < x.count - 1 if side == 0 else x.me > 0
            pl.when(sends)(lambda number=number, side=side: halo_copy(number, side).wait_send())


def split_scratch(count, fields, lanes):
    vmem = lambda *shape: pltpu.VMEM(shape, jnp.float32)
    parts = count if sublanes % count == 0 else 1
    rows = sublanes // parts
    return [
        vmem(parts, 12, 3, rows, lanes),
        vmem(count, 12, 3, rows, lanes),
        vmem(parts, 4, fields, rows, lanes),
        vmem(count, 4, fields, rows, lanes),
        vmem(count, 4, fields, rows, lanes),
        vmem(count, 4, fields, rows, lanes),
        vmem(4, fields, sublanes, lanes),
        pltpu.SemaphoreType.DMA((5, count)),
        pltpu.SemaphoreType.DMA((5, count)),
    ]


def on_device(counts, residual, flow_state, factors_zeta, factors_eta, factors_xi):
    n_xi, n_eta, n_zeta = counts
    fields, cz, cx, cy = flow_state.shape
    total = -(-(fields * cz * cx) // cy) * cy
    tiles = total // cy
    steps = cy // sublanes
    packs = -(-(fields * cz) // (cy // 4))
    distinct = len(line_tiles(cy // (cz * cx))[0])
    vmem = lambda *shape: pltpu.VMEM(shape, jnp.float32)
    dma = pltpu.SemaphoreType.DMA
    whole = pl.BlockSpec(memory_space=pltpu.VMEM)
    scratch = (
        [
            vmem(fields, cz, cx, cy),
            vmem(fields, cz, cx, cy),
            vmem(3, 5, cz, cx, cy),
            vmem(15, cz * cx, cy),
            vmem(15 * cz * cx, cy),
            dma((5,)),
        ]
        + split_scratch(n_zeta, fields, cy)
        + split_scratch(n_xi, fields, cy)
        + [
            vmem(12, distinct, sublanes, cy),
            vmem(12, distinct, 1, cy),
            vmem(n_eta, 12, distinct, 1, cy),
            vmem(4, tiles, sublanes, cy),
            vmem(4, tiles, 1, cy),
            vmem(n_eta, 4, tiles, 1, cy),
            vmem(n_eta, 4, tiles, 1, cy),
            vmem(4, tiles, sublanes, cy),
            vmem(4, 4, distinct, sublanes, cy),
            dma((2, n_eta)),
            dma((2, n_eta)),
            vmem(cz, 4, 3, cx, cy),
            vmem(cx, 4, 3, cz, cy),
            vmem(steps, 4, distinct, sublanes, cy),
            vmem(5, cx, 3, cz, cy),
            vmem(5, steps, distinct, sublanes, cy),
            vmem(total, cy),
            vmem(total, cy),
            vmem(distinct * cy, cy),
            vmem(2, fields, 2, cx, cy),
            vmem(2, fields, cz, 2, cy),
            vmem(2, fields, cz, 2, cy),
            vmem(packs, cx, cy),
            vmem(2, packs, cx, cy),
            vmem(fields, cz, cx + 16, cy),
            vmem(fields, cz, cx, cy),
            dma((3, 2)),
            dma((3, 2)),
        ]
    )
    update = pl.pallas_call(
        functools.partial(kernel, counts),
        out_shape=jax.ShapeDtypeStruct((fields * cz * cx, cy), jnp.float32),
        in_specs=[pl.BlockSpec(memory_space=pltpu.HBM)] * 5,
        out_specs=whole,
        scratch_shapes=scratch,
        compiler_params=pltpu.CompilerParams(
            collective_id=0, has_side_effects=True, vmem_limit_bytes=24 * 2**20
        ),
    )(
        *(
            pltpu.with_memory_space_constraint(operand, pltpu.HBM)
            for operand in (
                residual,
                flow_state,
                factors_zeta,
                factors_eta.reshape(15, cz * cx, cy),
                factors_xi.reshape(15 * cz * cx, cy),
            )
        )
    )
    return update.reshape(flow_state.shape)


def solution(mesh):
    fields = P(None, "zeta", "xi", "eta")
    factors = P(None, None, "zeta", "xi", "eta")
    counts = tuple(mesh.shape[axis] for axis in ("xi", "eta", "zeta"))
    return jax.shard_map(
        functools.partial(on_device, counts),
        mesh=mesh,
        in_specs=(fields, fields, factors, factors, factors),
        out_specs=fields,
        check_vma=False,
    )
```

```python
import functools

import jax
import jax.numpy as jnp
from jax import lax
from jax.experimental import pallas as pl
from jax.experimental.pallas import tpu as pltpu
from jax.sharding import PartitionSpec as P

field_group = (0, 0, 0, 1, 2)
dissipation = 0.05
sublanes = 8
MESH = pl.DeviceIdType.MESH


line_order = (0, 3, 1, 4, 2)


def spread(planes):
    return jnp.concatenate([planes[g : g + 1] for g in field_group], 0)


def line_spread(planes):
    return jnp.concatenate([planes[field_group[f]][None] for f in line_order], 0)


def line_tiles(per_tile):
    distinct, uses = [], []
    for start in range(0, len(line_order), per_tile):
        groups = [field_group[f] for f in line_order[start : start + per_tile]]
        for number, have in enumerate(distinct):
            if have[: len(groups)] == groups:
                break
        else:
            number = len(distinct)
            distinct.append(groups + [groups[-1]] * (per_tile - len(groups)))
        uses.append(number)
    return distinct, uses


def forward_sweep(steps, factor, value, recent, before):
    rows = []
    for s in range(steps):
        now = -(factor(1, s) * before) if value is None else value(s) - factor(1, s) * before
        now = now - factor(0, s) * recent
        rows.append(now)
        recent, before = now, recent
    return rows


def backward_sweep(steps, factor, value, recent, before, keep):
    rows = [None] * steps
    for s in reversed(range(steps)):
        now = factor(2, s) * value(s) - factor(4, s) * before - factor(3, s) * recent
        rows[s] = now
        keep(s, now)
        recent, before = now, recent
    return rows


def responses(steps, factor, keep):
    one = jnp.ones_like(factor(0, 0))
    zero = jnp.zeros_like(one)
    lift = lambda k, s: factor(k, s)[None]
    forward = forward_sweep(
        steps, lift, None, jnp.stack([one, zero]), jnp.stack([zero, one])
    )
    none = jnp.zeros((2,) + one.shape, jnp.float32)
    backward = backward_sweep(
        steps,
        lift,
        lambda s: jnp.concatenate([forward[s], none], 0),
        jnp.stack([zero, zero, one, zero]),
        jnp.stack([zero, zero, zero, one]),
        keep,
    )
    return jnp.concatenate([forward[-1], forward[-2], backward[0], backward[1]], 0)


def chain(count, matrices, offsets, into, closed):
    c1, c2, d1, d2 = into
    entered = []
    for q in range(count):
        entered.append((c1, c2))
        if q < count - 1 or not closed:
            m, o = matrices(q), offsets(q)
            n1, n2 = m[0] * c1 + m[1] * c2, m[2] * c1 + m[3] * c2
            c1, c2 = (n1, n2) if o is None else (o[0] + n1, o[1] + n2)
    out = (c1, c2)
    result = [None] * count
    for q in reversed(range(count)):
        c1, c2 = entered[q]
        result[q] = (c1, c2, d1, d2)
        if q > 0 or not closed:
            m, o = matrices(q), offsets(q)
            n1, n2 = m[4] * c1 + m[5] * c2, m[8] * c1 + m[9] * c2
            if o is not None:
                n1, n2 = o[2] + n1, o[3] + n2
            d1, d2 = n1 + (m[6] * d1 + m[7] * d2), n2 + (m[10] * d1 + m[11] * d2)
    return result, out + (d1, d2)


class Exchange:
    def __init__(self, axis, count, send_sem, recv_sem):
        self.axis, self.count = axis, count
        self.send_sem, self.recv_sem = send_sem, recv_sem
        self.me = lax.axis_index(axis)

    def peers(self):
        return [lax.rem(self.me + k, self.count) for k in range(1, self.count)]

    def copy(self, kind, source, slots, p, slot, cut):
        pick = (lambda ref: ref) if cut is None else (lambda ref: ref.at[cut[0] : cut[1]])
        return pltpu.make_async_remote_copy(
            src_ref=pick(source(p)),
            dst_ref=pick(slots.at[slot]),
            send_sem=self.send_sem.at[kind, p],
            recv_sem=self.recv_sem.at[kind, slot],
            device_id={self.axis: p},
            device_id_type=MESH,
        )

    def start(self, kind, source, slots, cut=None, sends=None):
        for p in self.peers():
            go = lambda p=p: self.copy(kind, source, slots, p, self.me, cut).start()
            go() if sends is None else pl.when(sends(self.me, p))(go)

    def wait_recv(self, kind, source, slots, cut=None, sends=None):
        for p in self.peers():
            go = lambda p=p: self.copy(kind, source, slots, p, p, cut).wait_recv()
            go() if sends is None else pl.when(sends(p, self.me))(go)

    def wait_send(self, kind, source, slots, cut=None, sends=None):
        for p in self.peers():
            go = lambda p=p: self.copy(kind, source, slots, p, self.me, cut).wait_send()
            go() if sends is None else pl.when(sends(self.me, p))(go)


class Split:
    def __init__(self, exchange, lift, m_send, m_slots, o_send, o_slots, r_send, r_slots, full):
        self.x, self.lift = exchange, lift
        self.m_send, self.m_slots = m_send, m_slots
        self.o_send, self.o_slots = o_send, o_slots
        self.r_send, self.r_slots, self.full = r_send, r_slots, full
        self.parts = m_send.shape[0]
        self.rows = sublanes // self.parts
        pick = (lambda p: p) if self.parts > 1 else (lambda p: 0)
        last = exchange.count - 1
        m_from = lambda p: m_send.at[pick(p)]
        o_from = lambda p: o_send.at[pick(p)]
        r_from = lambda p: r_send.at[p]
        self.matrices = (0, m_from, m_slots)
        self.ahead = (1, o_from, o_slots, (0, 2), lambda a, b: a < last)
        self.behind = (2, o_from, o_slots, (2, 4), lambda a, b: a > 0)
        self.carried = (3, r_from, r_slots, (0, 2), lambda a, b: b > 0)
        self.returned = (4, r_from, r_slots, (2, 4), lambda a, b: b < last)
        self.pick = pick

    def clear_ends(self):
        if self.parts > 1:
            nothing = jnp.zeros((self.parts, 2) + self.r_slots.shape[2:], jnp.float32)

            @pl.when(self.x.me == 0)
            def _():
                self.r_slots[:, 0:2] = nothing

            @pl.when(self.x.me == self.x.count - 1)
            def _():
                self.r_slots[:, 2:4] = nothing

    def put(self, route, value, send, slots, lo):
        hi = lo + value.shape[0]
        for p in range(self.parts):
            send[p, lo:hi] = value[:, :, p * self.rows : (p + 1) * self.rows, :]
        slots[self.x.me, lo:hi] = send[self.pick(self.x.me), lo:hi]
        self.x.start(*route)

    def put_matrices(self, value):
        self.put(self.matrices, value, self.m_send, self.m_slots, 0)

    def join_matrices(self):
        pass

    def put_ahead(self, value):
        self.put(self.ahead, value, self.o_send, self.o_slots, 0)

    def put_behind(self, value):
        self.put(self.behind, value, self.o_send, self.o_slots, 2)

    def solve(self):
        x = self.x
        for route in (self.matrices, self.ahead, self.behind):
            x.wait_recv(*route)
        zero = jnp.zeros(self.o_slots.shape[2:], jnp.float32)
        solved, _ = chain(
            x.count,
            lambda q: [self.lift(self.m_slots[q, k]) for k in range(12)],
            lambda q: [self.o_slots[q, k] for k in range(4)],
            (zero,) * 4,
            True,
        )
        for q, planes in enumerate(solved):
            for k in range(4):
                self.r_send[q, k] = planes[k]
        if self.parts > 1:
            x.start(*self.carried)
            x.start(*self.returned)
            me = x.me

            @pl.when(me > 0)
            def _():
                self.r_slots[me, 0:2] = self.r_send[me, 0:2]

            @pl.when(me < x.count - 1)
            def _():
                self.r_slots[me, 2:4] = self.r_send[me, 2:4]

    def result(self):
        x = self.x
        if self.parts == 1:
            return [self.r_send[x.me, k] for k in range(4)]
        x.wait_recv(*self.carried)
        x.wait_recv(*self.returned)
        for p in range(self.parts):
            self.full[:, :, p * self.rows : (p + 1) * self.rows, :] = self.r_slots[p]
        return [self.full[k] for k in range(4)]

    def finish(self):
        for route in (self.matrices, self.ahead, self.behind):
            self.x.wait_send(*route)
        if self.parts > 1:
            self.x.wait_send(*self.carried)
            self.x.wait_send(*self.returned)


def times(m, v):
    return m[0] * v[0] + m[1] * v[1], m[2] * v[0] + m[3] * v[1]


def plus(a, b):
    return a[0] + b[0], a[1] + b[1]


class Pairs:
    def __init__(
        self, exchange, lift, m_own, m_in, g_own, g_in, o_own, o_in, j_own, j_in, full, ss, rs
    ):
        self.axis, self.me, self.lift = exchange.axis, exchange.me, lift
        self.m_own, self.m_in, self.g_own, self.g_in = m_own, m_in, g_own, g_in
        self.o_own, self.o_in, self.j_own, self.j_in, self.full = o_own, o_in, j_own, j_in, full
        ahead, behind, top, mid = (slice(0, 2), slice(2, 4), slice(0, 4), slice(4, 8))
        cut = lambda a, b, part: (a.at[part], b.at[part])
        self.messages = [
            (0, 1, 0, m_own, m_in),
            (0, 3, 2, *cut(m_own, m_in, mid)),
            (0, 2, 3, *cut(m_own, m_in, top)),
            (1, 2, 1, g_own, g_in),
            (1, 2, 0, g_own, g_in),
            (2, 0, 1, *cut(o_own, o_in, ahead)),
            (2, 1, 0, *cut(o_own, o_in, ahead)),
            (2, 2, 3, *cut(o_own, o_in, ahead)),
            (3, 1, 0, *cut(o_own, o_in, behind)),
            (3, 3, 2, *cut(o_own, o_in, behind)),
            (4, 1, 2, j_own, j_in),
            (4, 1, 3, j_own, j_in),
            (4, 2, 1, j_own, j_in),
            (4, 2, 0, j_own, j_in),
        ]
        self.ss, self.rs = ss, rs

    def copy(self, message):
        kind, _, to, source, destination = message
        return pltpu.make_async_remote_copy(
            src_ref=source,
            dst_ref=destination,
            send_sem=self.ss.at[kind, to],
            recv_sem=self.rs.at[kind],
            device_id={self.axis: to},
            device_id_type=MESH,
        )

    def role(self, number):
        return pl.when(self.me == number)

    def start(self, kind, number):
        for message in self.messages:
            if message[0] == kind and message[1] == number:
                self.copy(message).start()

    def start_all(self, kind):
        for number in range(4):
            if any(m[0] == kind and m[1] == number for m in self.messages):
                self.role(number)(lambda number=number: self.start(kind, number))

    def wait(self, kind, number):
        for message in self.messages:
            if message[0] == kind and message[2] == number:
                self.copy(message).wait_recv()

    def lifted(self, ref, part):
        return [self.lift(ref[k]) for k in range(part.start, part.stop)]

    def clear_ends(self):
        pass

    def put_matrices(self, value):
        for place, k in enumerate((0, 1, 2, 3, 4, 5, 8, 9, 6, 7, 10, 11)):
            self.m_own[place] = value[k]
        self.start_all(0)

    def join_matrices(self):
        @self.role(2)
        def _():
            self.wait(0, 2)
            own = [self.m_own[k] for k in range(12)]
            far = [self.m_in[4 + k] for k in range(4)]
            columns = []
            for j in range(2):
                through = times(far, (own[j], own[2 + j]))
                columns.append(plus((own[4 + j], own[6 + j]), times(own[8:12], through)))
            for i in range(2):
                for j in range(2):
                    self.g_own[2 * i + j] = columns[j][i]
            self.start(1, 2)

    def put_ahead(self, value):
        self.o_own[0:2] = value
        self.start_all(2)

    def put_behind(self, value):
        self.o_own[2:4] = value
        self.start_all(3)

    def solve(self):
        @self.role(1)
        def _():
            self.wait(2, 1)
            t = self.lifted(self.m_own, slice(0, 4))
            c = plus((self.o_own[0], self.o_own[1]), times(t, (self.o_in[0], self.o_in[1])))
            self.j_own[0], self.j_own[1] = c
            self.start(4, 1)

        @self.role(2)
        def _():
            self.wait(3, 2)
            b = self.lifted(self.m_in, slice(4, 8))
            d = self.lifted(self.m_own, slice(8, 12))
            far = plus((self.o_in[2], self.o_in[3]), times(b, (self.o_own[0], self.o_own[1])))
            g = plus((self.o_own[2], self.o_own[3]), times(d, far))
            self.j_own[0], self.j_own[1] = g
            self.start(4, 2)

    def result(self):
        pair = lambda ref, k: (ref[k], ref[k + 1])
        zero = jnp.zeros(self.full.shape[1:], jnp.float32)

        def store(c, d):
            for k, plane in enumerate((*c, *d)):
                self.full[k] = plane

        @self.role(0)
        def _():
            for kind in (0, 1, 2, 3, 4):
                self.wait(kind, 0)
            t = self.lifted(self.m_in, slice(0, 4))
            b = self.lifted(self.m_in, slice(4, 8))
            d = self.lifted(self.m_in, slice(8, 12))
            g = self.lifted(self.g_in, slice(0, 4))
            c1 = pair(self.o_own, 0)
            c2 = plus(pair(self.o_in, 0), times(t, c1))
            d1 = plus(pair(self.j_in, 0), times(g, c2))
            store((zero, zero), plus(plus(pair(self.o_in, 2), times(b, c1)), times(d, d1)))

        @self.role(1)
        def _():
            self.wait(1, 1)
            self.wait(4, 1)
            g = self.lifted(self.g_in, slice(0, 4))
            store(
                pair(self.o_in, 0), plus(pair(self.j_in, 0), times(g, pair(self.j_own, 0)))
            )

        @self.role(2)
        def _():
            self.wait(4, 2)
            t = self.lifted(self.m_own, slice(0, 4))
            b = self.lifted(self.m_in, slice(4, 8))
            c2 = pair(self.j_in, 0)
            c3 = plus(pair(self.o_own, 0), times(t, c2))
            store(c2, plus(pair(self.o_in, 2), times(b, c3)))

        @self.role(3)
        def _():
            for kind in (0, 2, 4):
                self.wait(kind, 3)
            t = self.lifted(self.m_in, slice(0, 4))
            store(plus(pair(self.o_in, 0), times(t, pair(self.j_in, 0))), (zero, zero))

        return [self.full[k] for k in range(4)]

    def finish(self):
        for number in range(4):

            @self.role(number)
            def _(number=number):
                for message in self.messages:
                    if message[1] == number:
                        self.copy(message).wait_send()


def solver(exchange, lift, m, g, o, j, full, ss, rs):
    if exchange.count == 4:
        return Pairs(exchange, lift, *m, *g, *o, *j, full, ss, rs)
    return Split(exchange, lift, *m, *o, *g, full)


def corrected(local, response, incoming, lift):
    total = local
    for k in range(4):
        total = total + lift(response[k]) * incoming[k]
    return total


def kernel(
    counts, residual_hbm, flow_hbm, f_zeta_hbm, f_eta_hbm, f_xi_hbm, out,
    residual, flow, f_zeta, f_eta, f_xi, in_sem,
    z_m0, z_m1, z_g0, z_g1, z_o0, z_o1, z_j0, z_j1, z_full, z_ss, z_rs,
    x_m0, x_m1, x_g0, x_g1, x_o0, x_o1, x_j0, x_j1, x_full, x_ss, x_rs,
    e_matrices, e_msend, e_mslots, e_offsets, e_osend, e_oslots, e_result, e_own, e_inner,
    e_ss, e_rs,
    z_response, x_response, e_response, x_factors, e_factors, lines, turned, turned_factors,
    hz, hx_send, hx, he_send, he, padded, source, h_ss, h_rs,
):
    n_xi, n_eta, n_zeta = counts
    fields, cz, cx, cy = flow.shape
    planes = fields * cz
    xz = Exchange("zeta", n_zeta, z_ss, z_rs)
    xe = Exchange("eta", n_eta, e_ss, e_rs)
    xx = Exchange("xi", n_xi, x_ss, x_rs)
    zeta = solver(
        xz, spread, (z_m0, z_m1), (z_g0, z_g1), (z_o0, z_o1), (z_j0, z_j1), z_full, z_ss, z_rs
    )
    xi = solver(
        xx, line_spread, (x_m0, x_m1), (x_g0, x_g1), (x_o0, x_o1), (x_j0, x_j1), x_full, x_ss, x_rs
    )

    barrier = pltpu.get_barrier_semaphore()
    greeted = 0
    for x in (xz, xe, xx):
        for p in x.peers():
            pl.semaphore_signal(barrier, inc=1, device_id={x.axis: p}, device_id_type=MESH)
            greeted += 1

    loads = [
        pltpu.make_async_copy(src, dst, in_sem.at[k])
        for k, (src, dst) in enumerate(
            (
                (flow_hbm, flow),
                (f_zeta_hbm, f_zeta),
                (f_xi_hbm, f_xi),
                (residual_hbm, residual),
                (f_eta_hbm, f_eta),
            )
        )
    ]
    for load in loads:
        load.start()
    zeta.clear_ends()
    xi.clear_ends()
    loads[0].wait()

    per_pack = cy // 4
    lane = lax.broadcasted_iota(jnp.int32, (cx, cy), 1)
    packs = [jnp.zeros((cx, cy), jnp.float32) for _ in range(he_send.shape[0])]
    eta_part = []
    for k in range(planes):
        at = k % per_pack
        v = flow[k // cz, k % cz]
        up1, up2 = pltpu.roll(v, 1, 1), pltpu.roll(v, 2, 1)
        down1, down2 = pltpu.roll(v, cy - 1, 1), pltpu.roll(v, cy - 2, 1)
        near_low, near_high = lane < 1, lane >= cy - 1
        far_low, far_high = lane < 2, lane >= cy - 2
        near = jnp.where(near_low, 0.0, up1) + jnp.where(near_high, 0.0, down1)
        far = jnp.where(far_low, 0.0, up2) + jnp.where(far_high, 0.0, down2)
        eta_part.append(far - 4.0 * near)
        near = jnp.where(near_low, up1, jnp.where(near_high, down1, 0.0))
        far = jnp.where(far_low, up2, jnp.where(far_high, down2, 0.0))
        face = -dissipation * (far - 4.0 * near)
        moved = pltpu.roll(face, (4 * at + 2) % cy, 1)
        packs[k // per_pack] = jnp.where(lane // 4 == at, moved, packs[k // per_pack])
    for k, pack in enumerate(packs):
        he_send[k] = pack
    row = lambda x: flow[:, :, x : x + 1, :]
    hx_send[0, :, :, 0:1, :] = -dissipation * (row(cx - 2) - 4.0 * row(cx - 1))
    hx_send[0, :, :, 1:2, :] = -dissipation * row(cx - 1)
    hx_send[1, :, :, 0:1, :] = -dissipation * row(0)
    hx_send[1, :, :, 1:2, :] = -dissipation * (row(1) - 4.0 * row(0))

    pl.semaphore_wait(barrier, greeted)

    halos = (
        (xx, hx, lambda side: hx_send.at[side]),
        (xe, he, lambda side: he_send),
        (xz, hz, lambda side: flow.at[:, cz - 2 : cz] if side == 0 else flow.at[:, 0:2]),
    )

    def halo_copy(number, side):
        x, slots, origin = halos[number]
        step = 1 if side == 0 else x.count - 1
        return pltpu.make_async_remote_copy(
            src_ref=origin(side),
            dst_ref=slots.at[side],
            send_sem=h_ss.at[number, side],
            recv_sem=h_rs.at[number, side],
            device_id={x.axis: lax.rem(x.me + step, x.count)},
            device_id_type=MESH,
        )

    for number, (x, slots, origin) in enumerate(halos):
        for side in range(2):
            sends = x.me < x.count - 1 if side == 0 else x.me > 0
            has = x.me > 0 if side == 0 else x.me < x.count - 1
            pl.when(sends)(lambda number=number, side=side: halo_copy(number, side).start())

            @pl.when(jnp.logical_not(has))
            def _(slots=slots, side=side):
                slots[side] = jnp.zeros(slots.shape[1:], jnp.float32)

    loads[1].wait()

    def keep_z(s, now):
        z_response[s] = now

    zeta.put_matrices(responses(cz, lambda k, s: f_zeta[:, k, s], keep_z))

    state = flow[...]
    nothing = jnp.zeros((fields, cz, 2, cy), jnp.float32)
    padded[:, :, 8 - 2 : 8, :] = nothing
    padded[:, :, 8 : 8 + cx, :] = state
    padded[:, :, 8 + cx : 8 + cx + 2, :] = nothing
    none = jnp.zeros((fields, 2, cx, cy), jnp.float32)
    long = jnp.concatenate([none, state, none], 1)
    near = (padded[:, :, 7 : 7 + cx, :] + padded[:, :, 9 : 9 + cx, :]) + (
        long[:, 1 : 1 + cz] + long[:, 3 : 3 + cz]
    )
    far = (padded[:, :, 6 : 6 + cx, :] + padded[:, :, 10 : 10 + cx, :]) + (
        long[:, 0:cz] + long[:, 4 : 4 + cz]
    )
    total_part = 18.0 * state - 4.0 * near + far + jnp.stack(eta_part).reshape(flow.shape)
    loads[3].wait()
    source[...] = residual[...] - dissipation * total_part

    loads[2].wait()

    for s in range(cx):
        for k in range(5):
            for g in range(3):
                x_factors[k, s, g] = f_xi[pl.ds((g * 5 + k) * cz * cx + s, cz, stride=cx), :]

    def xi_factor(k, s):
        return x_factors[k, s]

    def keep_x(s, now):
        x_response[s] = now

    xi.put_matrices(responses(cx, xi_factor, keep_x))
    zeta.join_matrices()

    for number, (x, slots, origin) in enumerate(halos):
        for side in range(2):
            has = x.me > 0 if side == 0 else x.me < x.count - 1
            pl.when(has)(lambda number=number, side=side: halo_copy(number, side).wait_recv())

    source[:, :, 0:2, :] += hx[0]
    source[:, :, cx - 2 : cx, :] += hx[1]
    zeta_faces = {
        0: hz[0, :, 0] - 4.0 * hz[0, :, 1],
        1: hz[0, :, 1],
        cz - 2: hz[1, :, 0],
        cz - 1: hz[1, :, 1] - 4.0 * hz[1, :, 0],
    }
    faces = [jnp.where(lane % 4 >= 2, he[0, k], he[1, k]) for k in range(he.shape[1])]
    edge = jnp.logical_or(lane < 2, lane >= cy - 2)

    def eta_face(f, z):
        k = f * cz + z
        back = (cy - (4 * (k % per_pack) + 2)) % cy
        return jnp.where(edge, pltpu.roll(faces[k // per_pack], back, 1), 0.0)

    def source_plane(z):
        value = source[:, z] + jnp.stack([eta_face(f, z) for f in range(fields)])
        if z in zeta_faces:
            value = value - dissipation * zeta_faces[z]
        return value

    z_factor = lambda k, s: spread(f_zeta[:, k, s])
    zero = jnp.zeros((fields, cx, cy), jnp.float32)
    forward = forward_sweep(cz, z_factor, source_plane, zero, zero)
    zeta.put_ahead(jnp.stack([forward[-1], forward[-2]]))
    local = backward_sweep(cz, z_factor, lambda s: forward[s], zero, zero, lambda s, now: None)
    zeta.put_behind(jnp.stack([local[0], local[1]]))
    zeta.solve()

    loads[4].wait()
    tiles = lines.shape[0] // cy
    steps = cy // sublanes
    total = lines.shape[0]
    distinct, uses = line_tiles(cy // (cz * cx))
    for k in range(5):
        for t, groups in enumerate(distinct):
            whole = jnp.concatenate([f_eta[g * 5 + k] for g in groups], 0)
            turned_factors[t * cy : (t + 1) * cy, :] = whole.T
        for s in range(steps):
            e_factors[k, s] = turned_factors[
                pl.ds(s, len(distinct) * sublanes, stride=steps), :
            ].reshape(len(distinct), sublanes, cy)

    def tiled(planes):
        return jnp.concatenate([planes[u : u + 1] for u in uses], 0)

    xi.join_matrices()

    def eta_factor(k, s):
        return e_factors[k, s]

    def keep_e(s, now):
        e_response[s] = now

    e_matrices[...] = responses(steps, eta_factor, keep_e)
    chunk = lambda c: [e_matrices[k, :, c : c + 1, :] for k in range(12)]
    one = jnp.ones((1, len(distinct), 1, cy), jnp.float32)
    zero = jnp.zeros_like(one)
    unit = lambda j: jnp.concatenate([one if i == j else zero for i in range(4)], 0)
    inner, left = chain(sublanes, chunk, lambda c: None, [unit(j) for j in range(4)], False)
    for c, values in enumerate(inner):
        for k in range(4):
            e_inner[k, :, :, c : c + 1, :] = values[k]
    e_msend[...] = jnp.concatenate([left[0][0:2], left[1][0:2], left[2], left[3]], 0)
    e_mslots[xe.me] = e_msend[...]
    xe.start(0, lambda p: e_msend, e_mslots)

    incoming = zeta.result()
    for s in range(cz):
        done = corrected(local[s], z_response[s], incoming, spread)
        for place, f in enumerate(line_order):
            lines[(place * cz + s) * cx : (place * cz + s + 1) * cx, :] = done[f]
    if total > planes * cx:
        lines[planes * cx : total, :] = jnp.zeros((total - planes * cx, cy), jnp.float32)

    for t in range(tiles):
        turned[t * cy : (t + 1) * cy, :] = lines[t * cy : (t + 1) * cy, :].T
    zero = jnp.zeros((tiles, sublanes, cy), jnp.float32)

    eta_tiles = lambda k, s: tiled(e_factors[k, s])

    def at_step(s):
        return pl.ds(s, tiles * sublanes, stride=steps)

    forward = forward_sweep(
        steps, eta_tiles, lambda s: turned[at_step(s), :].reshape(zero.shape), zero, zero
    )
    local = backward_sweep(
        steps, eta_tiles, lambda s: forward[s], zero, zero, lambda s, now: None
    )
    for k, value in enumerate((forward[-1], forward[-2], local[0], local[1])):
        e_offsets[k] = value
    none = jnp.zeros((tiles, 1, cy), jnp.float32)
    inner, left = chain(
        sublanes,
        lambda c: [tiled(plane) for plane in chunk(c)],
        lambda c: [e_offsets[k, :, c : c + 1, :] for k in range(4)],
        (none,) * 4,
        False,
    )
    for k in range(4):
        e_osend[k] = left[k]
    e_oslots[xe.me] = e_osend[...]
    xe.start(1, lambda p: e_osend, e_oslots)
    for c, values in enumerate(inner):
        for k in range(4):
            e_own[k, :, c : c + 1, :] = values[k]
    xe.wait_recv(0, lambda p: e_msend, e_mslots)
    xe.wait_recv(1, lambda p: e_osend, e_oslots)
    solved, _ = chain(
        n_eta,
        lambda q: [tiled(e_mslots[q, k]) for k in range(12)],
        lambda q: [e_oslots[q, k] for k in range(4)],
        (none,) * 4,
        True,
    )
    for q, values in enumerate(solved):
        for k in range(4):
            e_result[q, k] = values[k]
    enters = [e_result[xe.me, k] for k in range(4)]
    incoming = []
    for k in range(4):
        value = e_own[k]
        for j in range(2 if k < 2 else 4):
            value = value + tiled(e_inner[k, j]) * enters[j]
        incoming.append(value)
    for s in range(steps):
        done = corrected(local[s], e_response[s], incoming, tiled)
        turned[at_step(s), :] = done.reshape(tiles * sublanes, cy)
    for t in range(tiles):
        lines[t * cy : (t + 1) * cy, :] = turned[t * cy : (t + 1) * cy, :].T

    x_factor = lambda k, s: line_spread(xi_factor(k, s))
    zero = jnp.zeros((fields, cz, cy), jnp.float32)
    forward = forward_sweep(
        cx,
        x_factor,
        lambda s: lines[pl.ds(s, planes, stride=cx), :].reshape(zero.shape),
        zero,
        zero,
    )
    xi.put_ahead(jnp.stack([forward[-1], forward[-2]]))
    local = backward_sweep(cx, x_factor, lambda s: forward[s], zero, zero, lambda s, now: None)
    xi.put_behind(jnp.stack([local[0], local[1]]))
    xi.solve()
    incoming = xi.result()
    for s in range(cx):
        done = corrected(local[s], x_response[s], incoming, line_spread)
        for place, f in enumerate(line_order):
            out[pl.ds(f * cz * cx + s, cz, stride=cx), :] = done[place]

    zeta.finish()
    xi.finish()
    xe.wait_send(0, lambda p: e_msend, e_mslots)
    xe.wait_send(1, lambda p: e_osend, e_oslots)
    for number, (x, slots, origin) in enumerate(halos):
        for side in range(2):
            sends = x.me < x.count - 1 if side == 0 else x.me > 0
            pl.when(sends)(lambda number=number, side=side: halo_copy(number, side).wait_send())


def solver_scratch(count, fields, lanes):
    vmem = lambda *shape: pltpu.VMEM(shape, jnp.float32)
    if count == 4:
        return [
            vmem(12, 3, sublanes, lanes),
            vmem(12, 3, sublanes, lanes),
            vmem(4, 3, sublanes, lanes),
            vmem(4, 3, sublanes, lanes),
            vmem(4, fields, sublanes, lanes),
            vmem(4, fields, sublanes, lanes),
            vmem(2, fields, sublanes, lanes),
            vmem(2, fields, sublanes, lanes),
            vmem(4, fields, sublanes, lanes),
            pltpu.SemaphoreType.DMA((5, count)),
            pltpu.SemaphoreType.DMA((5,)),
        ]
    parts = count if sublanes % count == 0 else 1
    rows = sublanes // parts
    return [
        vmem(parts, 12, 3, rows, lanes),
        vmem(count, 12, 3, rows, lanes),
        vmem(count, 4, fields, rows, lanes),
        vmem(count, 4, fields, rows, lanes),
        vmem(parts, 4, fields, rows, lanes),
        vmem(count, 4, fields, rows, lanes),
        vmem(sublanes, lanes),
        vmem(sublanes, lanes),
        vmem(4, fields, sublanes, lanes),
        pltpu.SemaphoreType.DMA((5, count)),
        pltpu.SemaphoreType.DMA((5, count)),
    ]


def on_device(counts, residual, flow_state, factors_zeta, factors_eta, factors_xi):
    n_xi, n_eta, n_zeta = counts
    fields, cz, cx, cy = flow_state.shape
    total = -(-(fields * cz * cx) // cy) * cy
    tiles = total // cy
    steps = cy // sublanes
    packs = -(-(fields * cz) // (cy // 4))
    distinct = len(line_tiles(cy // (cz * cx))[0])
    vmem = lambda *shape: pltpu.VMEM(shape, jnp.float32)
    dma = pltpu.SemaphoreType.DMA
    whole = pl.BlockSpec(memory_space=pltpu.VMEM)
    scratch = (
        [
            vmem(fields, cz, cx, cy),
            vmem(fields, cz, cx, cy),
            vmem(3, 5, cz, cx, cy),
            vmem(15, cz * cx, cy),
            vmem(15 * cz * cx, cy),
            dma((5,)),
        ]
        + solver_scratch(n_zeta, fields, cy)
        + solver_scratch(n_xi, fields, cy)
        + [
            vmem(12, distinct, sublanes, cy),
            vmem(12, distinct, 1, cy),
            vmem(n_eta, 12, distinct, 1, cy),
            vmem(4, tiles, sublanes, cy),
            vmem(4, tiles, 1, cy),
            vmem(n_eta, 4, tiles, 1, cy),
            vmem(n_eta, 4, tiles, 1, cy),
            vmem(4, tiles, sublanes, cy),
            vmem(4, 4, distinct, sublanes, cy),
            dma((2, n_eta)),
            dma((2, n_eta)),
            vmem(cz, 4, 3, cx, cy),
            vmem(cx, 4, 3, cz, cy),
            vmem(steps, 4, distinct, sublanes, cy),
            vmem(5, cx, 3, cz, cy),
            vmem(5, steps, distinct, sublanes, cy),
            vmem(total, cy),
            vmem(total, cy),
            vmem(distinct * cy, cy),
            vmem(2, fields, 2, cx, cy),
            vmem(2, fields, cz, 2, cy),
            vmem(2, fields, cz, 2, cy),
            vmem(packs, cx, cy),
            vmem(2, packs, cx, cy),
            vmem(fields, cz, cx + 16, cy),
            vmem(fields, cz, cx, cy),
            dma((3, 2)),
            dma((3, 2)),
        ]
    )
    update = pl.pallas_call(
        functools.partial(kernel, counts),
        out_shape=jax.ShapeDtypeStruct((fields * cz * cx, cy), jnp.float32),
        in_specs=[pl.BlockSpec(memory_space=pltpu.HBM)] * 5,
        out_specs=whole,
        scratch_shapes=scratch,
        compiler_params=pltpu.CompilerParams(
            collective_id=0, has_side_effects=True, vmem_limit_bytes=24 * 2**20
        ),
    )(
        *(
            pltpu.with_memory_space_constraint(operand, pltpu.HBM)
            for operand in (
                residual,
                flow_state,
                factors_zeta,
                factors_eta.reshape(15, cz * cx, cy),
                factors_xi.reshape(15 * cz * cx, cy),
            )
        )
    )
    return update.reshape(flow_state.shape)


def solution(mesh):
    fields = P(None, "zeta", "xi", "eta")
    factors = P(None, None, "zeta", "xi", "eta")
    counts = tuple(mesh.shape[axis] for axis in ("xi", "eta", "zeta"))
    return jax.shard_map(
        functools.partial(on_device, counts),
        mesh=mesh,
        in_specs=(fields, fields, factors, factors, factors),
        out_specs=fields,
        check_vma=False,
    )
```

```python
import functools

import jax
import jax.numpy as jnp
from jax import lax
from jax.experimental import pallas as pl
from jax.experimental.pallas import tpu as pltpu
from jax.sharding import PartitionSpec as P

field_group = (0, 0, 0, 1, 2)
dissipation = 0.05
sublanes = 8
MESH = pl.DeviceIdType.MESH


line_order = (0, 3, 1, 4, 2)


def field_spread(own):
    return lambda planes: jnp.concatenate([planes[field_group[f]][None] for f in own], 0)


def streams_of(per_tile):
    return [own for own in (line_order[:per_tile], line_order[per_tile:]) if own]


def line_tiles(per_tile):
    distinct, uses = [], []
    for start in range(0, len(line_order), per_tile):
        groups = [field_group[f] for f in line_order[start : start + per_tile]]
        for number, have in enumerate(distinct):
            if have[: len(groups)] == groups:
                break
        else:
            number = len(distinct)
            distinct.append(groups + [groups[-1]] * (per_tile - len(groups)))
        uses.append(number)
    return distinct, uses


def forward_sweep(steps, factor, value, recent, before):
    rows = []
    for s in range(steps):
        now = -(factor(1, s) * before) if value is None else value(s) - factor(1, s) * before
        now = now - factor(0, s) * recent
        rows.append(now)
        recent, before = now, recent
    return rows


def backward_sweep(steps, factor, value, recent, before, keep):
    rows = [None] * steps
    for s in reversed(range(steps)):
        now = factor(2, s) * value(s) - factor(4, s) * before - factor(3, s) * recent
        rows[s] = now
        keep(s, now)
        recent, before = now, recent
    return rows


def responses(steps, factor, keep):
    one = jnp.ones_like(factor(0, 0))
    zero = jnp.zeros_like(one)
    lift = lambda k, s: factor(k, s)[None]
    forward = forward_sweep(
        steps, lift, None, jnp.stack([one, zero]), jnp.stack([zero, one])
    )
    none = jnp.zeros((2,) + one.shape, jnp.float32)
    backward = backward_sweep(
        steps,
        lift,
        lambda s: jnp.concatenate([forward[s], none], 0),
        jnp.stack([zero, zero, one, zero]),
        jnp.stack([zero, zero, zero, one]),
        keep,
    )
    return jnp.concatenate([forward[-1], forward[-2], backward[0], backward[1]], 0)


def chain(count, matrices, offsets, into, closed):
    c1, c2, d1, d2 = into
    entered = []
    for q in range(count):
        entered.append((c1, c2))
        if q < count - 1 or not closed:
            m, o = matrices(q), offsets(q)
            n1, n2 = m[0] * c1 + m[1] * c2, m[2] * c1 + m[3] * c2
            c1, c2 = (n1, n2) if o is None else (o[0] + n1, o[1] + n2)
    out = (c1, c2)
    result = [None] * count
    for q in reversed(range(count)):
        c1, c2 = entered[q]
        result[q] = (c1, c2, d1, d2)
        if q > 0 or not closed:
            m, o = matrices(q), offsets(q)
            n1, n2 = m[4] * c1 + m[5] * c2, m[8] * c1 + m[9] * c2
            if o is not None:
                n1, n2 = o[2] + n1, o[3] + n2
            d1, d2 = n1 + (m[6] * d1 + m[7] * d2), n2 + (m[10] * d1 + m[11] * d2)
    return result, out + (d1, d2)


class Exchange:
    def __init__(self, axis, count, send_sem, recv_sem):
        self.axis, self.count = axis, count
        self.send_sem, self.recv_sem = send_sem, recv_sem
        self.me = lax.axis_index(axis)

    def peers(self):
        return [lax.rem(self.me + k, self.count) for k in range(1, self.count)]

    def copy(self, kind, source, slots, p, slot, cut):
        pick = (lambda ref: ref) if cut is None else (lambda ref: ref.at[cut[0] : cut[1]])
        return pltpu.make_async_remote_copy(
            src_ref=pick(source(p)),
            dst_ref=pick(slots.at[slot]),
            send_sem=self.send_sem.at[kind, p],
            recv_sem=self.recv_sem.at[kind, slot],
            device_id={self.axis: p},
            device_id_type=MESH,
        )

    def start(self, kind, source, slots, cut=None, sends=None):
        for p in self.peers():
            go = lambda p=p: self.copy(kind, source, slots, p, self.me, cut).start()
            go() if sends is None else pl.when(sends(self.me, p))(go)

    def wait_recv(self, kind, source, slots, cut=None, sends=None):
        for p in self.peers():
            go = lambda p=p: self.copy(kind, source, slots, p, p, cut).wait_recv()
            go() if sends is None else pl.when(sends(p, self.me))(go)

    def wait_send(self, kind, source, slots, cut=None, sends=None):
        for p in self.peers():
            go = lambda p=p: self.copy(kind, source, slots, p, self.me, cut).wait_send()
            go() if sends is None else pl.when(sends(self.me, p))(go)


class Split:
    def __init__(self, exchange, lift, m_send, m_slots, o_send, o_slots, r_send, r_slots, full):
        self.x, self.lift = exchange, lift
        self.m_send, self.m_slots = m_send, m_slots
        self.o_send, self.o_slots = o_send, o_slots
        self.r_send, self.r_slots, self.full = r_send, r_slots, full
        self.parts = m_send.shape[0]
        self.rows = sublanes // self.parts
        pick = (lambda p: p) if self.parts > 1 else (lambda p: 0)
        last = exchange.count - 1
        m_from = lambda p: m_send.at[pick(p)]
        o_from = lambda p: o_send.at[pick(p)]
        r_from = lambda p: r_send.at[p]
        self.matrices = (0, m_from, m_slots)
        self.ahead = (1, o_from, o_slots, (0, 2), lambda a, b: a < last)
        self.behind = (2, o_from, o_slots, (2, 4), lambda a, b: a > 0)
        self.carried = (3, r_from, r_slots, (0, 2), lambda a, b: b > 0)
        self.returned = (4, r_from, r_slots, (2, 4), lambda a, b: b < last)
        self.pick = pick

    def clear_ends(self):
        if self.parts > 1:
            nothing = jnp.zeros((self.parts, 2) + self.r_slots.shape[2:], jnp.float32)

            @pl.when(self.x.me == 0)
            def _():
                self.r_slots[:, 0:2] = nothing

            @pl.when(self.x.me == self.x.count - 1)
            def _():
                self.r_slots[:, 2:4] = nothing

    def put(self, route, value, send, slots, lo):
        hi = lo + value.shape[0]
        for p in range(self.parts):
            send[p, lo:hi] = value[:, :, p * self.rows : (p + 1) * self.rows, :]
        slots[self.x.me, lo:hi] = send[self.pick(self.x.me), lo:hi]
        self.x.start(*route)

    def put_matrices(self, value):
        self.put(self.matrices, value, self.m_send, self.m_slots, 0)

    def put_ahead(self, value):
        self.put(self.ahead, value, self.o_send, self.o_slots, 0)

    def put_behind(self, value):
        self.put(self.behind, value, self.o_send, self.o_slots, 2)

    def solve(self):
        x = self.x
        for route in (self.matrices, self.ahead, self.behind):
            x.wait_recv(*route)
        zero = jnp.zeros(self.o_slots.shape[2:], jnp.float32)
        solved, _ = chain(
            x.count,
            lambda q: [self.lift(self.m_slots[q, k]) for k in range(12)],
            lambda q: [self.o_slots[q, k] for k in range(4)],
            (zero,) * 4,
            True,
        )
        for q, planes in enumerate(solved):
            for k in range(4):
                self.r_send[q, k] = planes[k]
        if self.parts > 1:
            x.start(*self.carried)
            x.start(*self.returned)
            me = x.me

            @pl.when(me > 0)
            def _():
                self.r_slots[me, 0:2] = self.r_send[me, 0:2]

            @pl.when(me < x.count - 1)
            def _():
                self.r_slots[me, 2:4] = self.r_send[me, 2:4]

    def result(self):
        x = self.x
        if self.parts == 1:
            return [self.r_send[x.me, k] for k in range(4)]
        x.wait_recv(*self.carried)
        x.wait_recv(*self.returned)
        for p in range(self.parts):
            self.full[:, :, p * self.rows : (p + 1) * self.rows, :] = self.r_slots[p]
        return [self.full[k] for k in range(4)]

    def finish(self):
        for route in (self.matrices, self.ahead, self.behind):
            self.x.wait_send(*route)
        if self.parts > 1:
            self.x.wait_send(*self.carried)
            self.x.wait_send(*self.returned)


def times(m, v):
    return m[0] * v[0] + m[1] * v[1], m[2] * v[0] + m[3] * v[1]


def plus(a, b):
    return a[0] + b[0], a[1] + b[1]


class Pairs:
    def __init__(self, exchange, lifts, m_own, m_in, g_own, g_in, streams, ss, rs):
        self.axis, self.me, self.lifts = exchange.axis, exchange.me, lifts
        self.m_own, self.m_in, self.g_own, self.g_in = m_own, m_in, g_own, g_in
        self.streams = streams
        ahead, behind, top, mid = (slice(0, 2), slice(2, 4), slice(0, 4), slice(4, 8))
        cut = lambda a, b, part: (a.at[part], b.at[part])
        self.messages = [
            (0, 1, 0, m_own, m_in),
            (0, 3, 2, *cut(m_own, m_in, mid)),
            (0, 2, 3, *cut(m_own, m_in, top)),
            (1, 2, 1, g_own, g_in),
            (1, 2, 0, g_own, g_in),
        ]
        for h, (o_own, o_in, j_own, j_in, _) in enumerate(streams):
            kind = 2 + 3 * h
            self.messages += [
                (kind, 0, 1, *cut(o_own, o_in, ahead)),
                (kind, 1, 0, *cut(o_own, o_in, ahead)),
                (kind, 2, 3, *cut(o_own, o_in, ahead)),
                (kind + 1, 1, 0, *cut(o_own, o_in, behind)),
                (kind + 1, 3, 2, *cut(o_own, o_in, behind)),
                (kind + 2, 1, 2, j_own, j_in),
                (kind + 2, 1, 3, j_own, j_in),
                (kind + 2, 2, 1, j_own, j_in),
                (kind + 2, 2, 0, j_own, j_in),
            ]
        self.ss, self.rs = ss, rs

    def copy(self, message):
        kind, _, to, source, destination = message
        return pltpu.make_async_remote_copy(
            src_ref=source,
            dst_ref=destination,
            send_sem=self.ss.at[kind, to],
            recv_sem=self.rs.at[kind],
            device_id={self.axis: to},
            device_id_type=MESH,
        )

    def role(self, number):
        return pl.when(self.me == number)

    def start(self, kind, number):
        for message in self.messages:
            if message[0] == kind and message[1] == number:
                self.copy(message).start()

    def start_all(self, kind):
        for number in range(4):
            if any(m[0] == kind and m[1] == number for m in self.messages):
                self.role(number)(lambda number=number: self.start(kind, number))

    def wait(self, kind, number):
        for message in self.messages:
            if message[0] == kind and message[2] == number:
                self.copy(message).wait_recv()

    def clear_ends(self):
        pass

    def put_matrices(self, value):
        for place, k in enumerate((0, 1, 2, 3, 4, 5, 8, 9, 6, 7, 10, 11)):
            self.m_own[place] = value[k]
        self.start_all(0)

    def join_matrices(self):
        @self.role(2)
        def _():
            self.wait(0, 2)
            own = [self.m_own[k] for k in range(12)]
            far = [self.m_in[4 + k] for k in range(4)]
            columns = []
            for j in range(2):
                through = times(far, (own[j], own[2 + j]))
                columns.append(plus((own[4 + j], own[6 + j]), times(own[8:12], through)))
            for i in range(2):
                for j in range(2):
                    self.g_own[2 * i + j] = columns[j][i]
            self.start(1, 2)

    def put_ahead(self, h, value):
        self.streams[h][0][0:2] = value
        self.start_all(2 + 3 * h)

    def put_behind(self, h, value):
        self.streams[h][0][2:4] = value
        self.start_all(3 + 3 * h)

    def solve(self, h):
        o_own, o_in, j_own, j_in, full = self.streams[h]
        kind = 2 + 3 * h
        lifted = lambda ref, lo: [self.lifts[h](ref[k]) for k in range(lo, lo + 4)]

        @self.role(1)
        def _():
            self.wait(kind, 1)
            c = plus((o_own[0], o_own[1]), times(lifted(self.m_own, 0), (o_in[0], o_in[1])))
            j_own[0], j_own[1] = c
            self.start(kind + 2, 1)

        @self.role(2)
        def _():
            self.wait(kind + 1, 2)
            far = plus((o_in[2], o_in[3]), times(lifted(self.m_in, 4), (o_own[0], o_own[1])))
            g = plus((o_own[2], o_own[3]), times(lifted(self.m_own, 8), far))
            j_own[0], j_own[1] = g
            self.start(kind + 2, 2)

    def result(self, h):
        o_own, o_in, j_own, j_in, full = self.streams[h]
        kind = 2 + 3 * h
        lifted = lambda ref, lo: [self.lifts[h](ref[k]) for k in range(lo, lo + 4)]
        pair = lambda ref, k: (ref[k], ref[k + 1])
        zero = jnp.zeros(full.shape[1:], jnp.float32)

        def store(c, d):
            for k, plane in enumerate((*c, *d)):
                full[k] = plane

        def wait(number, once, kinds):
            for k in (once if h == 0 else ()) + kinds:
                self.wait(k, number)

        @self.role(0)
        def _():
            wait(0, (0, 1), (kind, kind + 1, kind + 2))
            c1 = pair(o_own, 0)
            c2 = plus(pair(o_in, 0), times(lifted(self.m_in, 0), c1))
            d1 = plus(pair(j_in, 0), times(lifted(self.g_in, 0), c2))
            d0 = plus(pair(o_in, 2), times(lifted(self.m_in, 4), c1))
            store((zero, zero), plus(d0, times(lifted(self.m_in, 8), d1)))

        @self.role(1)
        def _():
            wait(1, (1,), (kind + 2,))
            store(
                pair(o_in, 0), plus(pair(j_in, 0), times(lifted(self.g_in, 0), pair(j_own, 0)))
            )

        @self.role(2)
        def _():
            wait(2, (), (kind + 2,))
            c2 = pair(j_in, 0)
            c3 = plus(pair(o_own, 0), times(lifted(self.m_own, 0), c2))
            store(c2, plus(pair(o_in, 2), times(lifted(self.m_in, 4), c3)))

        @self.role(3)
        def _():
            wait(3, (0,), (kind, kind + 2))
            c3 = plus(pair(o_in, 0), times(lifted(self.m_in, 0), pair(j_in, 0)))
            store(c3, (zero, zero))

        return [full[k] for k in range(4)]

    def finish(self):
        for number in range(4):

            @self.role(number)
            def _(number=number):
                for message in self.messages:
                    if message[1] == number:
                        self.copy(message).wait_send()


class Splits:
    def __init__(self, exchange, lifts, scratch):
        self.each = []
        for lift, (*buffers, ss, rs) in zip(lifts, scratch):
            own = Exchange(exchange.axis, exchange.count, ss, rs)
            self.each.append(Split(own, lift, *buffers))

    def clear_ends(self):
        for one in self.each:
            one.clear_ends()

    def put_matrices(self, value):
        for one in self.each:
            one.put_matrices(value)

    def join_matrices(self):
        pass

    def put_ahead(self, h, value):
        self.each[h].put_ahead(value)

    def put_behind(self, h, value):
        self.each[h].put_behind(value)

    def solve(self, h):
        self.each[h].solve()

    def result(self, h):
        return self.each[h].result()

    def finish(self):
        for one in self.each:
            one.finish()


def solver(exchange, lifts, scratch):
    if exchange.count == 4:
        return Pairs(exchange, lifts, *scratch)
    return Splits(exchange, lifts, scratch)


def corrected(local, response, incoming, lift):
    total = local
    for k in range(4):
        total = total + lift(response[k]) * incoming[k]
    return total


def kernel(
    counts, residual_hbm, flow_hbm, f_zeta_hbm, f_eta_hbm, f_xi_hbm, out,
    residual, flow, f_zeta, f_eta, f_xi, in_sem,
    z_scratch, x_scratch, e_streams, e_matrices, e_msend, e_mslots, e_inner, e_ss, e_rs,
    z_response, x_response, e_response, x_factors, e_factors, lines, turned, turned_factors,
    hz, hx_send, hx, he_send, he, padded, source, h_ss, h_rs,
):
    n_xi, n_eta, n_zeta = counts
    fields, cz, cx, cy = flow.shape
    planes = fields * cz
    xz = Exchange("zeta", n_zeta, None, None)
    xe = Exchange("eta", n_eta, e_ss, e_rs)
    xx = Exchange("xi", n_xi, None, None)
    per_tile = cy // (cz * cx)
    streams = streams_of(per_tile)
    lifts = [field_spread(own) for own in streams]
    zeta = solver(xz, lifts, z_scratch)
    xi = solver(xx, lifts, x_scratch)

    barrier = pltpu.get_barrier_semaphore()
    greeted = 0
    for x in (xz, xe, xx):
        for p in x.peers():
            pl.semaphore_signal(barrier, inc=1, device_id={x.axis: p}, device_id_type=MESH)
            greeted += 1

    loads = [
        pltpu.make_async_copy(src, dst, in_sem.at[k])
        for k, (src, dst) in enumerate(
            (
                (flow_hbm, flow),
                (f_zeta_hbm, f_zeta),
                (f_xi_hbm, f_xi),
                (residual_hbm, residual),
                (f_eta_hbm, f_eta),
            )
        )
    ]
    for load in loads:
        load.start()
    zeta.clear_ends()
    xi.clear_ends()
    loads[0].wait()

    per_pack = cy // 4
    lane = lax.broadcasted_iota(jnp.int32, (cx, cy), 1)
    packs = [jnp.zeros((cx, cy), jnp.float32) for _ in range(he_send.shape[0])]
    eta_part = []
    for k in range(planes):
        at = k % per_pack
        v = flow[k // cz, k % cz]
        up1, up2 = pltpu.roll(v, 1, 1), pltpu.roll(v, 2, 1)
        down1, down2 = pltpu.roll(v, cy - 1, 1), pltpu.roll(v, cy - 2, 1)
        near_low, near_high = lane < 1, lane >= cy - 1
        far_low, far_high = lane < 2, lane >= cy - 2
        near = jnp.where(near_low, 0.0, up1) + jnp.where(near_high, 0.0, down1)
        far = jnp.where(far_low, 0.0, up2) + jnp.where(far_high, 0.0, down2)
        eta_part.append(far - 4.0 * near)
        near = jnp.where(near_low, up1, jnp.where(near_high, down1, 0.0))
        far = jnp.where(far_low, up2, jnp.where(far_high, down2, 0.0))
        face = -dissipation * (far - 4.0 * near)
        moved = pltpu.roll(face, (4 * at + 2) % cy, 1)
        packs[k // per_pack] = jnp.where(lane // 4 == at, moved, packs[k // per_pack])
    for k, pack in enumerate(packs):
        he_send[k] = pack
    row = lambda x: flow[:, :, x : x + 1, :]
    hx_send[0, :, :, 0:1, :] = -dissipation * (row(cx - 2) - 4.0 * row(cx - 1))
    hx_send[0, :, :, 1:2, :] = -dissipation * row(cx - 1)
    hx_send[1, :, :, 0:1, :] = -dissipation * row(0)
    hx_send[1, :, :, 1:2, :] = -dissipation * (row(1) - 4.0 * row(0))

    pl.semaphore_wait(barrier, greeted)

    halos = (
        (xx, hx, lambda side: hx_send.at[side]),
        (xe, he, lambda side: he_send),
        (xz, hz, lambda side: flow.at[:, cz - 2 : cz] if side == 0 else flow.at[:, 0:2]),
    )

    def halo_copy(number, side):
        x, slots, origin = halos[number]
        step = 1 if side == 0 else x.count - 1
        return pltpu.make_async_remote_copy(
            src_ref=origin(side),
            dst_ref=slots.at[side],
            send_sem=h_ss.at[number, side],
            recv_sem=h_rs.at[number, side],
            device_id={x.axis: lax.rem(x.me + step, x.count)},
            device_id_type=MESH,
        )

    for number, (x, slots, origin) in enumerate(halos):
        for side in range(2):
            sends = x.me < x.count - 1 if side == 0 else x.me > 0
            has = x.me > 0 if side == 0 else x.me < x.count - 1
            pl.when(sends)(lambda number=number, side=side: halo_copy(number, side).start())

            @pl.when(jnp.logical_not(has))
            def _(slots=slots, side=side):
                slots[side] = jnp.zeros(slots.shape[1:], jnp.float32)

    loads[1].wait()

    def keep_z(s, now):
        z_response[s] = now

    zeta.put_matrices(responses(cz, lambda k, s: f_zeta[:, k, s], keep_z))

    state = flow[...]
    nothing = jnp.zeros((fields, cz, 2, cy), jnp.float32)
    padded[:, :, 8 - 2 : 8, :] = nothing
    padded[:, :, 8 : 8 + cx, :] = state
    padded[:, :, 8 + cx : 8 + cx + 2, :] = nothing
    none = jnp.zeros((fields, 2, cx, cy), jnp.float32)
    long = jnp.concatenate([none, state, none], 1)
    near = (padded[:, :, 7 : 7 + cx, :] + padded[:, :, 9 : 9 + cx, :]) + (
        long[:, 1 : 1 + cz] + long[:, 3 : 3 + cz]
    )
    far = (padded[:, :, 6 : 6 + cx, :] + padded[:, :, 10 : 10 + cx, :]) + (
        long[:, 0:cz] + long[:, 4 : 4 + cz]
    )
    total_part = 18.0 * state - 4.0 * near + far + jnp.stack(eta_part).reshape(flow.shape)
    loads[3].wait()
    source[...] = residual[...] - dissipation * total_part

    loads[2].wait()

    for s in range(cx):
        for k in range(5):
            for g in range(3):
                x_factors[k, s, g] = f_xi[pl.ds((g * 5 + k) * cz * cx + s, cz, stride=cx), :]

    def xi_factor(k, s):
        return x_factors[k, s]

    def keep_x(s, now):
        x_response[s] = now

    xi.put_matrices(responses(cx, xi_factor, keep_x))
    zeta.join_matrices()

    for number, (x, slots, origin) in enumerate(halos):
        for side in range(2):
            has = x.me > 0 if side == 0 else x.me < x.count - 1
            pl.when(has)(lambda number=number, side=side: halo_copy(number, side).wait_recv())

    source[:, :, 0:2, :] += hx[0]
    source[:, :, cx - 2 : cx, :] += hx[1]
    zeta_faces = {
        0: hz[0, :, 0] - 4.0 * hz[0, :, 1],
        1: hz[0, :, 1],
        cz - 2: hz[1, :, 0],
        cz - 1: hz[1, :, 1] - 4.0 * hz[1, :, 0],
    }
    faces = [jnp.where(lane % 4 >= 2, he[0, k], he[1, k]) for k in range(he.shape[1])]
    edge = jnp.logical_or(lane < 2, lane >= cy - 2)

    def eta_face(f, z):
        k = f * cz + z
        back = (cy - (4 * (k % per_pack) + 2)) % cy
        return jnp.where(edge, pltpu.roll(faces[k // per_pack], back, 1), 0.0)

    def source_plane(own, z):
        value = jnp.stack([source[f, z] + eta_face(f, z) for f in own])
        if z in zeta_faces:
            value = value - dissipation * jnp.stack([zeta_faces[z][f] for f in own])
        return value

    z_local = []
    for h, own in enumerate(streams):
        z_factor = lambda k, s: lifts[h](f_zeta[:, k, s])
        zero = jnp.zeros((len(own), cx, cy), jnp.float32)
        forward = forward_sweep(cz, z_factor, lambda s: source_plane(own, s), zero, zero)
        zeta.put_ahead(h, jnp.stack([forward[-1], forward[-2]]))
        local = backward_sweep(
            cz, z_factor, lambda s: forward[s], zero, zero, lambda s, now: None
        )
        zeta.put_behind(h, jnp.stack([local[0], local[1]]))
        z_local.append(local)
    for h in range(len(streams)):
        zeta.solve(h)

    loads[4].wait()
    tiles = lines.shape[0] // cy
    steps = cy // sublanes
    total = lines.shape[0]
    distinct, uses = line_tiles(cy // (cz * cx))
    for k in range(5):
        for t, groups in enumerate(distinct):
            whole = jnp.concatenate([f_eta[g * 5 + k] for g in groups], 0)
            turned_factors[t * cy : (t + 1) * cy, :] = whole.T
        for s in range(steps):
            e_factors[k, s] = turned_factors[
                pl.ds(s, len(distinct) * sublanes, stride=steps), :
            ].reshape(len(distinct), sublanes, cy)

    def tiled(planes, at=slice(None)):
        return jnp.concatenate([planes[u : u + 1] for u in uses[at]], 0)

    xi.join_matrices()

    def eta_factor(k, s):
        return e_factors[k, s]

    def keep_e(s, now):
        e_response[s] = now

    e_matrices[...] = responses(steps, eta_factor, keep_e)
    chunk = lambda c: [e_matrices[k, :, c : c + 1, :] for k in range(12)]
    one = jnp.ones((1, len(distinct), 1, cy), jnp.float32)
    zero = jnp.zeros_like(one)
    unit = lambda j: jnp.concatenate([one if i == j else zero for i in range(4)], 0)
    inner, left = chain(sublanes, chunk, lambda c: None, [unit(j) for j in range(4)], False)
    for c, values in enumerate(inner):
        for k in range(4):
            e_inner[k, :, :, c : c + 1, :] = values[k]
    e_msend[...] = jnp.concatenate([left[0][0:2], left[1][0:2], left[2], left[3]], 0)
    e_mslots[xe.me] = e_msend[...]
    xe.start(0, lambda p: e_msend, e_mslots)

    if total > planes * cx:
        lines[planes * cx : total, :] = jnp.zeros((total - planes * cx, cy), jnp.float32)

    def turn(source_ref, target_ref, at):
        for t in range(at.start, at.stop):
            target_ref[t * cy : (t + 1) * cy, :] = source_ref[t * cy : (t + 1) * cy, :].T

    first, parts = 0, []
    for own in streams:
        count = -(-len(own) // per_tile)
        parts.append((first, slice(first // per_tile, first // per_tile + count)))
        first += len(own)
    e_local = []
    for h, own in enumerate(streams):
        place, at = parts[h]
        count = at.stop - at.start
        incoming = zeta.result(h)
        for s in range(cz):
            done = corrected(z_local[h][s], z_response[s], incoming, lifts[h])
            for k in range(len(own)):
                row = ((place + k) * cz + s) * cx
                lines[row : row + cx, :] = done[k]
        turn(lines, turned, at)
        offsets, o_send, o_slots, results, inside = e_streams[h]
        rows = lambda s: pl.ds(at.start * cy + s, count * sublanes, stride=steps)
        zero = jnp.zeros((count, sublanes, cy), jnp.float32)
        eta_tiles = lambda k, s: tiled(e_factors[k, s], at)
        forward = forward_sweep(
            steps, eta_tiles, lambda s: turned[rows(s), :].reshape(zero.shape), zero, zero
        )
        local = backward_sweep(
            steps, eta_tiles, lambda s: forward[s], zero, zero, lambda s, now: None
        )
        e_local.append(local)
        for k, value in enumerate((forward[-1], forward[-2], local[0], local[1])):
            offsets[k] = value
        none = jnp.zeros((count, 1, cy), jnp.float32)
        inner, left = chain(
            sublanes,
            lambda c: [tiled(plane, at) for plane in chunk(c)],
            lambda c: [offsets[k, :, c : c + 1, :] for k in range(4)],
            (none,) * 4,
            False,
        )
        for k in range(4):
            o_send[k] = left[k]
        o_slots[xe.me] = o_send[...]
        xe.start(1 + h, lambda p: o_send, o_slots)
        for c, values in enumerate(inner):
            for k in range(4):
                inside[k, :, c : c + 1, :] = values[k]

    x_local = []
    for h, own in enumerate(streams):
        place, at = parts[h]
        count = at.stop - at.start
        offsets, o_send, o_slots, results, inside = e_streams[h]
        if h == 0:
            xe.wait_recv(0, lambda p: e_msend, e_mslots)
        xe.wait_recv(1 + h, lambda p: o_send, o_slots)
        none = jnp.zeros((count, 1, cy), jnp.float32)
        solved, _ = chain(
            n_eta,
            lambda q: [tiled(e_mslots[q, k], at) for k in range(12)],
            lambda q: [o_slots[q, k] for k in range(4)],
            (none,) * 4,
            True,
        )
        for q, values in enumerate(solved):
            for k in range(4):
                results[q, k] = values[k]
        enters = [results[xe.me, k] for k in range(4)]
        incoming = []
        for k in range(4):
            value = inside[k]
            for j in range(2 if k < 2 else 4):
                value = value + tiled(e_inner[k, j], at) * enters[j]
            incoming.append(value)
        rows = lambda s: pl.ds(at.start * cy + s, count * sublanes, stride=steps)
        for s in range(steps):
            done = corrected(e_local[h][s], e_response[s], incoming, lambda r: tiled(r, at))
            turned[rows(s), :] = done.reshape(count * sublanes, cy)
        turn(turned, lines, at)
        x_factor = lambda k, s: lifts[h](xi_factor(k, s))
        zero = jnp.zeros((len(own), cz, cy), jnp.float32)
        columns = lambda s: pl.ds(place * cz * cx + s, len(own) * cz, stride=cx)
        forward = forward_sweep(
            cx, x_factor, lambda s: lines[columns(s), :].reshape(zero.shape), zero, zero
        )
        xi.put_ahead(h, jnp.stack([forward[-1], forward[-2]]))
        local = backward_sweep(
            cx, x_factor, lambda s: forward[s], zero, zero, lambda s, now: None
        )
        xi.put_behind(h, jnp.stack([local[0], local[1]]))
        x_local.append(local)
    for h in range(len(streams)):
        xi.solve(h)
    for h, own in enumerate(streams):
        incoming = xi.result(h)
        for s in range(cx):
            done = corrected(x_local[h][s], x_response[s], incoming, lifts[h])
            for k, f in enumerate(own):
                out[pl.ds(f * cz * cx + s, cz, stride=cx), :] = done[k]

    zeta.finish()
    xi.finish()
    xe.wait_send(0, lambda p: e_msend, e_mslots)
    for h, (_, o_send, o_slots, _, _) in enumerate(e_streams):
        xe.wait_send(1 + h, lambda p: o_send, o_slots)
    for number, (x, slots, origin) in enumerate(halos):
        for side in range(2):
            sends = x.me < x.count - 1 if side == 0 else x.me > 0
            pl.when(sends)(lambda number=number, side=side: halo_copy(number, side).wait_send())


def solver_scratch(count, streams, lanes):
    vmem = lambda *shape: pltpu.VMEM(shape, jnp.float32)
    dma = pltpu.SemaphoreType.DMA
    if count == 4:
        plane = (sublanes, lanes)
        return (
            vmem(12, 3, *plane),
            vmem(12, 3, *plane),
            vmem(4, 3, *plane),
            vmem(4, 3, *plane),
            tuple(
                tuple(vmem(n, len(own), *plane) for n in (4, 4, 2, 2, 4)) for own in streams
            ),
            dma((2 + 3 * len(streams), count)),
            dma((2 + 3 * len(streams),)),
        )
    parts = count if sublanes % count == 0 else 1
    rows = sublanes // parts
    return tuple(
        (
            vmem(parts, 12, 3, rows, lanes),
            vmem(count, 12, 3, rows, lanes),
            vmem(parts, 4, len(own), rows, lanes),
            vmem(count, 4, len(own), rows, lanes),
            vmem(count, 4, len(own), rows, lanes),
            vmem(count, 4, len(own), rows, lanes),
            vmem(4, len(own), sublanes, lanes),
            dma((5, count)),
            dma((5, count)),
        )
        for own in streams
    )


def on_device(counts, residual, flow_state, factors_zeta, factors_eta, factors_xi):
    n_xi, n_eta, n_zeta = counts
    fields, cz, cx, cy = flow_state.shape
    total = -(-(fields * cz * cx) // cy) * cy
    tiles = total // cy
    steps = cy // sublanes
    packs = -(-(fields * cz) // (cy // 4))
    distinct = len(line_tiles(cy // (cz * cx))[0])
    vmem = lambda *shape: pltpu.VMEM(shape, jnp.float32)
    dma = pltpu.SemaphoreType.DMA
    whole = pl.BlockSpec(memory_space=pltpu.VMEM)
    per_tile = cy // (cz * cx)
    streams = streams_of(per_tile)
    eta_streams = []
    for own in streams:
        count = -(-len(own) // per_tile)
        eta_streams.append(
            (
                vmem(4, count, sublanes, cy),
                vmem(4, count, 1, cy),
                vmem(n_eta, 4, count, 1, cy),
                vmem(n_eta, 4, count, 1, cy),
                vmem(4, count, sublanes, cy),
            )
        )
    scratch = (
        [
            vmem(fields, cz, cx, cy),
            vmem(fields, cz, cx, cy),
            vmem(3, 5, cz, cx, cy),
            vmem(15, cz * cx, cy),
            vmem(15 * cz * cx, cy),
            dma((5,)),
            solver_scratch(n_zeta, streams, cy),
            solver_scratch(n_xi, streams, cy),
            tuple(eta_streams),
            vmem(12, distinct, sublanes, cy),
            vmem(12, distinct, 1, cy),
            vmem(n_eta, 12, distinct, 1, cy),
            vmem(4, 4, distinct, sublanes, cy),
            dma((1 + len(streams), n_eta)),
            dma((1 + len(streams), n_eta)),
            vmem(cz, 4, 3, cx, cy),
            vmem(cx, 4, 3, cz, cy),
            vmem(steps, 4, distinct, sublanes, cy),
            vmem(5, cx, 3, cz, cy),
            vmem(5, steps, distinct, sublanes, cy),
            vmem(total, cy),
            vmem(total, cy),
            vmem(distinct * cy, cy),
            vmem(2, fields, 2, cx, cy),
            vmem(2, fields, cz, 2, cy),
            vmem(2, fields, cz, 2, cy),
            vmem(packs, cx, cy),
            vmem(2, packs, cx, cy),
            vmem(fields, cz, cx + 16, cy),
            vmem(fields, cz, cx, cy),
            dma((3, 2)),
            dma((3, 2)),
        ]
    )
    update = pl.pallas_call(
        functools.partial(kernel, counts),
        out_shape=jax.ShapeDtypeStruct((fields * cz * cx, cy), jnp.float32),
        in_specs=[pl.BlockSpec(memory_space=pltpu.HBM)] * 5,
        out_specs=whole,
        scratch_shapes=scratch,
        compiler_params=pltpu.CompilerParams(
            collective_id=0, has_side_effects=True, vmem_limit_bytes=24 * 2**20
        ),
    )(
        *(
            pltpu.with_memory_space_constraint(operand, pltpu.HBM)
            for operand in (
                residual,
                flow_state,
                factors_zeta,
                factors_eta.reshape(15, cz * cx, cy),
                factors_xi.reshape(15 * cz * cx, cy),
            )
        )
    )
    return update.reshape(flow_state.shape)


def solution(mesh):
    fields = P(None, "zeta", "xi", "eta")
    factors = P(None, None, "zeta", "xi", "eta")
    counts = tuple(mesh.shape[axis] for axis in ("xi", "eta", "zeta"))
    return jax.shard_map(
        functools.partial(on_device, counts),
        mesh=mesh,
        in_specs=(fields, fields, factors, factors, factors),
        out_specs=fields,
        check_vma=False,
    )
```

```python
import functools

import jax
import jax.numpy as jnp
from jax import lax
from jax.experimental import pallas as pl
from jax.experimental.pallas import tpu as pltpu
from jax.sharding import PartitionSpec as P

field_group = (0, 0, 0, 1, 2)
dissipation = 0.05
sublanes = 8
MESH = pl.DeviceIdType.MESH


line_order = (0, 3, 1, 4, 2)


def field_spread(own):
    return lambda planes: jnp.concatenate([planes[field_group[f]][None] for f in own], 0)


def streams_of(per_tile):
    return [own for own in (line_order[:per_tile], line_order[per_tile:]) if own]


def line_tiles(per_tile):
    distinct, uses = [], []
    for start in range(0, len(line_order), per_tile):
        groups = [field_group[f] for f in line_order[start : start + per_tile]]
        for number, have in enumerate(distinct):
            if have[: len(groups)] == groups:
                break
        else:
            number = len(distinct)
            distinct.append(groups + [groups[-1]] * (per_tile - len(groups)))
        uses.append(number)
    return distinct, uses


def forward_sweep(steps, factor, value, recent, before):
    rows = []
    for s in range(steps):
        now = -(factor(1, s) * before) if value is None else value(s) - factor(1, s) * before
        now = now - factor(0, s) * recent
        rows.append(now)
        recent, before = now, recent
    return rows


def backward_sweep(steps, factor, value, recent, before, keep):
    rows = [None] * steps
    for s in reversed(range(steps)):
        now = factor(2, s) * value(s) - factor(4, s) * before - factor(3, s) * recent
        rows[s] = now
        keep(s, now)
        recent, before = now, recent
    return rows


def responses(steps, factor, keep):
    one = jnp.ones_like(factor(0, 0))
    zero = jnp.zeros_like(one)
    lift = lambda k, s: factor(k, s)[None]
    forward = forward_sweep(
        steps, lift, None, jnp.stack([one, zero]), jnp.stack([zero, one])
    )
    none = jnp.zeros((2,) + one.shape, jnp.float32)
    backward = backward_sweep(
        steps,
        lift,
        lambda s: jnp.concatenate([forward[s], none], 0),
        jnp.stack([zero, zero, one, zero]),
        jnp.stack([zero, zero, zero, one]),
        keep,
    )
    return jnp.concatenate([forward[-1], forward[-2], backward[0], backward[1]], 0)


def chain(count, matrices, offsets, into, closed):
    c1, c2, d1, d2 = into
    entered = []
    for q in range(count):
        entered.append((c1, c2))
        if q < count - 1 or not closed:
            m, o = matrices(q), offsets(q)
            n1, n2 = m[0] * c1 + m[1] * c2, m[2] * c1 + m[3] * c2
            c1, c2 = (n1, n2) if o is None else (o[0] + n1, o[1] + n2)
    out = (c1, c2)
    result = [None] * count
    for q in reversed(range(count)):
        c1, c2 = entered[q]
        result[q] = (c1, c2, d1, d2)
        if q > 0 or not closed:
            m, o = matrices(q), offsets(q)
            n1, n2 = m[4] * c1 + m[5] * c2, m[8] * c1 + m[9] * c2
            if o is not None:
                n1, n2 = o[2] + n1, o[3] + n2
            d1, d2 = n1 + (m[6] * d1 + m[7] * d2), n2 + (m[10] * d1 + m[11] * d2)
    return result, out + (d1, d2)


class Exchange:
    def __init__(self, axis, count, send_sem, recv_sem):
        self.axis, self.count = axis, count
        self.send_sem, self.recv_sem = send_sem, recv_sem
        self.me = lax.axis_index(axis)

    def peers(self):
        return [lax.rem(self.me + k, self.count) for k in range(1, self.count)]

    def copy(self, kind, source, slots, p, slot, cut):
        pick = (lambda ref: ref) if cut is None else (lambda ref: ref.at[cut[0] : cut[1]])
        return pltpu.make_async_remote_copy(
            src_ref=pick(source(p)),
            dst_ref=pick(slots.at[slot]),
            send_sem=self.send_sem.at[kind, p],
            recv_sem=self.recv_sem.at[kind, slot],
            device_id={self.axis: p},
            device_id_type=MESH,
        )

    def start(self, kind, source, slots, cut=None, sends=None):
        for p in self.peers():
            go = lambda p=p: self.copy(kind, source, slots, p, self.me, cut).start()
            go() if sends is None else pl.when(sends(self.me, p))(go)

    def wait_recv(self, kind, source, slots, cut=None, sends=None):
        for p in self.peers():
            go = lambda p=p: self.copy(kind, source, slots, p, p, cut).wait_recv()
            go() if sends is None else pl.when(sends(p, self.me))(go)

    def wait_send(self, kind, source, slots, cut=None, sends=None):
        for p in self.peers():
            go = lambda p=p: self.copy(kind, source, slots, p, self.me, cut).wait_send()
            go() if sends is None else pl.when(sends(self.me, p))(go)


class Split:
    def __init__(self, exchange, lift, m_send, m_slots, o_send, o_slots, r_send, r_slots, full):
        self.x, self.lift = exchange, lift
        self.m_send, self.m_slots = m_send, m_slots
        self.o_send, self.o_slots = o_send, o_slots
        self.r_send, self.r_slots, self.full = r_send, r_slots, full
        self.parts = m_send.shape[0]
        self.rows = sublanes // self.parts
        pick = (lambda p: p) if self.parts > 1 else (lambda p: 0)
        last = exchange.count - 1
        m_from = lambda p: m_send.at[pick(p)]
        o_from = lambda p: o_send.at[pick(p)]
        r_from = lambda p: r_send.at[p]
        self.matrices = (0, m_from, m_slots)
        self.ahead = (1, o_from, o_slots, (0, 2), lambda a, b: a < last)
        self.behind = (2, o_from, o_slots, (2, 4), lambda a, b: a > 0)
        self.carried = (3, r_from, r_slots, (0, 2), lambda a, b: b > 0)
        self.returned = (4, r_from, r_slots, (2, 4), lambda a, b: b < last)
        self.pick = pick

    def clear_ends(self):
        if self.parts > 1:
            nothing = jnp.zeros((self.parts, 2) + self.r_slots.shape[2:], jnp.float32)

            @pl.when(self.x.me == 0)
            def _():
                self.r_slots[:, 0:2] = nothing

            @pl.when(self.x.me == self.x.count - 1)
            def _():
                self.r_slots[:, 2:4] = nothing

    def put(self, route, value, send, slots, lo):
        hi = lo + value.shape[0]
        for p in range(self.parts):
            send[p, lo:hi] = value[:, :, p * self.rows : (p + 1) * self.rows, :]
        slots[self.x.me, lo:hi] = send[self.pick(self.x.me), lo:hi]
        self.x.start(*route)

    def put_matrices(self, value):
        self.put(self.matrices, value, self.m_send, self.m_slots, 0)

    def put_ahead(self, value):
        self.put(self.ahead, value, self.o_send, self.o_slots, 0)

    def put_behind(self, value):
        self.put(self.behind, value, self.o_send, self.o_slots, 2)

    def solve(self):
        x = self.x
        for route in (self.matrices, self.ahead, self.behind):
            x.wait_recv(*route)
        zero = jnp.zeros(self.o_slots.shape[2:], jnp.float32)
        solved, _ = chain(
            x.count,
            lambda q: [self.lift(self.m_slots[q, k]) for k in range(12)],
            lambda q: [self.o_slots[q, k] for k in range(4)],
            (zero,) * 4,
            True,
        )
        for q, planes in enumerate(solved):
            for k in range(4):
                self.r_send[q, k] = planes[k]
        if self.parts > 1:
            x.start(*self.carried)
            x.start(*self.returned)
            me = x.me

            @pl.when(me > 0)
            def _():
                self.r_slots[me, 0:2] = self.r_send[me, 0:2]

            @pl.when(me < x.count - 1)
            def _():
                self.r_slots[me, 2:4] = self.r_send[me, 2:4]

    def result(self):
        x = self.x
        if self.parts == 1:
            return [self.r_send[x.me, k] for k in range(4)]
        x.wait_recv(*self.carried)
        x.wait_recv(*self.returned)
        for p in range(self.parts):
            self.full[:, :, p * self.rows : (p + 1) * self.rows, :] = self.r_slots[p]
        return [self.full[k] for k in range(4)]

    def finish(self):
        for route in (self.matrices, self.ahead, self.behind):
            self.x.wait_send(*route)
        if self.parts > 1:
            self.x.wait_send(*self.carried)
            self.x.wait_send(*self.returned)


def times(m, v):
    return m[0] * v[0] + m[1] * v[1], m[2] * v[0] + m[3] * v[1]


def plus(a, b):
    return a[0] + b[0], a[1] + b[1]


class Pairs:
    def __init__(self, exchange, lifts, m_own, m_in, g_own, g_in, streams, ss, rs):
        self.axis, self.me, self.lifts = exchange.axis, exchange.me, lifts
        self.m_own, self.m_in, self.g_own, self.g_in = m_own, m_in, g_own, g_in
        self.streams = streams
        ahead, behind, top, mid = (slice(0, 2), slice(2, 4), slice(0, 4), slice(4, 8))
        cut = lambda a, b, part: (a.at[part], b.at[part])
        self.messages = [
            (0, 1, 0, m_own, m_in),
            (0, 3, 2, *cut(m_own, m_in, mid)),
            (0, 2, 3, *cut(m_own, m_in, top)),
            (1, 2, 1, g_own, g_in),
            (1, 2, 0, g_own, g_in),
        ]
        for h, (o_own, o_in, j_own, j_in, _) in enumerate(streams):
            kind = 2 + 3 * h
            self.messages += [
                (kind, 0, 1, *cut(o_own, o_in, ahead)),
                (kind, 1, 0, *cut(o_own, o_in, ahead)),
                (kind, 2, 3, *cut(o_own, o_in, ahead)),
                (kind + 1, 1, 0, *cut(o_own, o_in, behind)),
                (kind + 1, 3, 2, *cut(o_own, o_in, behind)),
                (kind + 2, 1, 2, j_own, j_in),
                (kind + 2, 1, 3, j_own, j_in),
                (kind + 2, 2, 1, j_own, j_in),
                (kind + 2, 2, 0, j_own, j_in),
            ]
        self.ss, self.rs = ss, rs

    def copy(self, message):
        kind, _, to, source, destination = message
        return pltpu.make_async_remote_copy(
            src_ref=source,
            dst_ref=destination,
            send_sem=self.ss.at[kind, to],
            recv_sem=self.rs.at[kind],
            device_id={self.axis: to},
            device_id_type=MESH,
        )

    def role(self, number):
        return pl.when(self.me == number)

    def start(self, kind, number):
        for message in self.messages:
            if message[0] == kind and message[1] == number:
                self.copy(message).start()

    def start_all(self, kind):
        for number in range(4):
            if any(m[0] == kind and m[1] == number for m in self.messages):
                self.role(number)(lambda number=number: self.start(kind, number))

    def wait(self, kind, number):
        for message in self.messages:
            if message[0] == kind and message[2] == number:
                self.copy(message).wait_recv()

    def clear_ends(self):
        pass

    def put_matrices(self, value):
        for place, k in enumerate((0, 1, 2, 3, 4, 5, 8, 9, 6, 7, 10, 11)):
            self.m_own[place] = value[k]
        self.start_all(0)

    def join_matrices(self):
        @self.role(2)
        def _():
            self.wait(0, 2)
            own = [self.m_own[k] for k in range(12)]
            far = [self.m_in[4 + k] for k in range(4)]
            columns = []
            for j in range(2):
                through = times(far, (own[j], own[2 + j]))
                columns.append(plus((own[4 + j], own[6 + j]), times(own[8:12], through)))
            for i in range(2):
                for j in range(2):
                    self.g_own[2 * i + j] = columns[j][i]
            self.start(1, 2)

    def put_ahead(self, h, value):
        self.streams[h][0][0:2] = value
        self.start_all(2 + 3 * h)

    def put_behind(self, h, value):
        self.streams[h][0][2:4] = value
        self.start_all(3 + 3 * h)

    def solve(self, h):
        o_own, o_in, j_own, j_in, full = self.streams[h]
        kind = 2 + 3 * h
        lifted = lambda ref, lo: [self.lifts[h](ref[k]) for k in range(lo, lo + 4)]

        @self.role(1)
        def _():
            self.wait(kind, 1)
            c = plus((o_own[0], o_own[1]), times(lifted(self.m_own, 0), (o_in[0], o_in[1])))
            j_own[0], j_own[1] = c
            self.start(kind + 2, 1)

        @self.role(2)
        def _():
            self.wait(kind + 1, 2)
            far = plus((o_in[2], o_in[3]), times(lifted(self.m_in, 4), (o_own[0], o_own[1])))
            g = plus((o_own[2], o_own[3]), times(lifted(self.m_own, 8), far))
            j_own[0], j_own[1] = g
            self.start(kind + 2, 2)

    def result(self, h):
        o_own, o_in, j_own, j_in, full = self.streams[h]
        kind = 2 + 3 * h
        lifted = lambda ref, lo: [self.lifts[h](ref[k]) for k in range(lo, lo + 4)]
        pair = lambda ref, k: (ref[k], ref[k + 1])
        zero = jnp.zeros(full.shape[1:], jnp.float32)

        def store(c, d):
            for k, plane in enumerate((*c, *d)):
                full[k] = plane

        def wait(number, once, kinds):
            for k in (once if h == 0 else ()) + kinds:
                self.wait(k, number)

        @self.role(0)
        def _():
            wait(0, (0, 1), (kind, kind + 1, kind + 2))
            c1 = pair(o_own, 0)
            c2 = plus(pair(o_in, 0), times(lifted(self.m_in, 0), c1))
            d1 = plus(pair(j_in, 0), times(lifted(self.g_in, 0), c2))
            d0 = plus(pair(o_in, 2), times(lifted(self.m_in, 4), c1))
            store((zero, zero), plus(d0, times(lifted(self.m_in, 8), d1)))

        @self.role(1)
        def _():
            wait(1, (1,), (kind + 2,))
            store(
                pair(o_in, 0), plus(pair(j_in, 0), times(lifted(self.g_in, 0), pair(j_own, 0)))
            )

        @self.role(2)
        def _():
            wait(2, (), (kind + 2,))
            c2 = pair(j_in, 0)
            c3 = plus(pair(o_own, 0), times(lifted(self.m_own, 0), c2))
            store(c2, plus(pair(o_in, 2), times(lifted(self.m_in, 4), c3)))

        @self.role(3)
        def _():
            wait(3, (0,), (kind, kind + 2))
            c3 = plus(pair(o_in, 0), times(lifted(self.m_in, 0), pair(j_in, 0)))
            store(c3, (zero, zero))

        return [full[k] for k in range(4)]

    def finish(self):
        for number in range(4):

            @self.role(number)
            def _(number=number):
                for message in self.messages:
                    if message[1] == number:
                        self.copy(message).wait_send()


class Splits:
    def __init__(self, exchange, lifts, scratch):
        self.each = []
        for lift, (*buffers, ss, rs) in zip(lifts, scratch):
            own = Exchange(exchange.axis, exchange.count, ss, rs)
            self.each.append(Split(own, lift, *buffers))

    def clear_ends(self):
        for one in self.each:
            one.clear_ends()

    def put_matrices(self, value):
        for one in self.each:
            one.put_matrices(value)

    def join_matrices(self):
        pass

    def put_ahead(self, h, value):
        self.each[h].put_ahead(value)

    def put_behind(self, h, value):
        self.each[h].put_behind(value)

    def solve(self, h):
        self.each[h].solve()

    def result(self, h):
        return self.each[h].result()

    def finish(self):
        for one in self.each:
            one.finish()


def solver(exchange, lifts, scratch):
    if exchange.count == 4:
        return Pairs(exchange, lifts, *scratch)
    return Splits(exchange, lifts, scratch)


def corrected(local, response, incoming, lift):
    total = local
    for k in range(4):
        total = total + lift(response[k]) * incoming[k]
    return total


def kernel(
    counts, residual_hbm, flow_hbm, f_zeta_hbm, f_eta_hbm, f_xi_hbm, out,
    residual, flow, f_zeta, f_eta, f_xi, in_sem,
    z_scratch, x_scratch, e_streams, e_matrices, e_msend, e_mslots, e_inner, e_ss, e_rs,
    z_response, x_response, e_response, x_factors, e_factors, lines, turned, turned_factors,
    hz, hx_send, hx, he_send, he, padded, source, h_ss, h_rs,
):
    n_xi, n_eta, n_zeta = counts
    fields, cz, cx, cy = flow.shape
    planes = fields * cz
    xz = Exchange("zeta", n_zeta, None, None)
    xe = Exchange("eta", n_eta, e_ss, e_rs)
    xx = Exchange("xi", n_xi, None, None)
    per_tile = cy // (cz * cx)
    streams = streams_of(per_tile)
    lifts = [field_spread(own) for own in streams]
    zeta = solver(xz, lifts, z_scratch)
    xi = solver(xx, lifts, x_scratch)

    loads = [
        pltpu.make_async_copy(src, dst, in_sem.at[k])
        for k, (src, dst) in enumerate(
            (
                (flow_hbm, flow),
                (f_zeta_hbm, f_zeta),
                (f_xi_hbm, f_xi),
                (residual_hbm, residual),
                (f_eta_hbm, f_eta),
            )
        )
    ]
    loads[0].start()

    barrier = pltpu.get_barrier_semaphore()
    greeted = 0
    for x in (xz, xe, xx):
        for p in x.peers():
            pl.semaphore_signal(barrier, inc=1, device_id={x.axis: p}, device_id_type=MESH)
            greeted += 1

    for load in loads[1:]:
        load.start()
    zeta.clear_ends()
    xi.clear_ends()
    loads[0].wait()

    row = lambda x: flow[:, :, x : x + 1, :]
    hx_send[0, :, :, 0:1, :] = -dissipation * (row(cx - 2) - 4.0 * row(cx - 1))
    hx_send[0, :, :, 1:2, :] = -dissipation * row(cx - 1)
    hx_send[1, :, :, 0:1, :] = -dissipation * row(0)
    hx_send[1, :, :, 1:2, :] = -dissipation * (row(1) - 4.0 * row(0))

    pl.semaphore_wait(barrier, greeted)

    halos = (
        (xx, hx, lambda side: hx_send.at[side]),
        (xe, he, lambda side: he_send),
        (xz, hz, lambda side: flow_hbm.at[:, cz - 2 : cz] if side == 0 else flow_hbm.at[:, 0:2]),
    )

    def halo_copy(number, side):
        x, slots, origin = halos[number]
        step = 1 if side == 0 else x.count - 1
        return pltpu.make_async_remote_copy(
            src_ref=origin(side),
            dst_ref=slots.at[side],
            send_sem=h_ss.at[number, side],
            recv_sem=h_rs.at[number, side],
            device_id={x.axis: lax.rem(x.me + step, x.count)},
            device_id_type=MESH,
        )

    def halo_start(number):
        x = halos[number][0]
        for side in range(2):
            sends = x.me < x.count - 1 if side == 0 else x.me > 0
            pl.when(sends)(lambda side=side: halo_copy(number, side).start())

    halo_start(0)
    halo_start(2)
    per_pack = cy // 4
    lane = lax.broadcasted_iota(jnp.int32, (cx, cy), 1)
    packs = [jnp.zeros((cx, cy), jnp.float32) for _ in range(he_send.shape[0])]
    eta_part = []
    for k in range(planes):
        at = k % per_pack
        v = flow[k // cz, k % cz]
        up1, up2 = pltpu.roll(v, 1, 1), pltpu.roll(v, 2, 1)
        down1, down2 = pltpu.roll(v, cy - 1, 1), pltpu.roll(v, cy - 2, 1)
        near_low, near_high = lane < 1, lane >= cy - 1
        far_low, far_high = lane < 2, lane >= cy - 2
        near = jnp.where(near_low, 0.0, up1) + jnp.where(near_high, 0.0, down1)
        far = jnp.where(far_low, 0.0, up2) + jnp.where(far_high, 0.0, down2)
        eta_part.append(far - 4.0 * near)
        near = jnp.where(near_low, up1, jnp.where(near_high, down1, 0.0))
        far = jnp.where(far_low, up2, jnp.where(far_high, down2, 0.0))
        face = -dissipation * (far - 4.0 * near)
        moved = pltpu.roll(face, (4 * at + 2) % cy, 1)
        packs[k // per_pack] = jnp.where(lane // 4 == at, moved, packs[k // per_pack])
    for k, pack in enumerate(packs):
        he_send[k] = pack
    halo_start(1)
    for x, slots, origin in halos:
        for side in range(2):
            has = x.me > 0 if side == 0 else x.me < x.count - 1

            @pl.when(jnp.logical_not(has))
            def _(slots=slots, side=side):
                slots[side] = jnp.zeros(slots.shape[1:], jnp.float32)

    loads[1].wait()

    def keep_z(s, now):
        z_response[s] = now

    zeta.put_matrices(responses(cz, lambda k, s: f_zeta[:, k, s], keep_z))

    state = flow[...]
    nothing = jnp.zeros((fields, cz, 2, cy), jnp.float32)
    padded[:, :, 8 - 2 : 8, :] = nothing
    padded[:, :, 8 : 8 + cx, :] = state
    padded[:, :, 8 + cx : 8 + cx + 2, :] = nothing
    none = jnp.zeros((fields, 2, cx, cy), jnp.float32)
    long = jnp.concatenate([none, state, none], 1)
    near = (padded[:, :, 7 : 7 + cx, :] + padded[:, :, 9 : 9 + cx, :]) + (
        long[:, 1 : 1 + cz] + long[:, 3 : 3 + cz]
    )
    far = (padded[:, :, 6 : 6 + cx, :] + padded[:, :, 10 : 10 + cx, :]) + (
        long[:, 0:cz] + long[:, 4 : 4 + cz]
    )
    total_part = 18.0 * state - 4.0 * near + far + jnp.stack(eta_part).reshape(flow.shape)
    loads[3].wait()
    source[...] = residual[...] - dissipation * total_part

    loads[2].wait()

    for s in range(cx):
        for k in range(5):
            for g in range(3):
                x_factors[k, s, g] = f_xi[pl.ds((g * 5 + k) * cz * cx + s, cz, stride=cx), :]

    def xi_factor(k, s):
        return x_factors[k, s]

    def keep_x(s, now):
        x_response[s] = now

    xi.put_matrices(responses(cx, xi_factor, keep_x))
    zeta.join_matrices()

    for number, (x, slots, origin) in enumerate(halos):
        for side in range(2):
            has = x.me > 0 if side == 0 else x.me < x.count - 1
            pl.when(has)(lambda number=number, side=side: halo_copy(number, side).wait_recv())

    source[:, :, 0:2, :] += hx[0]
    source[:, :, cx - 2 : cx, :] += hx[1]
    zeta_faces = {
        0: hz[0, :, 0] - 4.0 * hz[0, :, 1],
        1: hz[0, :, 1],
        cz - 2: hz[1, :, 0],
        cz - 1: hz[1, :, 1] - 4.0 * hz[1, :, 0],
    }
    faces = [jnp.where(lane % 4 >= 2, he[0, k], he[1, k]) for k in range(he.shape[1])]
    edge = jnp.logical_or(lane < 2, lane >= cy - 2)

    def eta_face(f, z):
        k = f * cz + z
        back = (cy - (4 * (k % per_pack) + 2)) % cy
        return jnp.where(edge, pltpu.roll(faces[k // per_pack], back, 1), 0.0)

    def source_plane(own, z):
        value = jnp.stack([source[f, z] + eta_face(f, z) for f in own])
        if z in zeta_faces:
            value = value - dissipation * jnp.stack([zeta_faces[z][f] for f in own])
        return value

    z_local = []
    for h, own in enumerate(streams):
        z_factor = lambda k, s: lifts[h](f_zeta[:, k, s])
        zero = jnp.zeros((len(own), cx, cy), jnp.float32)
        forward = forward_sweep(cz, z_factor, lambda s: source_plane(own, s), zero, zero)
        zeta.put_ahead(h, jnp.stack([forward[-1], forward[-2]]))
        local = backward_sweep(
            cz, z_factor, lambda s: forward[s], zero, zero, lambda s, now: None
        )
        zeta.put_behind(h, jnp.stack([local[0], local[1]]))
        z_local.append(local)
    for h in range(len(streams)):
        zeta.solve(h)

    loads[4].wait()
    tiles = lines.shape[0] // cy
    steps = cy // sublanes
    total = lines.shape[0]
    distinct, uses = line_tiles(cy // (cz * cx))
    for k in range(5):
        for t, groups in enumerate(distinct):
            whole = jnp.concatenate([f_eta[g * 5 + k] for g in groups], 0)
            turned_factors[t * cy : (t + 1) * cy, :] = whole.T
        for s in range(steps):
            e_factors[k, s] = turned_factors[
                pl.ds(s, len(distinct) * sublanes, stride=steps), :
            ].reshape(len(distinct), sublanes, cy)

    def tiled(planes, at=slice(None)):
        return jnp.concatenate([planes[u : u + 1] for u in uses[at]], 0)

    xi.join_matrices()

    def eta_factor(k, s):
        return e_factors[k, s]

    def keep_e(s, now):
        e_response[s] = now

    e_matrices[...] = responses(steps, eta_factor, keep_e)
    chunk = lambda c: [e_matrices[k, :, c : c + 1, :] for k in range(12)]
    one = jnp.ones((1, len(distinct), 1, cy), jnp.float32)
    zero = jnp.zeros_like(one)
    unit = lambda j: jnp.concatenate([one if i == j else zero for i in range(4)], 0)
    inner, left = chain(sublanes, chunk, lambda c: None, [unit(j) for j in range(4)], False)
    for c, values in enumerate(inner):
        for k in range(4):
            e_inner[k, :, :, c : c + 1, :] = values[k]
    e_msend[...] = jnp.concatenate([left[0][0:2], left[1][0:2], left[2], left[3]], 0)
    e_mslots[xe.me] = e_msend[...]
    xe.start(0, lambda p: e_msend, e_mslots)

    if total > planes * cx:
        lines[planes * cx : total, :] = jnp.zeros((total - planes * cx, cy), jnp.float32)

    def turn(source_ref, target_ref, at):
        for t in range(at.start, at.stop):
            target_ref[t * cy : (t + 1) * cy, :] = source_ref[t * cy : (t + 1) * cy, :].T

    first, parts = 0, []
    for own in streams:
        count = -(-len(own) // per_tile)
        parts.append((first, slice(first // per_tile, first // per_tile + count)))
        first += len(own)
    e_local = []
    for h, own in enumerate(streams):
        place, at = parts[h]
        count = at.stop - at.start
        incoming = zeta.result(h)
        for s in range(cz):
            done = corrected(z_local[h][s], z_response[s], incoming, lifts[h])
            for k in range(len(own)):
                row = ((place + k) * cz + s) * cx
                lines[row : row + cx, :] = done[k]
        turn(lines, turned, at)
        offsets, o_send, o_slots, results, inside = e_streams[h]
        rows = lambda s: pl.ds(at.start * cy + s, count * sublanes, stride=steps)
        zero = jnp.zeros((count, sublanes, cy), jnp.float32)
        eta_tiles = lambda k, s: tiled(e_factors[k, s], at)
        forward = forward_sweep(
            steps, eta_tiles, lambda s: turned[rows(s), :].reshape(zero.shape), zero, zero
        )
        local = backward_sweep(
            steps, eta_tiles, lambda s: forward[s], zero, zero, lambda s, now: None
        )
        e_local.append(local)
        for k, value in enumerate((forward[-1], forward[-2], local[0], local[1])):
            offsets[k] = value
        none = jnp.zeros((count, 1, cy), jnp.float32)
        inner, left = chain(
            sublanes,
            lambda c: [tiled(plane, at) for plane in chunk(c)],
            lambda c: [offsets[k, :, c : c + 1, :] for k in range(4)],
            (none,) * 4,
            False,
        )
        for k in range(4):
            o_send[k] = left[k]
        o_slots[xe.me] = o_send[...]
        xe.start(1 + h, lambda p: o_send, o_slots)
        for c, values in enumerate(inner):
            for k in range(4):
                inside[k, :, c : c + 1, :] = values[k]

    x_local = []
    for h, own in enumerate(streams):
        place, at = parts[h]
        count = at.stop - at.start
        offsets, o_send, o_slots, results, inside = e_streams[h]
        if h == 0:
            xe.wait_recv(0, lambda p: e_msend, e_mslots)
        xe.wait_recv(1 + h, lambda p: o_send, o_slots)
        none = jnp.zeros((count, 1, cy), jnp.float32)
        solved, _ = chain(
            n_eta,
            lambda q: [tiled(e_mslots[q, k], at) for k in range(12)],
            lambda q: [o_slots[q, k] for k in range(4)],
            (none,) * 4,
            True,
        )
        for q, values in enumerate(solved):
            for k in range(4):
                results[q, k] = values[k]
        enters = [results[xe.me, k] for k in range(4)]
        incoming = []
        for k in range(4):
            value = inside[k]
            for j in range(2 if k < 2 else 4):
                value = value + tiled(e_inner[k, j], at) * enters[j]
            incoming.append(value)
        rows = lambda s: pl.ds(at.start * cy + s, count * sublanes, stride=steps)
        for s in range(steps):
            done = corrected(e_local[h][s], e_response[s], incoming, lambda r: tiled(r, at))
            turned[rows(s), :] = done.reshape(count * sublanes, cy)
        turn(turned, lines, at)
        x_factor = lambda k, s: lifts[h](xi_factor(k, s))
        zero = jnp.zeros((len(own), cz, cy), jnp.float32)
        columns = lambda s: pl.ds(place * cz * cx + s, len(own) * cz, stride=cx)
        forward = forward_sweep(
            cx, x_factor, lambda s: lines[columns(s), :].reshape(zero.shape), zero, zero
        )
        xi.put_ahead(h, jnp.stack([forward[-1], forward[-2]]))
        local = backward_sweep(
            cx, x_factor, lambda s: forward[s], zero, zero, lambda s, now: None
        )
        xi.put_behind(h, jnp.stack([local[0], local[1]]))
        x_local.append(local)
    for h in range(len(streams)):
        xi.solve(h)
    for h, own in enumerate(streams):
        incoming = xi.result(h)
        for s in range(cx):
            done = corrected(x_local[h][s], x_response[s], incoming, lifts[h])
            for k, f in enumerate(own):
                out[pl.ds(f * cz * cx + s, cz, stride=cx), :] = done[k]

    zeta.finish()
    xi.finish()
    xe.wait_send(0, lambda p: e_msend, e_mslots)
    for h, (_, o_send, o_slots, _, _) in enumerate(e_streams):
        xe.wait_send(1 + h, lambda p: o_send, o_slots)
    for number, (x, slots, origin) in enumerate(halos):
        for side in range(2):
            sends = x.me < x.count - 1 if side == 0 else x.me > 0
            pl.when(sends)(lambda number=number, side=side: halo_copy(number, side).wait_send())


def solver_scratch(count, streams, lanes):
    vmem = lambda *shape: pltpu.VMEM(shape, jnp.float32)
    dma = pltpu.SemaphoreType.DMA
    if count == 4:
        plane = (sublanes, lanes)
        return (
            vmem(12, 3, *plane),
            vmem(12, 3, *plane),
            vmem(4, 3, *plane),
            vmem(4, 3, *plane),
            tuple(
                tuple(vmem(n, len(own), *plane) for n in (4, 4, 2, 2, 4)) for own in streams
            ),
            dma((2 + 3 * len(streams), count)),
            dma((2 + 3 * len(streams),)),
        )
    parts = count if sublanes % count == 0 else 1
    rows = sublanes // parts
    return tuple(
        (
            vmem(parts, 12, 3, rows, lanes),
            vmem(count, 12, 3, rows, lanes),
            vmem(parts, 4, len(own), rows, lanes),
            vmem(count, 4, len(own), rows, lanes),
            vmem(count, 4, len(own), rows, lanes),
            vmem(count, 4, len(own), rows, lanes),
            vmem(4, len(own), sublanes, lanes),
            dma((5, count)),
            dma((5, count)),
        )
        for own in streams
    )


def on_device(counts, residual, flow_state, factors_zeta, factors_eta, factors_xi):
    n_xi, n_eta, n_zeta = counts
    fields, cz, cx, cy = flow_state.shape
    total = -(-(fields * cz * cx) // cy) * cy
    tiles = total // cy
    steps = cy // sublanes
    packs = -(-(fields * cz) // (cy // 4))
    distinct = len(line_tiles(cy // (cz * cx))[0])
    vmem = lambda *shape: pltpu.VMEM(shape, jnp.float32)
    dma = pltpu.SemaphoreType.DMA
    whole = pl.BlockSpec(memory_space=pltpu.VMEM)
    per_tile = cy // (cz * cx)
    streams = streams_of(per_tile)
    eta_streams = []
    for own in streams:
        count = -(-len(own) // per_tile)
        eta_streams.append(
            (
                vmem(4, count, sublanes, cy),
                vmem(4, count, 1, cy),
                vmem(n_eta, 4, count, 1, cy),
                vmem(n_eta, 4, count, 1, cy),
                vmem(4, count, sublanes, cy),
            )
        )
    scratch = (
        [
            vmem(fields, cz, cx, cy),
            vmem(fields, cz, cx, cy),
            vmem(3, 5, cz, cx, cy),
            vmem(15, cz * cx, cy),
            vmem(15 * cz * cx, cy),
            dma((5,)),
            solver_scratch(n_zeta, streams, cy),
            solver_scratch(n_xi, streams, cy),
            tuple(eta_streams),
            vmem(12, distinct, sublanes, cy),
            vmem(12, distinct, 1, cy),
            vmem(n_eta, 12, distinct, 1, cy),
            vmem(4, 4, distinct, sublanes, cy),
            dma((1 + len(streams), n_eta)),
            dma((1 + len(streams), n_eta)),
            vmem(cz, 4, 3, cx, cy),
            vmem(cx, 4, 3, cz, cy),
            vmem(steps, 4, distinct, sublanes, cy),
            vmem(5, cx, 3, cz, cy),
            vmem(5, steps, distinct, sublanes, cy),
            vmem(total, cy),
            vmem(total, cy),
            vmem(distinct * cy, cy),
            vmem(2, fields, 2, cx, cy),
            vmem(2, fields, cz, 2, cy),
            vmem(2, fields, cz, 2, cy),
            vmem(packs, cx, cy),
            vmem(2, packs, cx, cy),
            vmem(fields, cz, cx + 16, cy),
            vmem(fields, cz, cx, cy),
            dma((3, 2)),
            dma((3, 2)),
        ]
    )
    update = pl.pallas_call(
        functools.partial(kernel, counts),
        out_shape=jax.ShapeDtypeStruct((fields * cz * cx, cy), jnp.float32),
        in_specs=[pl.BlockSpec(memory_space=pltpu.HBM)] * 5,
        out_specs=whole,
        scratch_shapes=scratch,
        compiler_params=pltpu.CompilerParams(
            collective_id=0, has_side_effects=True, vmem_limit_bytes=24 * 2**20
        ),
    )(
        *(
            pltpu.with_memory_space_constraint(operand, pltpu.HBM)
            for operand in (
                residual,
                flow_state,
                factors_zeta,
                factors_eta.reshape(15, cz * cx, cy),
                factors_xi.reshape(15 * cz * cx, cy),
            )
        )
    )
    return update.reshape(flow_state.shape)


def solution(mesh):
    fields = P(None, "zeta", "xi", "eta")
    factors = P(None, None, "zeta", "xi", "eta")
    counts = tuple(mesh.shape[axis] for axis in ("xi", "eta", "zeta"))
    return jax.shard_map(
        functools.partial(on_device, counts),
        mesh=mesh,
        in_specs=(fields, fields, factors, factors, factors),
        out_specs=fields,
        check_vma=False,
    )
```

```python
import functools

import jax
import jax.numpy as jnp
from jax import lax
from jax.experimental import pallas as pl
from jax.experimental.pallas import tpu as pltpu
from jax.sharding import PartitionSpec as P

field_group = (0, 0, 0, 1, 2)
dissipation = 0.05
sublanes = 8
MESH = pl.DeviceIdType.MESH


line_order = (0, 3, 1, 4, 2)


def field_spread(own):
    return lambda planes: jnp.concatenate([planes[field_group[f]][None] for f in own], 0)


def streams_of(per_tile):
    return [own for own in (line_order[:per_tile], line_order[per_tile:]) if own]


def line_tiles(per_tile):
    distinct, uses = [], []
    for start in range(0, len(line_order), per_tile):
        groups = [field_group[f] for f in line_order[start : start + per_tile]]
        for number, have in enumerate(distinct):
            if have[: len(groups)] == groups:
                break
        else:
            number = len(distinct)
            distinct.append(groups + [groups[-1]] * (per_tile - len(groups)))
        uses.append(number)
    return distinct, uses


def forward_sweep(steps, factor, value, recent, before):
    rows = []
    for s in range(steps):
        now = -(factor(1, s) * before) if value is None else value(s) - factor(1, s) * before
        now = now - factor(0, s) * recent
        rows.append(now)
        recent, before = now, recent
    return rows


def backward_sweep(steps, factor, value, recent, before, keep):
    rows = [None] * steps
    for s in reversed(range(steps)):
        now = factor(2, s) * value(s) - factor(4, s) * before - factor(3, s) * recent
        rows[s] = now
        keep(s, now)
        recent, before = now, recent
    return rows


def responses(steps, factor, keep):
    one = jnp.ones_like(factor(0, 0))
    zero = jnp.zeros_like(one)
    lift = lambda k, s: factor(k, s)[None]
    forward = forward_sweep(
        steps, lift, None, jnp.stack([one, zero]), jnp.stack([zero, one])
    )
    none = jnp.zeros((2,) + one.shape, jnp.float32)
    backward = backward_sweep(
        steps,
        lift,
        lambda s: jnp.concatenate([forward[s], none], 0),
        jnp.stack([zero, zero, one, zero]),
        jnp.stack([zero, zero, zero, one]),
        keep,
    )
    return jnp.concatenate([forward[-1], forward[-2], backward[0], backward[1]], 0)


def chain(count, matrices, offsets, into, closed):
    c1, c2, d1, d2 = into
    entered = []
    for q in range(count):
        entered.append((c1, c2))
        if q < count - 1 or not closed:
            m, o = matrices(q), offsets(q)
            n1, n2 = m[0] * c1 + m[1] * c2, m[2] * c1 + m[3] * c2
            c1, c2 = (n1, n2) if o is None else (o[0] + n1, o[1] + n2)
    out = (c1, c2)
    result = [None] * count
    for q in reversed(range(count)):
        c1, c2 = entered[q]
        result[q] = (c1, c2, d1, d2)
        if q > 0 or not closed:
            m, o = matrices(q), offsets(q)
            n1, n2 = m[4] * c1 + m[5] * c2, m[8] * c1 + m[9] * c2
            if o is not None:
                n1, n2 = o[2] + n1, o[3] + n2
            d1, d2 = n1 + (m[6] * d1 + m[7] * d2), n2 + (m[10] * d1 + m[11] * d2)
    return result, out + (d1, d2)


class Exchange:
    def __init__(self, axis, count, send_sem, recv_sem):
        self.axis, self.count = axis, count
        self.send_sem, self.recv_sem = send_sem, recv_sem
        self.me = lax.axis_index(axis)

    def peers(self):
        return [lax.rem(self.me + k, self.count) for k in range(1, self.count)]

    def copy(self, kind, source, slots, p, slot, cut):
        pick = (lambda ref: ref) if cut is None else (lambda ref: ref.at[cut[0] : cut[1]])
        return pltpu.make_async_remote_copy(
            src_ref=pick(source(p)),
            dst_ref=pick(slots.at[slot]),
            send_sem=self.send_sem.at[kind, p],
            recv_sem=self.recv_sem.at[kind, slot],
            device_id={self.axis: p},
            device_id_type=MESH,
        )

    def start(self, kind, source, slots, cut=None, sends=None):
        for p in self.peers():
            go = lambda p=p: self.copy(kind, source, slots, p, self.me, cut).start()
            go() if sends is None else pl.when(sends(self.me, p))(go)

    def wait_recv(self, kind, source, slots, cut=None, sends=None):
        for p in self.peers():
            go = lambda p=p: self.copy(kind, source, slots, p, p, cut).wait_recv()
            go() if sends is None else pl.when(sends(p, self.me))(go)

    def wait_send(self, kind, source, slots, cut=None, sends=None):
        for p in self.peers():
            go = lambda p=p: self.copy(kind, source, slots, p, self.me, cut).wait_send()
            go() if sends is None else pl.when(sends(self.me, p))(go)


class Split:
    def __init__(self, exchange, lift, m_send, m_slots, o_send, o_slots, r_send, r_slots, full):
        self.x, self.lift = exchange, lift
        self.m_send, self.m_slots = m_send, m_slots
        self.o_send, self.o_slots = o_send, o_slots
        self.r_send, self.r_slots, self.full = r_send, r_slots, full
        self.parts = m_send.shape[0]
        self.rows = sublanes // self.parts
        pick = (lambda p: p) if self.parts > 1 else (lambda p: 0)
        last = exchange.count - 1
        m_from = lambda p: m_send.at[pick(p)]
        o_from = lambda p: o_send.at[pick(p)]
        r_from = lambda p: r_send.at[p]
        self.matrices = (0, m_from, m_slots)
        self.ahead = (1, o_from, o_slots, (0, 2), lambda a, b: a < last)
        self.behind = (2, o_from, o_slots, (2, 4), lambda a, b: a > 0)
        self.carried = (3, r_from, r_slots, (0, 2), lambda a, b: b > 0)
        self.returned = (4, r_from, r_slots, (2, 4), lambda a, b: b < last)
        self.pick = pick

    def clear_ends(self):
        if self.parts > 1:
            nothing = jnp.zeros((self.parts, 2) + self.r_slots.shape[2:], jnp.float32)

            @pl.when(self.x.me == 0)
            def _():
                self.r_slots[:, 0:2] = nothing

            @pl.when(self.x.me == self.x.count - 1)
            def _():
                self.r_slots[:, 2:4] = nothing

    def put(self, route, value, send, slots, lo):
        hi = lo + value.shape[0]
        for p in range(self.parts):
            send[p, lo:hi] = value[:, :, p * self.rows : (p + 1) * self.rows, :]
        slots[self.x.me, lo:hi] = send[self.pick(self.x.me), lo:hi]
        self.x.start(*route)

    def put_matrices(self, value):
        self.put(self.matrices, value, self.m_send, self.m_slots, 0)

    def put_ahead(self, value):
        self.put(self.ahead, value, self.o_send, self.o_slots, 0)

    def put_behind(self, value):
        self.put(self.behind, value, self.o_send, self.o_slots, 2)

    def solve(self):
        x = self.x
        for route in (self.matrices, self.ahead, self.behind):
            x.wait_recv(*route)
        zero = jnp.zeros(self.o_slots.shape[2:], jnp.float32)
        solved, _ = chain(
            x.count,
            lambda q: [self.lift(self.m_slots[q, k]) for k in range(12)],
            lambda q: [self.o_slots[q, k] for k in range(4)],
            (zero,) * 4,
            True,
        )
        for q, planes in enumerate(solved):
            for k in range(4):
                self.r_send[q, k] = planes[k]
        if self.parts > 1:
            x.start(*self.carried)
            x.start(*self.returned)
            me = x.me

            @pl.when(me > 0)
            def _():
                self.r_slots[me, 0:2] = self.r_send[me, 0:2]

            @pl.when(me < x.count - 1)
            def _():
                self.r_slots[me, 2:4] = self.r_send[me, 2:4]

    def result(self):
        x = self.x
        if self.parts == 1:
            return [self.r_send[x.me, k] for k in range(4)]
        x.wait_recv(*self.carried)
        x.wait_recv(*self.returned)
        for p in range(self.parts):
            self.full[:, :, p * self.rows : (p + 1) * self.rows, :] = self.r_slots[p]
        return [self.full[k] for k in range(4)]

    def finish(self):
        for route in (self.matrices, self.ahead, self.behind):
            self.x.wait_send(*route)
        if self.parts > 1:
            self.x.wait_send(*self.carried)
            self.x.wait_send(*self.returned)


def times(m, v):
    return m[0] * v[0] + m[1] * v[1], m[2] * v[0] + m[3] * v[1]


def plus(a, b):
    return a[0] + b[0], a[1] + b[1]


class Pairs:
    def __init__(self, exchange, lifts, m_own, m_in, g_own, g_in, streams, ss, rs):
        self.axis, self.me, self.lifts = exchange.axis, exchange.me, lifts
        self.m_own, self.m_in, self.g_own, self.g_in = m_own, m_in, g_own, g_in
        self.streams = streams
        ahead, behind, top, mid = (slice(0, 2), slice(2, 4), slice(0, 4), slice(4, 8))
        cut = lambda a, b, part: (a.at[part], b.at[part])
        self.messages = [
            (0, 1, 0, m_own, m_in),
            (0, 3, 2, *cut(m_own, m_in, mid)),
            (0, 2, 3, *cut(m_own, m_in, top)),
            (1, 2, 1, g_own, g_in),
            (1, 2, 0, g_own, g_in),
        ]
        for h, (o_own, o_in, j_own, j_in, _) in enumerate(streams):
            kind = 2 + 3 * h
            self.messages += [
                (kind, 0, 1, *cut(o_own, o_in, ahead)),
                (kind, 1, 0, *cut(o_own, o_in, ahead)),
                (kind, 2, 3, *cut(o_own, o_in, ahead)),
                (kind + 1, 1, 0, *cut(o_own, o_in, behind)),
                (kind + 1, 3, 2, *cut(o_own, o_in, behind)),
                (kind + 2, 1, 2, j_own, j_in),
                (kind + 2, 1, 3, j_own, j_in),
                (kind + 2, 2, 1, j_own, j_in),
                (kind + 2, 2, 0, j_own, j_in),
            ]
        self.ss, self.rs = ss, rs

    def copy(self, message):
        kind, _, to, source, destination = message
        return pltpu.make_async_remote_copy(
            src_ref=source,
            dst_ref=destination,
            send_sem=self.ss.at[kind, to],
            recv_sem=self.rs.at[kind],
            device_id={self.axis: to},
            device_id_type=MESH,
        )

    def role(self, number):
        return pl.when(self.me == number)

    def start(self, kind, number):
        for message in self.messages:
            if message[0] == kind and message[1] == number:
                self.copy(message).start()

    def start_all(self, kind):
        for number in range(4):
            if any(m[0] == kind and m[1] == number for m in self.messages):
                self.role(number)(lambda number=number: self.start(kind, number))

    def wait(self, kind, number):
        for message in self.messages:
            if message[0] == kind and message[2] == number:
                self.copy(message).wait_recv()

    def clear_ends(self):
        pass

    def put_matrices(self, value):
        for place, k in enumerate((0, 1, 2, 3, 4, 5, 8, 9, 6, 7, 10, 11)):
            self.m_own[place] = value[k]
        self.start_all(0)

    def join_matrices(self):
        @self.role(2)
        def _():
            self.wait(0, 2)
            own = [self.m_own[k] for k in range(12)]
            far = [self.m_in[4 + k] for k in range(4)]
            columns = []
            for j in range(2):
                through = times(far, (own[j], own[2 + j]))
                columns.append(plus((own[4 + j], own[6 + j]), times(own[8:12], through)))
            for i in range(2):
                for j in range(2):
                    self.g_own[2 * i + j] = columns[j][i]
            self.start(1, 2)

    def put_ahead(self, h, value):
        self.streams[h][0][0:2] = value
        self.start_all(2 + 3 * h)

    def put_behind(self, h, value):
        self.streams[h][0][2:4] = value
        self.start_all(3 + 3 * h)

    def solve(self, h):
        o_own, o_in, j_own, j_in, full = self.streams[h]
        kind = 2 + 3 * h
        lifted = lambda ref, lo: [self.lifts[h](ref[k]) for k in range(lo, lo + 4)]

        @self.role(1)
        def _():
            self.wait(kind, 1)
            c = plus((o_own[0], o_own[1]), times(lifted(self.m_own, 0), (o_in[0], o_in[1])))
            j_own[0], j_own[1] = c
            self.start(kind + 2, 1)

        @self.role(2)
        def _():
            self.wait(kind + 1, 2)
            far = plus((o_in[2], o_in[3]), times(lifted(self.m_in, 4), (o_own[0], o_own[1])))
            g = plus((o_own[2], o_own[3]), times(lifted(self.m_own, 8), far))
            j_own[0], j_own[1] = g
            self.start(kind + 2, 2)

    def result(self, h):
        o_own, o_in, j_own, j_in, full = self.streams[h]
        kind = 2 + 3 * h
        lifted = lambda ref, lo: [self.lifts[h](ref[k]) for k in range(lo, lo + 4)]
        pair = lambda ref, k: (ref[k], ref[k + 1])
        zero = jnp.zeros(full.shape[1:], jnp.float32)

        def store(c, d):
            for k, plane in enumerate((*c, *d)):
                full[k] = plane

        def wait(number, once, kinds):
            for k in (once if h == 0 else ()) + kinds:
                self.wait(k, number)

        @self.role(0)
        def _():
            wait(0, (0, 1), (kind, kind + 1, kind + 2))
            c1 = pair(o_own, 0)
            c2 = plus(pair(o_in, 0), times(lifted(self.m_in, 0), c1))
            d1 = plus(pair(j_in, 0), times(lifted(self.g_in, 0), c2))
            d0 = plus(pair(o_in, 2), times(lifted(self.m_in, 4), c1))
            store((zero, zero), plus(d0, times(lifted(self.m_in, 8), d1)))

        @self.role(1)
        def _():
            wait(1, (1,), (kind + 2,))
            store(
                pair(o_in, 0), plus(pair(j_in, 0), times(lifted(self.g_in, 0), pair(j_own, 0)))
            )

        @self.role(2)
        def _():
            wait(2, (), (kind + 2,))
            c2 = pair(j_in, 0)
            c3 = plus(pair(o_own, 0), times(lifted(self.m_own, 0), c2))
            store(c2, plus(pair(o_in, 2), times(lifted(self.m_in, 4), c3)))

        @self.role(3)
        def _():
            wait(3, (0,), (kind, kind + 2))
            c3 = plus(pair(o_in, 0), times(lifted(self.m_in, 0), pair(j_in, 0)))
            store(c3, (zero, zero))

        return [full[k] for k in range(4)]

    def finish(self):
        for number in range(4):

            @self.role(number)
            def _(number=number):
                for message in self.messages:
                    if message[1] == number:
                        self.copy(message).wait_send()


class Splits:
    def __init__(self, exchange, lifts, scratch):
        self.each = []
        for lift, (*buffers, ss, rs) in zip(lifts, scratch):
            own = Exchange(exchange.axis, exchange.count, ss, rs)
            self.each.append(Split(own, lift, *buffers))

    def clear_ends(self):
        for one in self.each:
            one.clear_ends()

    def put_matrices(self, value):
        for one in self.each:
            one.put_matrices(value)

    def join_matrices(self):
        pass

    def put_ahead(self, h, value):
        self.each[h].put_ahead(value)

    def put_behind(self, h, value):
        self.each[h].put_behind(value)

    def solve(self, h):
        self.each[h].solve()

    def result(self, h):
        return self.each[h].result()

    def finish(self):
        for one in self.each:
            one.finish()


def solver(exchange, lifts, scratch):
    if exchange.count == 4:
        return Pairs(exchange, lifts, *scratch)
    return Splits(exchange, lifts, scratch)


def corrected(local, response, incoming, lift):
    total = local
    for k in range(4):
        total = total + lift(response[k]) * incoming[k]
    return total


def kernel(
    counts, residual_hbm, flow_hbm, f_zeta_hbm, f_eta_hbm, f_xi_hbm, out,
    residual, flow, f_zeta, f_eta, f_xi, in_sem,
    z_scratch, x_scratch, e_streams, e_matrices, e_msend, e_mslots, e_inner, e_ss, e_rs,
    z_response, x_response, e_response, x_factors, e_factors, lines, turned, turned_factors,
    hz, hx_send, hx, he_send, he, padded, source, h_ss, h_rs,
):
    n_xi, n_eta, n_zeta = counts
    fields, cz, cx, cy = flow.shape
    planes = fields * cz
    xz = Exchange("zeta", n_zeta, None, None)
    xe = Exchange("eta", n_eta, e_ss, e_rs)
    xx = Exchange("xi", n_xi, None, None)
    per_tile = cy // (cz * cx)
    streams = streams_of(per_tile)
    lifts = [field_spread(own) for own in streams]
    zeta = solver(xz, lifts, z_scratch)
    xi = solver(xx, lifts, x_scratch)

    barrier = pltpu.get_barrier_semaphore()
    greeted = 0
    for x in (xz, xe, xx):
        for p in x.peers():
            pl.semaphore_signal(barrier, inc=1, device_id={x.axis: p}, device_id_type=MESH)
            greeted += 1

    loads = [
        pltpu.make_async_copy(src, dst, in_sem.at[k])
        for k, (src, dst) in enumerate(
            (
                (flow_hbm, flow),
                (f_zeta_hbm, f_zeta),
                (f_xi_hbm, f_xi),
                (residual_hbm, residual),
                (f_eta_hbm, f_eta),
            )
        )
    ]
    for load in loads:
        load.start()
    zeta.clear_ends()
    xi.clear_ends()
    loads[0].wait()

    per_pack = cy // 4
    lane = lax.broadcasted_iota(jnp.int32, (cx, cy), 1)
    packs = [jnp.zeros((cx, cy), jnp.float32) for _ in range(he_send.shape[0])]
    eta_part = []
    for k in range(planes):
        at = k % per_pack
        v = flow[k // cz, k % cz]
        up1, up2 = pltpu.roll(v, 1, 1), pltpu.roll(v, 2, 1)
        down1, down2 = pltpu.roll(v, cy - 1, 1), pltpu.roll(v, cy - 2, 1)
        near_low, near_high = lane < 1, lane >= cy - 1
        far_low, far_high = lane < 2, lane >= cy - 2
        near = jnp.where(near_low, 0.0, up1) + jnp.where(near_high, 0.0, down1)
        far = jnp.where(far_low, 0.0, up2) + jnp.where(far_high, 0.0, down2)
        eta_part.append(far - 4.0 * near)
        near = jnp.where(near_low, up1, jnp.where(near_high, down1, 0.0))
        far = jnp.where(far_low, up2, jnp.where(far_high, down2, 0.0))
        face = -dissipation * (far - 4.0 * near)
        moved = pltpu.roll(face, (4 * at + 2) % cy, 1)
        packs[k // per_pack] = jnp.where(lane // 4 == at, moved, packs[k // per_pack])
    for k, pack in enumerate(packs):
        he_send[k] = pack
    row = lambda x: flow[:, :, x : x + 1, :]
    hx_send[0, :, :, 0:1, :] = -dissipation * (row(cx - 2) - 4.0 * row(cx - 1))
    hx_send[0, :, :, 1:2, :] = -dissipation * row(cx - 1)
    hx_send[1, :, :, 0:1, :] = -dissipation * row(0)
    hx_send[1, :, :, 1:2, :] = -dissipation * (row(1) - 4.0 * row(0))

    pl.semaphore_wait(barrier, greeted)

    halos = (
        (xx, hx, lambda side: hx_send.at[side]),
        (xe, he, lambda side: he_send),
        (xz, hz, lambda side: flow.at[:, cz - 2 : cz] if side == 0 else flow.at[:, 0:2]),
    )

    def halo_copy(number, side):
        x, slots, origin = halos[number]
        step = 1 if side == 0 else x.count - 1
        return pltpu.make_async_remote_copy(
            src_ref=origin(side),
            dst_ref=slots.at[side],
            send_sem=h_ss.at[number, side],
            recv_sem=h_rs.at[number, side],
            device_id={x.axis: lax.rem(x.me + step, x.count)},
            device_id_type=MESH,
        )

    for number, (x, slots, origin) in enumerate(halos):
        for side in range(2):
            sends = x.me < x.count - 1 if side == 0 else x.me > 0
            has = x.me > 0 if side == 0 else x.me < x.count - 1
            pl.when(sends)(lambda number=number, side=side: halo_copy(number, side).start())

            @pl.when(jnp.logical_not(has))
            def _(slots=slots, side=side):
                slots[side] = jnp.zeros(slots.shape[1:], jnp.float32)

    loads[1].wait()

    def keep_z(s, now):
        z_response[s] = now

    zeta.put_matrices(responses(cz, lambda k, s: f_zeta[:, k, s], keep_z))

    state = flow[...]
    nothing = jnp.zeros((fields, cz, 2, cy), jnp.float32)
    padded[:, :, 8 - 2 : 8, :] = nothing
    padded[:, :, 8 : 8 + cx, :] = state
    padded[:, :, 8 + cx : 8 + cx + 2, :] = nothing
    none = jnp.zeros((fields, 2, cx, cy), jnp.float32)
    long = jnp.concatenate([none, state, none], 1)
    near = (padded[:, :, 7 : 7 + cx, :] + padded[:, :, 9 : 9 + cx, :]) + (
        long[:, 1 : 1 + cz] + long[:, 3 : 3 + cz]
    )
    far = (padded[:, :, 6 : 6 + cx, :] + padded[:, :, 10 : 10 + cx, :]) + (
        long[:, 0:cz] + long[:, 4 : 4 + cz]
    )
    total_part = 18.0 * state - 4.0 * near + far + jnp.stack(eta_part).reshape(flow.shape)
    loads[3].wait()
    source[...] = residual[...] - dissipation * total_part

    zeta.join_matrices()

    for number, (x, slots, origin) in enumerate(halos):
        for side in range(2):
            has = x.me > 0 if side == 0 else x.me < x.count - 1
            pl.when(has)(lambda number=number, side=side: halo_copy(number, side).wait_recv())

    source[:, :, 0:2, :] += hx[0]
    source[:, :, cx - 2 : cx, :] += hx[1]
    zeta_faces = {
        0: hz[0, :, 0] - 4.0 * hz[0, :, 1],
        1: hz[0, :, 1],
        cz - 2: hz[1, :, 0],
        cz - 1: hz[1, :, 1] - 4.0 * hz[1, :, 0],
    }
    faces = [jnp.where(lane % 4 >= 2, he[0, k], he[1, k]) for k in range(he.shape[1])]
    edge = jnp.logical_or(lane < 2, lane >= cy - 2)

    def eta_face(f, z):
        k = f * cz + z
        back = (cy - (4 * (k % per_pack) + 2)) % cy
        return jnp.where(edge, pltpu.roll(faces[k // per_pack], back, 1), 0.0)

    def source_plane(own, z):
        value = jnp.stack([source[f, z] + eta_face(f, z) for f in own])
        if z in zeta_faces:
            value = value - dissipation * jnp.stack([zeta_faces[z][f] for f in own])
        return value

    z_local = []
    for h, own in enumerate(streams):
        z_factor = lambda k, s: lifts[h](f_zeta[:, k, s])
        zero = jnp.zeros((len(own), cx, cy), jnp.float32)
        forward = forward_sweep(cz, z_factor, lambda s: source_plane(own, s), zero, zero)
        zeta.put_ahead(h, jnp.stack([forward[-1], forward[-2]]))
        local = backward_sweep(
            cz, z_factor, lambda s: forward[s], zero, zero, lambda s, now: None
        )
        zeta.put_behind(h, jnp.stack([local[0], local[1]]))
        z_local.append(local)
    for h in range(len(streams)):
        zeta.solve(h)

    loads[2].wait()

    for s in range(cx):
        for k in range(5):
            for g in range(3):
                x_factors[k, s, g] = f_xi[pl.ds((g * 5 + k) * cz * cx + s, cz, stride=cx), :]

    def xi_factor(k, s):
        return x_factors[k, s]

    def keep_x(s, now):
        x_response[s] = now

    xi.put_matrices(responses(cx, xi_factor, keep_x))

    loads[4].wait()
    tiles = lines.shape[0] // cy
    steps = cy // sublanes
    total = lines.shape[0]
    distinct, uses = line_tiles(cy // (cz * cx))
    for k in range(5):
        for t, groups in enumerate(distinct):
            whole = jnp.concatenate([f_eta[g * 5 + k] for g in groups], 0)
            turned_factors[t * cy : (t + 1) * cy, :] = whole.T
        for s in range(steps):
            e_factors[k, s] = turned_factors[
                pl.ds(s, len(distinct) * sublanes, stride=steps), :
            ].reshape(len(distinct), sublanes, cy)

    def tiled(planes, at=slice(None)):
        return jnp.concatenate([planes[u : u + 1] for u in uses[at]], 0)


    def eta_factor(k, s):
        return e_factors[k, s]

    def keep_e(s, now):
        e_response[s] = now

    e_matrices[...] = responses(steps, eta_factor, keep_e)
    chunk = lambda c: [e_matrices[k, :, c : c + 1, :] for k in range(12)]
    one = jnp.ones((1, len(distinct), 1, cy), jnp.float32)
    zero = jnp.zeros_like(one)
    unit = lambda j: jnp.concatenate([one if i == j else zero for i in range(4)], 0)
    inner, left = chain(sublanes, chunk, lambda c: None, [unit(j) for j in range(4)], False)
    for c, values in enumerate(inner):
        for k in range(4):
            e_inner[k, :, :, c : c + 1, :] = values[k]
    xi.join_matrices()
    e_msend[...] = jnp.concatenate([left[0][0:2], left[1][0:2], left[2], left[3]], 0)
    e_mslots[xe.me] = e_msend[...]
    xe.start(0, lambda p: e_msend, e_mslots)

    if total > planes * cx:
        lines[planes * cx : total, :] = jnp.zeros((total - planes * cx, cy), jnp.float32)

    def turn(source_ref, target_ref, at):
        for t in range(at.start, at.stop):
            target_ref[t * cy : (t + 1) * cy, :] = source_ref[t * cy : (t + 1) * cy, :].T

    first, parts = 0, []
    for own in streams:
        count = -(-len(own) // per_tile)
        parts.append((first, slice(first // per_tile, first // per_tile + count)))
        first += len(own)
    e_local = []
    for h, own in enumerate(streams):
        place, at = parts[h]
        count = at.stop - at.start
        incoming = zeta.result(h)
        for s in range(cz):
            done = corrected(z_local[h][s], z_response[s], incoming, lifts[h])
            for k in range(len(own)):
                row = ((place + k) * cz + s) * cx
                lines[row : row + cx, :] = done[k]
        turn(lines, turned, at)
        offsets, o_send, o_slots, results, inside = e_streams[h]
        rows = lambda s: pl.ds(at.start * cy + s, count * sublanes, stride=steps)
        zero = jnp.zeros((count, sublanes, cy), jnp.float32)
        eta_tiles = lambda k, s: tiled(e_factors[k, s], at)
        forward = forward_sweep(
            steps, eta_tiles, lambda s: turned[rows(s), :].reshape(zero.shape), zero, zero
        )
        local = backward_sweep(
            steps, eta_tiles, lambda s: forward[s], zero, zero, lambda s, now: None
        )
        e_local.append(local)
        for k, value in enumerate((forward[-1], forward[-2], local[0], local[1])):
            offsets[k] = value
        none = jnp.zeros((count, 1, cy), jnp.float32)
        inner, left = chain(
            sublanes,
            lambda c: [tiled(plane, at) for plane in chunk(c)],
            lambda c: [offsets[k, :, c : c + 1, :] for k in range(4)],
            (none,) * 4,
            False,
        )
        for k in range(4):
            o_send[k] = left[k]
        o_slots[xe.me] = o_send[...]
        xe.start(1 + h, lambda p: o_send, o_slots)
        for c, values in enumerate(inner):
            for k in range(4):
                inside[k, :, c : c + 1, :] = values[k]

    x_local = []
    for h, own in enumerate(streams):
        place, at = parts[h]
        count = at.stop - at.start
        offsets, o_send, o_slots, results, inside = e_streams[h]
        if h == 0:
            xe.wait_recv(0, lambda p: e_msend, e_mslots)
        xe.wait_recv(1 + h, lambda p: o_send, o_slots)
        none = jnp.zeros((count, 1, cy), jnp.float32)
        solved, _ = chain(
            n_eta,
            lambda q: [tiled(e_mslots[q, k], at) for k in range(12)],
            lambda q: [o_slots[q, k] for k in range(4)],
            (none,) * 4,
            True,
        )
        for q, values in enumerate(solved):
            for k in range(4):
                results[q, k] = values[k]
        enters = [results[xe.me, k] for k in range(4)]
        incoming = []
        for k in range(4):
            value = inside[k]
            for j in range(2 if k < 2 else 4):
                value = value + tiled(e_inner[k, j], at) * enters[j]
            incoming.append(value)
        rows = lambda s: pl.ds(at.start * cy + s, count * sublanes, stride=steps)
        for s in range(steps):
            done = corrected(e_local[h][s], e_response[s], incoming, lambda r: tiled(r, at))
            turned[rows(s), :] = done.reshape(count * sublanes, cy)
        turn(turned, lines, at)
        x_factor = lambda k, s: lifts[h](xi_factor(k, s))
        zero = jnp.zeros((len(own), cz, cy), jnp.float32)
        columns = lambda s: pl.ds(place * cz * cx + s, len(own) * cz, stride=cx)
        forward = forward_sweep(
            cx, x_factor, lambda s: lines[columns(s), :].reshape(zero.shape), zero, zero
        )
        xi.put_ahead(h, jnp.stack([forward[-1], forward[-2]]))
        local = backward_sweep(
            cx, x_factor, lambda s: forward[s], zero, zero, lambda s, now: None
        )
        xi.put_behind(h, jnp.stack([local[0], local[1]]))
        x_local.append(local)
    for h in range(len(streams)):
        xi.solve(h)
    for h, own in enumerate(streams):
        incoming = xi.result(h)
        for s in range(cx):
            done = corrected(x_local[h][s], x_response[s], incoming, lifts[h])
            for k, f in enumerate(own):
                out[pl.ds(f * cz * cx + s, cz, stride=cx), :] = done[k]

    zeta.finish()
    xi.finish()
    xe.wait_send(0, lambda p: e_msend, e_mslots)
    for h, (_, o_send, o_slots, _, _) in enumerate(e_streams):
        xe.wait_send(1 + h, lambda p: o_send, o_slots)
    for number, (x, slots, origin) in enumerate(halos):
        for side in range(2):
            sends = x.me < x.count - 1 if side == 0 else x.me > 0
            pl.when(sends)(lambda number=number, side=side: halo_copy(number, side).wait_send())


def solver_scratch(count, streams, lanes):
    vmem = lambda *shape: pltpu.VMEM(shape, jnp.float32)
    dma = pltpu.SemaphoreType.DMA
    if count == 4:
        plane = (sublanes, lanes)
        return (
            vmem(12, 3, *plane),
            vmem(12, 3, *plane),
            vmem(4, 3, *plane),
            vmem(4, 3, *plane),
            tuple(
                tuple(vmem(n, len(own), *plane) for n in (4, 4, 2, 2, 4)) for own in streams
            ),
            dma((2 + 3 * len(streams), count)),
            dma((2 + 3 * len(streams),)),
        )
    parts = count if sublanes % count == 0 else 1
    rows = sublanes // parts
    return tuple(
        (
            vmem(parts, 12, 3, rows, lanes),
            vmem(count, 12, 3, rows, lanes),
            vmem(parts, 4, len(own), rows, lanes),
            vmem(count, 4, len(own), rows, lanes),
            vmem(count, 4, len(own), rows, lanes),
            vmem(count, 4, len(own), rows, lanes),
            vmem(4, len(own), sublanes, lanes),
            dma((5, count)),
            dma((5, count)),
        )
        for own in streams
    )


def on_device(counts, residual, flow_state, factors_zeta, factors_eta, factors_xi):
    n_xi, n_eta, n_zeta = counts
    fields, cz, cx, cy = flow_state.shape
    total = -(-(fields * cz * cx) // cy) * cy
    tiles = total // cy
    steps = cy // sublanes
    packs = -(-(fields * cz) // (cy // 4))
    distinct = len(line_tiles(cy // (cz * cx))[0])
    vmem = lambda *shape: pltpu.VMEM(shape, jnp.float32)
    dma = pltpu.SemaphoreType.DMA
    whole = pl.BlockSpec(memory_space=pltpu.VMEM)
    per_tile = cy // (cz * cx)
    streams = streams_of(per_tile)
    eta_streams = []
    for own in streams:
        count = -(-len(own) // per_tile)
        eta_streams.append(
            (
                vmem(4, count, sublanes, cy),
                vmem(4, count, 1, cy),
                vmem(n_eta, 4, count, 1, cy),
                vmem(n_eta, 4, count, 1, cy),
                vmem(4, count, sublanes, cy),
            )
        )
    scratch = (
        [
            vmem(fields, cz, cx, cy),
            vmem(fields, cz, cx, cy),
            vmem(3, 5, cz, cx, cy),
            vmem(15, cz * cx, cy),
            vmem(15 * cz * cx, cy),
            dma((5,)),
            solver_scratch(n_zeta, streams, cy),
            solver_scratch(n_xi, streams, cy),
            tuple(eta_streams),
            vmem(12, distinct, sublanes, cy),
            vmem(12, distinct, 1, cy),
            vmem(n_eta, 12, distinct, 1, cy),
            vmem(4, 4, distinct, sublanes, cy),
            dma((1 + len(streams), n_eta)),
            dma((1 + len(streams), n_eta)),
            vmem(cz, 4, 3, cx, cy),
            vmem(cx, 4, 3, cz, cy),
            vmem(steps, 4, distinct, sublanes, cy),
            vmem(5, cx, 3, cz, cy),
            vmem(5, steps, distinct, sublanes, cy),
            vmem(total, cy),
            vmem(total, cy),
            vmem(distinct * cy, cy),
            vmem(2, fields, 2, cx, cy),
            vmem(2, fields, cz, 2, cy),
            vmem(2, fields, cz, 2, cy),
            vmem(packs, cx, cy),
            vmem(2, packs, cx, cy),
            vmem(fields, cz, cx + 16, cy),
            vmem(fields, cz, cx, cy),
            dma((3, 2)),
            dma((3, 2)),
        ]
    )
    update = pl.pallas_call(
        functools.partial(kernel, counts),
        out_shape=jax.ShapeDtypeStruct((fields * cz * cx, cy), jnp.float32),
        in_specs=[pl.BlockSpec(memory_space=pltpu.HBM)] * 5,
        out_specs=whole,
        scratch_shapes=scratch,
        compiler_params=pltpu.CompilerParams(
            collective_id=0, has_side_effects=True, vmem_limit_bytes=24 * 2**20
        ),
    )(
        *(
            pltpu.with_memory_space_constraint(operand, pltpu.HBM)
            for operand in (
                residual,
                flow_state,
                factors_zeta,
                factors_eta.reshape(15, cz * cx, cy),
                factors_xi.reshape(15 * cz * cx, cy),
            )
        )
    )
    return update.reshape(flow_state.shape)


def solution(mesh):
    fields = P(None, "zeta", "xi", "eta")
    factors = P(None, None, "zeta", "xi", "eta")
    counts = tuple(mesh.shape[axis] for axis in ("xi", "eta", "zeta"))
    return jax.shard_map(
        functools.partial(on_device, counts),
        mesh=mesh,
        in_specs=(fields, fields, factors, factors, factors),
        out_specs=fields,
        check_vma=False,
    )
```

```python
import functools

import jax
import jax.numpy as jnp
from jax import lax
from jax.experimental import pallas as pl
from jax.experimental.pallas import tpu as pltpu
from jax.sharding import PartitionSpec as P

field_group = (0, 0, 0, 1, 2)
dissipation = 0.05
sublanes = 8
MESH = pl.DeviceIdType.MESH


line_order = (0, 3, 1, 4, 2)


def field_spread(own):
    return lambda planes: jnp.concatenate([planes[field_group[f]][None] for f in own], 0)


def streams_of(per_tile):
    return [line_order[k : k + per_tile] for k in range(0, len(line_order), per_tile)]


def line_tiles(per_tile):
    distinct, uses = [], []
    for start in range(0, len(line_order), per_tile):
        groups = [field_group[f] for f in line_order[start : start + per_tile]]
        for number, have in enumerate(distinct):
            if have[: len(groups)] == groups:
                break
        else:
            number = len(distinct)
            distinct.append(groups + [groups[-1]] * (per_tile - len(groups)))
        uses.append(number)
    return distinct, uses


def forward_sweep(steps, factor, value, recent, before):
    rows = []
    for s in range(steps):
        now = -(factor(1, s) * before) if value is None else value(s) - factor(1, s) * before
        now = now - factor(0, s) * recent
        rows.append(now)
        recent, before = now, recent
    return rows


def backward_sweep(steps, factor, value, recent, before, keep):
    rows = [None] * steps
    for s in reversed(range(steps)):
        now = factor(2, s) * value(s) - factor(4, s) * before - factor(3, s) * recent
        rows[s] = now
        keep(s, now)
        recent, before = now, recent
    return rows


def responses(steps, factor, keep):
    one = jnp.ones_like(factor(0, 0))
    zero = jnp.zeros_like(one)
    lift = lambda k, s: factor(k, s)[None]
    forward = forward_sweep(
        steps, lift, None, jnp.stack([one, zero]), jnp.stack([zero, one])
    )
    none = jnp.zeros((2,) + one.shape, jnp.float32)
    backward = backward_sweep(
        steps,
        lift,
        lambda s: jnp.concatenate([forward[s], none], 0),
        jnp.stack([zero, zero, one, zero]),
        jnp.stack([zero, zero, zero, one]),
        keep,
    )
    return jnp.concatenate([forward[-1], forward[-2], backward[0], backward[1]], 0)


def chain(count, matrices, offsets, into, closed):
    c1, c2, d1, d2 = into
    entered = []
    for q in range(count):
        entered.append((c1, c2))
        if q < count - 1 or not closed:
            m, o = matrices(q), offsets(q)
            n1, n2 = m[0] * c1 + m[1] * c2, m[2] * c1 + m[3] * c2
            c1, c2 = (n1, n2) if o is None else (o[0] + n1, o[1] + n2)
    out = (c1, c2)
    result = [None] * count
    for q in reversed(range(count)):
        c1, c2 = entered[q]
        result[q] = (c1, c2, d1, d2)
        if q > 0 or not closed:
            m, o = matrices(q), offsets(q)
            n1, n2 = m[4] * c1 + m[5] * c2, m[8] * c1 + m[9] * c2
            if o is not None:
                n1, n2 = o[2] + n1, o[3] + n2
            d1, d2 = n1 + (m[6] * d1 + m[7] * d2), n2 + (m[10] * d1 + m[11] * d2)
    return result, out + (d1, d2)


class Exchange:
    def __init__(self, axis, count, send_sem, recv_sem):
        self.axis, self.count = axis, count
        self.send_sem, self.recv_sem = send_sem, recv_sem
        self.me = lax.axis_index(axis)

    def peers(self):
        return [lax.rem(self.me + k, self.count) for k in range(1, self.count)]

    def copy(self, kind, source, slots, p, slot, cut):
        pick = (lambda ref: ref) if cut is None else (lambda ref: ref.at[cut[0] : cut[1]])
        return pltpu.make_async_remote_copy(
            src_ref=pick(source(p)),
            dst_ref=pick(slots.at[slot]),
            send_sem=self.send_sem.at[kind, p],
            recv_sem=self.recv_sem.at[kind, slot],
            device_id={self.axis: p},
            device_id_type=MESH,
        )

    def start(self, kind, source, slots, cut=None, sends=None):
        for p in self.peers():
            go = lambda p=p: self.copy(kind, source, slots, p, self.me, cut).start()
            go() if sends is None else pl.when(sends(self.me, p))(go)

    def wait_recv(self, kind, source, slots, cut=None, sends=None):
        for p in self.peers():
            go = lambda p=p: self.copy(kind, source, slots, p, p, cut).wait_recv()
            go() if sends is None else pl.when(sends(p, self.me))(go)

    def wait_send(self, kind, source, slots, cut=None, sends=None):
        for p in self.peers():
            go = lambda p=p: self.copy(kind, source, slots, p, self.me, cut).wait_send()
            go() if sends is None else pl.when(sends(self.me, p))(go)


class Split:
    def __init__(self, exchange, lift, m_send, m_slots, o_send, o_slots, r_send, r_slots, full):
        self.x, self.lift = exchange, lift
        self.m_send, self.m_slots = m_send, m_slots
        self.o_send, self.o_slots = o_send, o_slots
        self.r_send, self.r_slots, self.full = r_send, r_slots, full
        self.parts = m_send.shape[0]
        self.rows = sublanes // self.parts
        pick = (lambda p: p) if self.parts > 1 else (lambda p: 0)
        last = exchange.count - 1
        m_from = lambda p: m_send.at[pick(p)]
        o_from = lambda p: o_send.at[pick(p)]
        r_from = lambda p: r_send.at[p]
        self.matrices = (0, m_from, m_slots)
        self.ahead = (1, o_from, o_slots, (0, 2), lambda a, b: a < last)
        self.behind = (2, o_from, o_slots, (2, 4), lambda a, b: a > 0)
        self.carried = (3, r_from, r_slots, (0, 2), lambda a, b: b > 0)
        self.returned = (4, r_from, r_slots, (2, 4), lambda a, b: b < last)
        self.pick = pick

    def clear_ends(self):
        if self.parts > 1:
            nothing = jnp.zeros((self.parts, 2) + self.r_slots.shape[2:], jnp.float32)

            @pl.when(self.x.me == 0)
            def _():
                self.r_slots[:, 0:2] = nothing

            @pl.when(self.x.me == self.x.count - 1)
            def _():
                self.r_slots[:, 2:4] = nothing

    def put(self, route, value, send, slots, lo):
        hi = lo + value.shape[0]
        for p in range(self.parts):
            send[p, lo:hi] = value[:, :, p * self.rows : (p + 1) * self.rows, :]
        slots[self.x.me, lo:hi] = send[self.pick(self.x.me), lo:hi]
        self.x.start(*route)

    def put_matrices(self, value):
        self.put(self.matrices, value, self.m_send, self.m_slots, 0)

    def put_ahead(self, value):
        self.put(self.ahead, value, self.o_send, self.o_slots, 0)

    def put_behind(self, value):
        self.put(self.behind, value, self.o_send, self.o_slots, 2)

    def solve(self):
        x = self.x
        for route in (self.matrices, self.ahead, self.behind):
            x.wait_recv(*route)
        zero = jnp.zeros(self.o_slots.shape[2:], jnp.float32)
        solved, _ = chain(
            x.count,
            lambda q: [self.lift(self.m_slots[q, k]) for k in range(12)],
            lambda q: [self.o_slots[q, k] for k in range(4)],
            (zero,) * 4,
            True,
        )
        for q, planes in enumerate(solved):
            for k in range(4):
                self.r_send[q, k] = planes[k]
        if self.parts > 1:
            x.start(*self.carried)
            x.start(*self.returned)
            me = x.me

            @pl.when(me > 0)
            def _():
                self.r_slots[me, 0:2] = self.r_send[me, 0:2]

            @pl.when(me < x.count - 1)
            def _():
                self.r_slots[me, 2:4] = self.r_send[me, 2:4]

    def result(self):
        x = self.x
        if self.parts == 1:
            return [self.r_send[x.me, k] for k in range(4)]
        x.wait_recv(*self.carried)
        x.wait_recv(*self.returned)
        for p in range(self.parts):
            self.full[:, :, p * self.rows : (p + 1) * self.rows, :] = self.r_slots[p]
        return [self.full[k] for k in range(4)]

    def finish(self):
        for route in (self.matrices, self.ahead, self.behind):
            self.x.wait_send(*route)
        if self.parts > 1:
            self.x.wait_send(*self.carried)
            self.x.wait_send(*self.returned)


def times(m, v):
    return m[0] * v[0] + m[1] * v[1], m[2] * v[0] + m[3] * v[1]


def plus(a, b):
    return a[0] + b[0], a[1] + b[1]


class Pairs:
    def __init__(self, exchange, lifts, m_own, m_in, g_own, g_in, streams, ss, rs):
        self.axis, self.me, self.lifts = exchange.axis, exchange.me, lifts
        self.m_own, self.m_in, self.g_own, self.g_in = m_own, m_in, g_own, g_in
        self.streams = streams
        ahead, behind, top, mid = (slice(0, 2), slice(2, 4), slice(0, 4), slice(4, 8))
        cut = lambda a, b, part: (a.at[part], b.at[part])
        self.messages = [
            (0, 1, 0, m_own, m_in),
            (0, 3, 2, *cut(m_own, m_in, mid)),
            (0, 2, 3, *cut(m_own, m_in, top)),
            (1, 2, 1, g_own, g_in),
            (1, 2, 0, g_own, g_in),
        ]
        for h, (o_own, o_in, j_own, j_in, _) in enumerate(streams):
            kind = 2 + 3 * h
            self.messages += [
                (kind, 0, 1, *cut(o_own, o_in, ahead)),
                (kind, 1, 0, *cut(o_own, o_in, ahead)),
                (kind, 2, 3, *cut(o_own, o_in, ahead)),
                (kind + 1, 1, 0, *cut(o_own, o_in, behind)),
                (kind + 1, 3, 2, *cut(o_own, o_in, behind)),
                (kind + 2, 1, 2, j_own, j_in),
                (kind + 2, 1, 3, j_own, j_in),
                (kind + 2, 2, 1, j_own, j_in),
                (kind + 2, 2, 0, j_own, j_in),
            ]
        self.ss, self.rs = ss, rs

    def copy(self, message):
        kind, _, to, source, destination = message
        return pltpu.make_async_remote_copy(
            src_ref=source,
            dst_ref=destination,
            send_sem=self.ss.at[kind, to],
            recv_sem=self.rs.at[kind],
            device_id={self.axis: to},
            device_id_type=MESH,
        )

    def role(self, number):
        return pl.when(self.me == number)

    def start(self, kind, number):
        for message in self.messages:
            if message[0] == kind and message[1] == number:
                self.copy(message).start()

    def start_all(self, kind):
        for number in range(4):
            if any(m[0] == kind and m[1] == number for m in self.messages):
                self.role(number)(lambda number=number: self.start(kind, number))

    def wait(self, kind, number):
        for message in self.messages:
            if message[0] == kind and message[2] == number:
                self.copy(message).wait_recv()

    def clear_ends(self):
        pass

    def put_matrices(self, value):
        for place, k in enumerate((0, 1, 2, 3, 4, 5, 8, 9, 6, 7, 10, 11)):
            self.m_own[place] = value[k]
        self.start_all(0)

    def join_matrices(self):
        @self.role(2)
        def _():
            self.wait(0, 2)
            own = [self.m_own[k] for k in range(12)]
            far = [self.m_in[4 + k] for k in range(4)]
            columns = []
            for j in range(2):
                through = times(far, (own[j], own[2 + j]))
                columns.append(plus((own[4 + j], own[6 + j]), times(own[8:12], through)))
            for i in range(2):
                for j in range(2):
                    self.g_own[2 * i + j] = columns[j][i]
            self.start(1, 2)

    def put_ahead(self, h, value):
        self.streams[h][0][0:2] = value
        self.start_all(2 + 3 * h)

    def put_behind(self, h, value):
        self.streams[h][0][2:4] = value
        self.start_all(3 + 3 * h)

    def solve(self, h):
        o_own, o_in, j_own, j_in, full = self.streams[h]
        kind = 2 + 3 * h
        lifted = lambda ref, lo: [self.lifts[h](ref[k]) for k in range(lo, lo + 4)]

        @self.role(1)
        def _():
            self.wait(kind, 1)
            c = plus((o_own[0], o_own[1]), times(lifted(self.m_own, 0), (o_in[0], o_in[1])))
            j_own[0], j_own[1] = c
            self.start(kind + 2, 1)

        @self.role(2)
        def _():
            self.wait(kind + 1, 2)
            far = plus((o_in[2], o_in[3]), times(lifted(self.m_in, 4), (o_own[0], o_own[1])))
            g = plus((o_own[2], o_own[3]), times(lifted(self.m_own, 8), far))
            j_own[0], j_own[1] = g
            self.start(kind + 2, 2)

    def result(self, h):
        o_own, o_in, j_own, j_in, full = self.streams[h]
        kind = 2 + 3 * h
        lifted = lambda ref, lo: [self.lifts[h](ref[k]) for k in range(lo, lo + 4)]
        pair = lambda ref, k: (ref[k], ref[k + 1])
        zero = jnp.zeros(full.shape[1:], jnp.float32)

        def store(c, d):
            for k, plane in enumerate((*c, *d)):
                full[k] = plane

        def wait(number, once, kinds):
            for k in (once if h == 0 else ()) + kinds:
                self.wait(k, number)

        @self.role(0)
        def _():
            wait(0, (0, 1), (kind, kind + 1, kind + 2))
            c1 = pair(o_own, 0)
            c2 = plus(pair(o_in, 0), times(lifted(self.m_in, 0), c1))
            d1 = plus(pair(j_in, 0), times(lifted(self.g_in, 0), c2))
            d0 = plus(pair(o_in, 2), times(lifted(self.m_in, 4), c1))
            store((zero, zero), plus(d0, times(lifted(self.m_in, 8), d1)))

        @self.role(1)
        def _():
            wait(1, (1,), (kind + 2,))
            store(
                pair(o_in, 0), plus(pair(j_in, 0), times(lifted(self.g_in, 0), pair(j_own, 0)))
            )

        @self.role(2)
        def _():
            wait(2, (), (kind + 2,))
            c2 = pair(j_in, 0)
            c3 = plus(pair(o_own, 0), times(lifted(self.m_own, 0), c2))
            store(c2, plus(pair(o_in, 2), times(lifted(self.m_in, 4), c3)))

        @self.role(3)
        def _():
            wait(3, (0,), (kind, kind + 2))
            c3 = plus(pair(o_in, 0), times(lifted(self.m_in, 0), pair(j_in, 0)))
            store(c3, (zero, zero))

        return [full[k] for k in range(4)]

    def finish(self):
        for number in range(4):

            @self.role(number)
            def _(number=number):
                for message in self.messages:
                    if message[1] == number:
                        self.copy(message).wait_send()


class Splits:
    def __init__(self, exchange, lifts, scratch):
        self.each = []
        for lift, (*buffers, ss, rs) in zip(lifts, scratch):
            own = Exchange(exchange.axis, exchange.count, ss, rs)
            self.each.append(Split(own, lift, *buffers))

    def clear_ends(self):
        for one in self.each:
            one.clear_ends()

    def put_matrices(self, value):
        for one in self.each:
            one.put_matrices(value)

    def join_matrices(self):
        pass

    def put_ahead(self, h, value):
        self.each[h].put_ahead(value)

    def put_behind(self, h, value):
        self.each[h].put_behind(value)

    def solve(self, h):
        self.each[h].solve()

    def result(self, h):
        return self.each[h].result()

    def finish(self):
        for one in self.each:
            one.finish()


def solver(exchange, lifts, scratch):
    if exchange.count == 4:
        return Pairs(exchange, lifts, *scratch)
    return Splits(exchange, lifts, scratch)


def corrected(local, response, incoming, lift):
    total = local
    for k in range(4):
        total = total + lift(response[k]) * incoming[k]
    return total


def kernel(
    counts, residual_hbm, flow_hbm, f_zeta_hbm, f_eta_hbm, f_xi_hbm, out,
    residual, flow, f_zeta, f_eta, f_xi, in_sem,
    z_scratch, x_scratch, e_streams, e_matrices, e_msend, e_mslots, e_inner, e_ss, e_rs,
    z_response, x_response, e_response, x_factors, e_factors, lines, turned, turned_factors,
    hz, hx_send, hx, he_send, he, padded, source, h_ss, h_rs,
):
    n_xi, n_eta, n_zeta = counts
    fields, cz, cx, cy = flow.shape
    planes = fields * cz
    xz = Exchange("zeta", n_zeta, None, None)
    xe = Exchange("eta", n_eta, e_ss, e_rs)
    xx = Exchange("xi", n_xi, None, None)
    per_tile = cy // (cz * cx)
    streams = streams_of(per_tile)
    lifts = [field_spread(own) for own in streams]
    zeta = solver(xz, lifts, z_scratch)
    xi = solver(xx, lifts, x_scratch)

    barrier = pltpu.get_barrier_semaphore()
    greeted = 0
    for x in (xz, xe, xx):
        for p in x.peers():
            pl.semaphore_signal(barrier, inc=1, device_id={x.axis: p}, device_id_type=MESH)
            greeted += 1

    loads = [
        pltpu.make_async_copy(src, dst, in_sem.at[k])
        for k, (src, dst) in enumerate(
            (
                (flow_hbm, flow),
                (f_zeta_hbm, f_zeta),
                (f_xi_hbm, f_xi),
                (residual_hbm, residual),
                (f_eta_hbm, f_eta),
            )
        )
    ]
    for load in loads:
        load.start()
    zeta.clear_ends()
    xi.clear_ends()
    loads[0].wait()

    per_pack = cy // 4
    lane = lax.broadcasted_iota(jnp.int32, (cx, cy), 1)
    packs = [jnp.zeros((cx, cy), jnp.float32) for _ in range(he_send.shape[0])]
    eta_part = []
    for k in range(planes):
        at = k % per_pack
        v = flow[k // cz, k % cz]
        up1, up2 = pltpu.roll(v, 1, 1), pltpu.roll(v, 2, 1)
        down1, down2 = pltpu.roll(v, cy - 1, 1), pltpu.roll(v, cy - 2, 1)
        near_low, near_high = lane < 1, lane >= cy - 1
        far_low, far_high = lane < 2, lane >= cy - 2
        near = jnp.where(near_low, 0.0, up1) + jnp.where(near_high, 0.0, down1)
        far = jnp.where(far_low, 0.0, up2) + jnp.where(far_high, 0.0, down2)
        eta_part.append(far - 4.0 * near)
        near = jnp.where(near_low, up1, jnp.where(near_high, down1, 0.0))
        far = jnp.where(far_low, up2, jnp.where(far_high, down2, 0.0))
        face = -dissipation * (far - 4.0 * near)
        moved = pltpu.roll(face, (4 * at + 2) % cy, 1)
        packs[k // per_pack] = jnp.where(lane // 4 == at, moved, packs[k // per_pack])
    for k, pack in enumerate(packs):
        he_send[k] = pack
    row = lambda x: flow[:, :, x : x + 1, :]
    hx_send[0, :, :, 0:1, :] = -dissipation * (row(cx - 2) - 4.0 * row(cx - 1))
    hx_send[0, :, :, 1:2, :] = -dissipation * row(cx - 1)
    hx_send[1, :, :, 0:1, :] = -dissipation * row(0)
    hx_send[1, :, :, 1:2, :] = -dissipation * (row(1) - 4.0 * row(0))

    pl.semaphore_wait(barrier, greeted)

    halos = (
        (xx, hx, lambda side: hx_send.at[side]),
        (xe, he, lambda side: he_send),
        (xz, hz, lambda side: flow.at[:, cz - 2 : cz] if side == 0 else flow.at[:, 0:2]),
    )

    def halo_copy(number, side):
        x, slots, origin = halos[number]
        step = 1 if side == 0 else x.count - 1
        return pltpu.make_async_remote_copy(
            src_ref=origin(side),
            dst_ref=slots.at[side],
            send_sem=h_ss.at[number, side],
            recv_sem=h_rs.at[number, side],
            device_id={x.axis: lax.rem(x.me + step, x.count)},
            device_id_type=MESH,
        )

    for number, (x, slots, origin) in enumerate(halos):
        for side in range(2):
            sends = x.me < x.count - 1 if side == 0 else x.me > 0
            has = x.me > 0 if side == 0 else x.me < x.count - 1
            pl.when(sends)(lambda number=number, side=side: halo_copy(number, side).start())

            @pl.when(jnp.logical_not(has))
            def _(slots=slots, side=side):
                slots[side] = jnp.zeros(slots.shape[1:], jnp.float32)

    loads[1].wait()

    def keep_z(s, now):
        z_response[s] = now

    zeta.put_matrices(responses(cz, lambda k, s: f_zeta[:, k, s], keep_z))

    state = flow[...]
    nothing = jnp.zeros((fields, cz, 2, cy), jnp.float32)
    padded[:, :, 8 - 2 : 8, :] = nothing
    padded[:, :, 8 : 8 + cx, :] = state
    padded[:, :, 8 + cx : 8 + cx + 2, :] = nothing
    none = jnp.zeros((fields, 2, cx, cy), jnp.float32)
    long = jnp.concatenate([none, state, none], 1)
    near = (padded[:, :, 7 : 7 + cx, :] + padded[:, :, 9 : 9 + cx, :]) + (
        long[:, 1 : 1 + cz] + long[:, 3 : 3 + cz]
    )
    far = (padded[:, :, 6 : 6 + cx, :] + padded[:, :, 10 : 10 + cx, :]) + (
        long[:, 0:cz] + long[:, 4 : 4 + cz]
    )
    total_part = 18.0 * state - 4.0 * near + far + jnp.stack(eta_part).reshape(flow.shape)
    loads[3].wait()
    source[...] = residual[...] - dissipation * total_part

    loads[2].wait()

    for s in range(cx):
        for k in range(5):
            for g in range(3):
                x_factors[k, s, g] = f_xi[pl.ds((g * 5 + k) * cz * cx + s, cz, stride=cx), :]

    def xi_factor(k, s):
        return x_factors[k, s]

    def keep_x(s, now):
        x_response[s] = now

    xi.put_matrices(responses(cx, xi_factor, keep_x))
    zeta.join_matrices()

    for number, (x, slots, origin) in enumerate(halos):
        for side in range(2):
            has = x.me > 0 if side == 0 else x.me < x.count - 1
            pl.when(has)(lambda number=number, side=side: halo_copy(number, side).wait_recv())

    source[:, :, 0:2, :] += hx[0]
    source[:, :, cx - 2 : cx, :] += hx[1]
    zeta_faces = {
        0: hz[0, :, 0] - 4.0 * hz[0, :, 1],
        1: hz[0, :, 1],
        cz - 2: hz[1, :, 0],
        cz - 1: hz[1, :, 1] - 4.0 * hz[1, :, 0],
    }
    faces = [jnp.where(lane % 4 >= 2, he[0, k], he[1, k]) for k in range(he.shape[1])]
    edge = jnp.logical_or(lane < 2, lane >= cy - 2)

    def eta_face(f, z):
        k = f * cz + z
        back = (cy - (4 * (k % per_pack) + 2)) % cy
        return jnp.where(edge, pltpu.roll(faces[k // per_pack], back, 1), 0.0)

    def source_plane(own, z):
        value = jnp.stack([source[f, z] + eta_face(f, z) for f in own])
        if z in zeta_faces:
            value = value - dissipation * jnp.stack([zeta_faces[z][f] for f in own])
        return value

    z_local = []
    for h, own in enumerate(streams):
        z_factor = lambda k, s: lifts[h](f_zeta[:, k, s])
        zero = jnp.zeros((len(own), cx, cy), jnp.float32)
        forward = forward_sweep(cz, z_factor, lambda s: source_plane(own, s), zero, zero)
        zeta.put_ahead(h, jnp.stack([forward[-1], forward[-2]]))
        local = backward_sweep(
            cz, z_factor, lambda s: forward[s], zero, zero, lambda s, now: None
        )
        zeta.put_behind(h, jnp.stack([local[0], local[1]]))
        z_local.append(local)
    for h in range(len(streams)):
        zeta.solve(h)

    loads[4].wait()
    tiles = lines.shape[0] // cy
    steps = cy // sublanes
    total = lines.shape[0]
    distinct, uses = line_tiles(cy // (cz * cx))
    for k in range(5):
        for t, groups in enumerate(distinct):
            whole = jnp.concatenate([f_eta[g * 5 + k] for g in groups], 0)
            turned_factors[t * cy : (t + 1) * cy, :] = whole.T
        for s in range(steps):
            e_factors[k, s] = turned_factors[
                pl.ds(s, len(distinct) * sublanes, stride=steps), :
            ].reshape(len(distinct), sublanes, cy)

    def tiled(planes, at=slice(None)):
        return jnp.concatenate([planes[u : u + 1] for u in uses[at]], 0)

    xi.join_matrices()

    def eta_factor(k, s):
        return e_factors[k, s]

    def keep_e(s, now):
        e_response[s] = now

    e_matrices[...] = responses(steps, eta_factor, keep_e)
    chunk = lambda c: [e_matrices[k, :, c : c + 1, :] for k in range(12)]
    one = jnp.ones((1, len(distinct), 1, cy), jnp.float32)
    zero = jnp.zeros_like(one)
    unit = lambda j: jnp.concatenate([one if i == j else zero for i in range(4)], 0)
    inner, left = chain(sublanes, chunk, lambda c: None, [unit(j) for j in range(4)], False)
    for c, values in enumerate(inner):
        for k in range(4):
            e_inner[k, :, :, c : c + 1, :] = values[k]
    e_msend[...] = jnp.concatenate([left[0][0:2], left[1][0:2], left[2], left[3]], 0)
    e_mslots[xe.me] = e_msend[...]
    xe.start(0, lambda p: e_msend, e_mslots)

    if total > planes * cx:
        lines[planes * cx : total, :] = jnp.zeros((total - planes * cx, cy), jnp.float32)

    def turn(source_ref, target_ref, at):
        for t in range(at.start, at.stop):
            target_ref[t * cy : (t + 1) * cy, :] = source_ref[t * cy : (t + 1) * cy, :].T

    first, parts = 0, []
    for own in streams:
        count = -(-len(own) // per_tile)
        parts.append((first, slice(first // per_tile, first // per_tile + count)))
        first += len(own)
    e_local = []
    for h, own in enumerate(streams):
        place, at = parts[h]
        count = at.stop - at.start
        incoming = zeta.result(h)
        for s in range(cz):
            done = corrected(z_local[h][s], z_response[s], incoming, lifts[h])
            for k in range(len(own)):
                row = ((place + k) * cz + s) * cx
                lines[row : row + cx, :] = done[k]
        turn(lines, turned, at)
        offsets, o_send, o_slots, results, inside = e_streams[h]
        rows = lambda s: pl.ds(at.start * cy + s, count * sublanes, stride=steps)
        zero = jnp.zeros((count, sublanes, cy), jnp.float32)
        eta_tiles = lambda k, s: tiled(e_factors[k, s], at)
        forward = forward_sweep(
            steps, eta_tiles, lambda s: turned[rows(s), :].reshape(zero.shape), zero, zero
        )
        local = backward_sweep(
            steps, eta_tiles, lambda s: forward[s], zero, zero, lambda s, now: None
        )
        e_local.append(local)
        for k, value in enumerate((forward[-1], forward[-2], local[0], local[1])):
            offsets[k] = value
        none = jnp.zeros((count, 1, cy), jnp.float32)
        inner, left = chain(
            sublanes,
            lambda c: [tiled(plane, at) for plane in chunk(c)],
            lambda c: [offsets[k, :, c : c + 1, :] for k in range(4)],
            (none,) * 4,
            False,
        )
        for k in range(4):
            o_send[k] = left[k]
        o_slots[xe.me] = o_send[...]
        xe.start(1 + h, lambda p: o_send, o_slots)
        for c, values in enumerate(inner):
            for k in range(4):
                inside[k, :, c : c + 1, :] = values[k]

    x_local = []
    for h, own in enumerate(streams):
        place, at = parts[h]
        count = at.stop - at.start
        offsets, o_send, o_slots, results, inside = e_streams[h]
        if h == 0:
            xe.wait_recv(0, lambda p: e_msend, e_mslots)
        xe.wait_recv(1 + h, lambda p: o_send, o_slots)
        none = jnp.zeros((count, 1, cy), jnp.float32)
        solved, _ = chain(
            n_eta,
            lambda q: [tiled(e_mslots[q, k], at) for k in range(12)],
            lambda q: [o_slots[q, k] for k in range(4)],
            (none,) * 4,
            True,
        )
        for q, values in enumerate(solved):
            for k in range(4):
                results[q, k] = values[k]
        enters = [results[xe.me, k] for k in range(4)]
        incoming = []
        for k in range(4):
            value = inside[k]
            for j in range(2 if k < 2 else 4):
                value = value + tiled(e_inner[k, j], at) * enters[j]
            incoming.append(value)
        rows = lambda s: pl.ds(at.start * cy + s, count * sublanes, stride=steps)
        for s in range(steps):
            done = corrected(e_local[h][s], e_response[s], incoming, lambda r: tiled(r, at))
            turned[rows(s), :] = done.reshape(count * sublanes, cy)
        turn(turned, lines, at)
        x_factor = lambda k, s: lifts[h](xi_factor(k, s))
        zero = jnp.zeros((len(own), cz, cy), jnp.float32)
        columns = lambda s: pl.ds(place * cz * cx + s, len(own) * cz, stride=cx)
        forward = forward_sweep(
            cx, x_factor, lambda s: lines[columns(s), :].reshape(zero.shape), zero, zero
        )
        xi.put_ahead(h, jnp.stack([forward[-1], forward[-2]]))
        local = backward_sweep(
            cx, x_factor, lambda s: forward[s], zero, zero, lambda s, now: None
        )
        xi.put_behind(h, jnp.stack([local[0], local[1]]))
        x_local.append(local)
    for h in range(len(streams)):
        xi.solve(h)
    for h, own in enumerate(streams):
        incoming = xi.result(h)
        for s in range(cx):
            done = corrected(x_local[h][s], x_response[s], incoming, lifts[h])
            for k, f in enumerate(own):
                out[pl.ds(f * cz * cx + s, cz, stride=cx), :] = done[k]

    zeta.finish()
    xi.finish()
    xe.wait_send(0, lambda p: e_msend, e_mslots)
    for h, (_, o_send, o_slots, _, _) in enumerate(e_streams):
        xe.wait_send(1 + h, lambda p: o_send, o_slots)
    for number, (x, slots, origin) in enumerate(halos):
        for side in range(2):
            sends = x.me < x.count - 1 if side == 0 else x.me > 0
            pl.when(sends)(lambda number=number, side=side: halo_copy(number, side).wait_send())


def solver_scratch(count, streams, lanes):
    vmem = lambda *shape: pltpu.VMEM(shape, jnp.float32)
    dma = pltpu.SemaphoreType.DMA
    if count == 4:
        plane = (sublanes, lanes)
        return (
            vmem(12, 3, *plane),
            vmem(12, 3, *plane),
            vmem(4, 3, *plane),
            vmem(4, 3, *plane),
            tuple(
                tuple(vmem(n, len(own), *plane) for n in (4, 4, 2, 2, 4)) for own in streams
            ),
            dma((2 + 3 * len(streams), count)),
            dma((2 + 3 * len(streams),)),
        )
    parts = count if sublanes % count == 0 else 1
    rows = sublanes // parts
    return tuple(
        (
            vmem(parts, 12, 3, rows, lanes),
            vmem(count, 12, 3, rows, lanes),
            vmem(parts, 4, len(own), rows, lanes),
            vmem(count, 4, len(own), rows, lanes),
            vmem(count, 4, len(own), rows, lanes),
            vmem(count, 4, len(own), rows, lanes),
            vmem(4, len(own), sublanes, lanes),
            dma((5, count)),
            dma((5, count)),
        )
        for own in streams
    )


def on_device(counts, residual, flow_state, factors_zeta, factors_eta, factors_xi):
    n_xi, n_eta, n_zeta = counts
    fields, cz, cx, cy = flow_state.shape
    total = -(-(fields * cz * cx) // cy) * cy
    tiles = total // cy
    steps = cy // sublanes
    packs = -(-(fields * cz) // (cy // 4))
    distinct = len(line_tiles(cy // (cz * cx))[0])
    vmem = lambda *shape: pltpu.VMEM(shape, jnp.float32)
    dma = pltpu.SemaphoreType.DMA
    whole = pl.BlockSpec(memory_space=pltpu.VMEM)
    per_tile = cy // (cz * cx)
    streams = streams_of(per_tile)
    eta_streams = []
    for own in streams:
        count = -(-len(own) // per_tile)
        eta_streams.append(
            (
                vmem(4, count, sublanes, cy),
                vmem(4, count, 1, cy),
                vmem(n_eta, 4, count, 1, cy),
                vmem(n_eta, 4, count, 1, cy),
                vmem(4, count, sublanes, cy),
            )
        )
    scratch = (
        [
            vmem(fields, cz, cx, cy),
            vmem(fields, cz, cx, cy),
            vmem(3, 5, cz, cx, cy),
            vmem(15, cz * cx, cy),
            vmem(15 * cz * cx, cy),
            dma((5,)),
            solver_scratch(n_zeta, streams, cy),
            solver_scratch(n_xi, streams, cy),
            tuple(eta_streams),
            vmem(12, distinct, sublanes, cy),
            vmem(12, distinct, 1, cy),
            vmem(n_eta, 12, distinct, 1, cy),
            vmem(4, 4, distinct, sublanes, cy),
            dma((1 + len(streams), n_eta)),
            dma((1 + len(streams), n_eta)),
            vmem(cz, 4, 3, cx, cy),
            vmem(cx, 4, 3, cz, cy),
            vmem(steps, 4, distinct, sublanes, cy),
            vmem(5, cx, 3, cz, cy),
            vmem(5, steps, distinct, sublanes, cy),
            vmem(total, cy),
            vmem(total, cy),
            vmem(distinct * cy, cy),
            vmem(2, fields, 2, cx, cy),
            vmem(2, fields, cz, 2, cy),
            vmem(2, fields, cz, 2, cy),
            vmem(packs, cx, cy),
            vmem(2, packs, cx, cy),
            vmem(fields, cz, cx + 16, cy),
            vmem(fields, cz, cx, cy),
            dma((3, 2)),
            dma((3, 2)),
        ]
    )
    update = pl.pallas_call(
        functools.partial(kernel, counts),
        out_shape=jax.ShapeDtypeStruct((fields * cz * cx, cy), jnp.float32),
        in_specs=[pl.BlockSpec(memory_space=pltpu.HBM)] * 5,
        out_specs=whole,
        scratch_shapes=scratch,
        compiler_params=pltpu.CompilerParams(
            collective_id=0, has_side_effects=True, vmem_limit_bytes=24 * 2**20
        ),
    )(
        *(
            pltpu.with_memory_space_constraint(operand, pltpu.HBM)
            for operand in (
                residual,
                flow_state,
                factors_zeta,
                factors_eta.reshape(15, cz * cx, cy),
                factors_xi.reshape(15 * cz * cx, cy),
            )
        )
    )
    return update.reshape(flow_state.shape)


def solution(mesh):
    fields = P(None, "zeta", "xi", "eta")
    factors = P(None, None, "zeta", "xi", "eta")
    counts = tuple(mesh.shape[axis] for axis in ("xi", "eta", "zeta"))
    return jax.shard_map(
        functools.partial(on_device, counts),
        mesh=mesh,
        in_specs=(fields, fields, factors, factors, factors),
        out_specs=fields,
        check_vma=False,
    )
```
